32 devices in a mesh: context: 8 (over z, x), head: 4 (over y, core).
Axes of the slice: x: 2, y: 2, z: 4, core: 2. Of those that a mesh axis runs over, the one named last changes fastest.
Arguments:
- queries: bfloat16 [4096, 4096], P(('context', 'head')), may hold values from -6 to 6
- key_input: bfloat16 [4096, 4096], P(('context', 'head')), may hold values from -32 to 32
- value_input: bfloat16 [4096, 4096], P(('context', 'head')), may hold values from -32 to 32
- gate_input: bfloat16 [4096, 4096], P(('context', 'head')), may hold values from -6 to 6
- decay_logit: float32 [4096, 32], P(('context', 'head')), may hold values from -5 to 16
- beta_logit: float32 [4096, 32], P(('context', 'head')), may hold values from -9 to 9
- decay_bias: float32 [32], P('head'), may hold values from -16 to -3
- norm_gain: float32 [128], replicated, may hold values from 0.1 to 1.9
- doc_start: int32 [64], P('context'), may hold values from 0 to 1, as said below
Outputs:
- layer_output: bfloat16 [4096, 4096], P(('context', 'head'))
The draws below stay inside these ranges and needn't reach their ends.
Inputs may be any that keep to these rules, and one draw needn't show every extreme that they name: `doc_start`: exactly one of the groups 1 to max(3, 8) holds a 1; apart from it, 1 appears only in the last max(2, 8) groups.
All inputs are finite; a program needn't handle non-finite values.
Results may differ from the reference program's by a relative error of at most 0.013.
Values may be sent and summed in bfloat16 or wider, within the bound.
No kernel may reach another device: no remote copies, remote signals or barrier semaphores. Data moves between devices by JAX's collectives and lax.ppermute only.
A program may use at most 192 MiB of HBM per device.

```python
import math
import jax
import jax.numpy as jnp
from jax import lax

HEAD_TOTAL = 32
DK = 128
DV = 128
C = 64
TOK_DEV = 128
STREAM_TOKENS = 4096
CH_DEV = 8
NCHUNK = 64


def rough_sample(base_key, row_count, col_count, shown_shared, shown_top, divisor):
    noise_key, shared_key, column_key, scale_key = jax.random.split(base_key, 4)
    sample = jax.random.normal(noise_key, (row_count, col_count), jnp.float32)
    sample = sample + shown_shared * jax.random.normal(shared_key, (1, col_count), jnp.float32)
    column_scale = jnp.exp(jax.random.uniform(column_key, (1, col_count), jnp.float32, 0.0, math.log(shown_top)))
    row_scale = jnp.exp(jax.random.uniform(scale_key, (row_count, 1), jnp.float32, 0.0, math.log(10.0)))
    return jnp.clip(sample * column_scale * row_scale / divisor, -32.0, 32.0)


def draw_key_input(key, part):
    return rough_sample(jax.random.fold_in(key, 11), STREAM_TOKENS, HEAD_TOTAL * DK, 2.5, 100.0, 64.0).astype(jnp.bfloat16)


def draw_value_input(key, part):
    return rough_sample(jax.random.fold_in(key, 13), STREAM_TOKENS, HEAD_TOTAL * DV, 0.0, 10.0, 8.0).astype(jnp.bfloat16)


def decay_pair(key):
    base_key = jax.random.fold_in(key, 31)
    key_sequence = jax.random.split(base_key, 7)
    fast_count = 4
    is_fast = jax.random.randint(key_sequence[0], (HEAD_TOTAL,), 0, 8) < fast_count
    log_tokens = math.log(STREAM_TOKENS)
    slow_bias = -log_tokens - jax.random.uniform(key_sequence[1], (HEAD_TOTAL,), jnp.float32, 1.0, 2.5)
    fast_bias = jax.random.uniform(key_sequence[2], (HEAD_TOTAL,), jnp.float32, -4.3, -3.2)
    per_head_bias = jnp.where(is_fast, fast_bias, slow_bias)
    blocks = STREAM_TOKENS // TOK_DEV
    offset = jax.random.uniform(key_sequence[3], (blocks, 1, HEAD_TOTAL), jnp.float32, -1.0, 1.0)
    jitter = 0.5 * jax.random.normal(key_sequence[4], (blocks, TOK_DEV, HEAD_TOTAL), jnp.float32)
    logit_matrix = (offset + jitter).reshape(STREAM_TOKENS, HEAD_TOTAL)
    token_positions = jax.random.randint(key_sequence[5], (3,), 0, STREAM_TOKENS)
    spike_mask = jnp.any(jnp.arange(STREAM_TOKENS)[:, None] == token_positions[None, :], axis=1)
    spike_value = -per_head_bias[None, :] - jax.random.uniform(key_sequence[6], (STREAM_TOKENS, HEAD_TOTAL), jnp.float32, 0.3, 1.5)
    logit_matrix = jnp.where(spike_mask[:, None], spike_value, logit_matrix)
    return (per_head_bias, jnp.clip(logit_matrix, -5.0, 16.0))


def draw_decay_logit(key, part):
    return decay_pair(key)[1]


def draw_decay_bias(key, part):
    return decay_pair(key)[0]


def draw_doc_start(key, part):
    first_key, coin_key = jax.random.split(jax.random.fold_in(key, 41))
    head_span = max(3, NCHUNK // 8)
    tail_count = max(2, NCHUNK // 8)
    first_group = jax.random.randint(first_key, (), 1, head_span + 1)
    tail_begin = NCHUNK - tail_count
    coin_bound = max(2, min(4 * CH_DEV, tail_count // 2))
    coins = jax.random.randint(coin_key, (NCHUNK,), 0, coin_bound) == 0
    group_index = jnp.arange(NCHUNK, dtype=jnp.int32)
    flags = jnp.logical_or(group_index == first_group, jnp.logical_and(group_index >= tail_begin, coins))
    return flags.astype(jnp.int32)


def shard_levels(own_key, extent, pieces, smallest, high):
    level, own = 1.0, jax.random.fold_in(own_key, 6)
    for dim, shards_of in pieces:
        steps = jnp.exp(jax.random.uniform(jax.random.fold_in(own, dim), (shards_of,), jnp.float32, smallest / len(pieces), high / len(pieces)))
        level = level * jnp.repeat(steps, extent[dim] // shards_of).reshape([-1 if axis == dim else 1 for axis in range(len(extent))])
    return level


def gaussian(own_key, extent, deviation, most, shards=(), held_as=jnp.bfloat16):
    values = deviation * jax.random.normal(own_key, extent, jnp.float32)
    if shards:
        values = values * shard_levels(own_key, extent, shards, -0.22, 0.18)
    return jnp.clip(values, -most, most).astype(held_as)


def setup_inputs(seed: int = 0) -> dict:
    streams_of = jax.random.split(jax.random.key(seed), 10)
    return {
        "queries": gaussian(streams_of[0], (STREAM_TOKENS, HEAD_TOTAL * DK), 1.0, 6.0, ((0, 32),)),
        "key_input": draw_key_input(jax.random.fold_in(streams_of[9], 71), 0),
        "value_input": draw_value_input(jax.random.fold_in(streams_of[9], 71), 0),
        "gate_input": gaussian(streams_of[3], (STREAM_TOKENS, HEAD_TOTAL * DV), 1.0, 6.0, ((0, 32),)),
        "decay_logit": draw_decay_logit(jax.random.fold_in(streams_of[9], 71), 0),
        "beta_logit": gaussian(streams_of[5], (STREAM_TOKENS, HEAD_TOTAL), 1.5, 9.0, ((0, 32),), jnp.float32),
        "decay_bias": draw_decay_bias(jax.random.fold_in(streams_of[9], 71), 0),
        "norm_gain": jnp.clip(1.0 + 0.18 * jax.random.normal(streams_of[7], (DV,), jnp.float32), 0.1, 1.9),
        "doc_start": draw_doc_start(jax.random.fold_in(streams_of[9], 71), 0),
    }


PRECISE = lax.Precision.HIGHEST

def normalize_keys(raw_keys):
    widened = raw_keys.astype(jnp.float32)
    scaled = widened * lax.rsqrt(lax.optimization_barrier(jnp.sum(widened * widened, axis=-1, keepdims=True)) + 1e-06)
    return scaled.astype(jnp.bfloat16)

def group_step(state_in, inputs):
    query_group, key_group, value_group, decay_group, beta_group, start_flag = inputs
    cum_decay = jnp.cumsum(decay_group, axis=0)
    row_index = lax.broadcasted_iota(jnp.int32, (C, C), 0)
    column_index = lax.broadcasted_iota(jnp.int32, (C, C), 1)
    cum_heads = cum_decay.T
    decay_gap = cum_heads[:, :, None] - cum_heads[:, None, :]
    strict = jnp.exp(jnp.where(row_index > column_index, decay_gap, -jnp.inf))
    inclusive = jnp.exp(jnp.where(row_index >= column_index, decay_gap, -jnp.inf))
    query_wide = query_group.astype(jnp.float32)
    key_wide = key_group.astype(jnp.float32)
    value_wide = value_group.astype(jnp.float32)
    key_gram = jnp.einsum('thd,shd->hts', key_wide, key_wide, precision=PRECISE)
    query_gram = jnp.einsum('thd,shd->hts', query_wide, key_wide, precision=PRECISE)
    lower_part = beta_group.T[:, :, None] * strict * key_gram
    scaled_keys = (beta_group * jnp.exp(cum_decay))[:, :, None] * key_wide
    scaled_values = beta_group[:, :, None] * value_wide
    right_side = jnp.transpose(jnp.concatenate([scaled_keys, scaled_values], axis=-1), (1, 0, 2))
    solved = jax.scipy.linalg.solve_triangular(jnp.eye(C, dtype=jnp.float32) + lower_part, right_side, lower=True, unit_diagonal=True)
    solved_keys = solved[:, :, :DK]
    solved_values = solved[:, :, DK:]
    entering = (1.0 - start_flag.astype(jnp.float32)) * state_in
    pseudo = solved_values - jnp.einsum('htd,hde->hte', solved_keys, entering, precision=PRECISE)
    last_cum = cum_decay[-1]
    back_weight = jnp.exp(last_cum[None, :] - cum_decay)
    back_keys = back_weight[:, :, None] * key_wide
    new_state = jnp.exp(last_cum)[:, None, None] * entering + jnp.einsum('thd,hte->hde', back_keys, pseudo, precision=PRECISE)
    query_mix = inclusive * query_gram
    through = jnp.exp(cum_decay)[:, :, None] * jnp.einsum('thd,hde->the', query_wide, entering, precision=PRECISE)
    core_rows = through + jnp.einsum('hts,hse->the', query_mix, pseudo, precision=PRECISE)
    return (new_state, core_rows)

def gated_norm(core_rows, gate_input, norm_gain):
    row_count = core_rows.shape[0]
    widened = core_rows.astype(jnp.float32).reshape(row_count, -1, norm_gain.shape[0])
    scaled = widened * lax.rsqrt(lax.optimization_barrier(jnp.mean(widened * widened, axis=-1, keepdims=True)) + 1e-06)
    gate_wide = gate_input.astype(jnp.float32).reshape(widened.shape)
    result = scaled * norm_gain * jax.nn.silu(gate_wide)
    return result.reshape(row_count, -1).astype(jnp.bfloat16)

def reference(queries, key_input, value_input, gate_input, decay_logit, beta_logit, decay_bias, norm_gain, doc_start):
    groups = STREAM_TOKENS // C
    log_decay = -jax.nn.softplus(decay_logit + decay_bias[None, :])
    beta_gate = jax.nn.sigmoid(beta_logit)
    normed = normalize_keys(key_input.reshape(STREAM_TOKENS, HEAD_TOTAL, DK))
    inputs = (queries.reshape(groups, C, HEAD_TOTAL, DK), normed.reshape(groups, C, HEAD_TOTAL, DK), value_input.reshape(groups, C, HEAD_TOTAL, DV), log_decay.reshape(groups, C, HEAD_TOTAL), beta_gate.reshape(groups, C, HEAD_TOTAL), doc_start)
    start_state = jnp.zeros((HEAD_TOTAL, DK, DV), jnp.float32)
    cores = lax.scan(group_step, start_state, inputs)[1]
    core_rows = cores.reshape(STREAM_TOKENS, HEAD_TOTAL * DV).astype(jnp.bfloat16)
    core_rows = lax.optimization_barrier(core_rows)
    return gated_norm(core_rows, gate_input, norm_gain)
```

```python
import functools

import jax
import jax.numpy as jnp
from jax import lax
from jax.experimental import pallas as pl
from jax.experimental.pallas import tpu as pltpu
from jax.sharding import PartitionSpec as P

C = 64
F32 = jnp.float32
BF16 = jnp.bfloat16
EXACT = lax.Precision.HIGHEST
VMEM_BYTES = 40 * 1024 * 1024
MASKED = -1e30


def params():
    return pltpu.CompilerParams(vmem_limit_bytes=VMEM_BYTES)


def cost(flops, moved):
    return pl.CostEstimate(flops=int(flops), bytes_accessed=int(moved), transcendentals=0)


def dot(a, b):
    return jnp.dot(a, b, preferred_element_type=F32)


def dot_t(a, b):
    return lax.dot_general(a, b, (((1,), (1,)), ((), ())), preferred_element_type=F32)


def gates_kernel(parts, width, decay_ref, beta_ref, resets_ref, resets_row_ref, *rest):
    bias_refs, (col_ref, row_ref, gap_ref) = rest[:-3], rest[-3:]
    bias = bias_refs[0][...]
    for ref in bias_refs[1:]:
        bias = bias + ref[...]
    tokens = decay_ref.shape[0]
    z = decay_ref[...] + bias
    log_decay = -(jnp.maximum(z, 0.0) + jnp.log1p(jnp.exp(-jnp.abs(z))))
    row = lax.broadcasted_iota(jnp.int32, (tokens, tokens), 0)
    column = lax.broadcasted_iota(jnp.int32, (tokens, tokens), 1)
    ones = jnp.where(row >= column, 1.0, 0.0).astype(F32)
    cum = jnp.dot(ones, log_decay, precision=EXACT, preferred_element_type=F32)
    beta = 1.0 / (1.0 + jnp.exp(-beta_ref[...]))
    resets = resets_ref[...]
    resets_row = resets_row_ref[...]
    gamma = jnp.exp(cum) * jnp.where(resets == 0.0, 1.0, 0.0)
    cum_row = jnp.transpose(cum)
    last = cum_row[:, tokens - 1 : tokens]
    final = resets_row[:, tokens - 1 : tokens]
    back = jnp.exp(last - cum_row) * jnp.where(resets_row == final, 1.0, 0.0)
    whole = jnp.broadcast_to(jnp.exp(last) * jnp.where(final == 0.0, 1.0, 0.0), cum_row.shape)
    for part in range(parts):
        span = slice(part * width, (part + 1) * width)
        for place, table in enumerate((cum, beta, beta * gamma, gamma)):
            col_ref[part, :, place * width : (place + 1) * width] = table[:, span]
        for place, table in enumerate((cum_row, back, whole)):
            row_ref[part, place * width : (place + 1) * width, :] = table[span, :]
    seen = jnp.logical_and(row >= column, resets == resets_row)
    gap_ref[...] = jnp.where(seen, 0.0, MASKED)


def gates(decay_logit, beta_logit, resets, biases, parts):
    tokens, heads = decay_logit.shape
    width = heads // parts
    return pl.pallas_call(
        functools.partial(gates_kernel, parts, width),
        out_shape=(
            jax.ShapeDtypeStruct((parts, tokens, 4 * width), F32),
            jax.ShapeDtypeStruct((parts, 3 * width, tokens), F32),
            jax.ShapeDtypeStruct((tokens, tokens), F32),
        ),
        compiler_params=params(),
        name="gates",
    )(decay_logit, beta_logit, resets[:, None], resets[None, :], *biases)


def local_kernel(width, half, head_bits, where_ref, col_ref, row_ref, gap_ref, q_ref, k_ref, v_ref, ab_ref, qo_ref):
    tokens = q_ref.shape[0]
    size = q_ref.shape[1] // width
    flip = where_ref[1]
    row = lax.broadcasted_iota(jnp.int32, (tokens, tokens), 0)
    column = lax.broadcasted_iota(jnp.int32, (tokens, tokens), 1)
    apart = jnp.bitwise_xor(row, column)
    eye = jnp.where(row == column, 1.0, 0.0)
    gap = gap_ref[...]
    steps = []
    block = 1
    while block < tokens:
        steps.append(jnp.logical_and(apart >= block, apart < 2 * block))
        block *= 2
    every = range(width)
    normed, lower, mix, inverse = [], [], [], []
    for j in every:
        span = slice(j * size, (j + 1) * size)
        keys = k_ref[:, span].astype(F32)
        keys = (keys * lax.rsqrt(jnp.sum(keys * keys, axis=-1, keepdims=True) + 1e-06)).astype(BF16)
        grams = dot_t(jnp.concatenate([keys, q_ref[:, span]], axis=0), keys)
        decay = jnp.exp(col_ref[0, :, j : j + 1] - row_ref[0, j : j + 1, :] + gap)
        low = col_ref[0, :, width + j : width + j + 1] * decay * grams[:tokens]
        normed.append(keys)
        mix.append((decay * grams[tokens:]).astype(BF16))
        inverse.append(eye - jnp.where(steps[0], low, 0.0))
        lower.append(low.astype(BF16))
    for step in steps[1:]:
        small = [inverse[j].astype(BF16) for j in every]
        inner = [
            dot(jnp.where(step, lower[j], jnp.zeros_like(lower[j])), small[j]).astype(BF16) for j in every
        ]
        inverse = [inverse[j] - dot(small[j], inner[j]) for j in every]
    solved = []
    for j in every:
        span = slice(j * size, (j + 1) * size)
        keys = col_ref[0, :, 2 * width + j : 2 * width + j + 1] * normed[j].astype(F32)
        values = col_ref[0, :, width + j : width + j + 1] * v_ref[:, span].astype(F32)
        right = jnp.concatenate([keys.astype(BF16), values.astype(BF16)], axis=1)
        solved.append(dot(inverse[j].astype(BF16), right).astype(BF16))
    for j in every:
        span = slice(j * size, (j + 1) * size)
        back = jnp.transpose(normed[j].astype(F32)) * row_ref[0, width + j : width + j + 1, :]
        both = dot(jnp.concatenate([back.astype(BF16), mix[j]], axis=0), solved[j])
        whole = eye * row_ref[0, 2 * width + j : 2 * width + j + 1, :]
        through = col_ref[0, :, 3 * width + j : 3 * width + j + 1] * q_ref[:, span].astype(F32)
        place = jnp.bitwise_xor(j // half, flip)
        ab_ref[0, place, j % half, :, :size] = (whole - both[:size, :size]).astype(BF16)
        ab_ref[0, place, j % half, :, size:] = both[:size, size:].astype(BF16)
        qo_ref[0, place, j % half, :, :size] = (through - both[size:, :size]).astype(BF16)
        qo_ref[0, place, j % half, :, size:] = both[size:, size:].astype(BF16)


def local(where, parts, col, rowt, gap, queries, keys, values):
    tokens = queries.shape[0]
    heads = queries.shape[1] // (rowt.shape[0] * rowt.shape[1] // 3)
    width = rowt.shape[1] // 3
    span = queries.shape[1] // rowt.shape[0]
    size = span // width
    half = width // 2
    first, stride = parts[0], parts[1] - parts[0] if len(parts) > 1 else 0
    del heads

    def part(i, where_ref):
        return jnp.bitwise_xor(where_ref[0], first + stride * i)

    strip = pl.BlockSpec((tokens, span), lambda i, w: (0, part(i, w)))
    result = jax.ShapeDtypeStruct((len(parts), 2, half, tokens, 2 * size), BF16)
    result_spec = pl.BlockSpec((1, 2, half, tokens, 2 * size), lambda i, w: (i, 0, 0, 0, 0))
    return pl.pallas_call(
        functools.partial(local_kernel, width, half, None),
        out_shape=(result, result),
        grid_spec=pltpu.PrefetchScalarGridSpec(
            num_scalar_prefetch=1,
            grid=(len(parts),),
            in_specs=[
                pl.BlockSpec((1,) + col.shape[1:], lambda i, w: (part(i, w), 0, 0)),
                pl.BlockSpec((1,) + rowt.shape[1:], lambda i, w: (part(i, w), 0, 0)),
                pl.BlockSpec(gap.shape, lambda i, w: (0, 0)),
                strip,
                strip,
                strip,
            ],
            out_specs=(result_spec, result_spec),
        ),
        compiler_params=params(),
        cost_estimate=cost(len(parts) * width * 6e7, len(parts) * 2**21),
        name="local_tokens",
    )(where, col, rowt, gap, queries, keys, values)


def pick(later, own, received):
    return jnp.where(later, received, own), jnp.where(later, own, received)


def joined(earlier, later):
    size = earlier.shape[0]
    product = dot(later[:, :size], earlier)
    return jnp.concatenate([product[:, :size], product[:, size:] + later[:, size:].astype(F32)], axis=1)


def compose_kernel(bit, where_ref, own_ref, received_ref, out_ref):
    later = where_ref[bit] == 1
    for j in range(own_ref.shape[0]):
        earlier_block, later_block = pick(later, own_ref[j], received_ref[j])
        out_ref[j] = joined(earlier_block, later_block).astype(BF16)


def compose(where, bit, own, received):
    return pl.pallas_call(
        functools.partial(compose_kernel, bit),
        out_shape=jax.ShapeDtypeStruct(own.shape, BF16),
        grid_spec=pltpu.PrefetchScalarGridSpec(
            num_scalar_prefetch=1,
            grid=(1,),
            in_specs=[pl.BlockSpec(own.shape, lambda i, w: (0, 0, 0))] * 2,
            out_specs=pl.BlockSpec(own.shape, lambda i, w: (0, 0, 0)),
        ),
        compiler_params=params(),
        cost_estimate=cost(own.size * 256, own.size * 6),
        name="compose",
    )(where, own, received)


def doubling_kernel(bit, first, where_ref, *refs):
    later = where_ref[bit] == 1
    own_ref, received_ref = refs[:2]
    total_ref, before_ref = refs[-2:]
    heads, size = own_ref.shape[:2]
    row = lax.broadcasted_iota(jnp.int32, (size, 2 * size), 0)
    column = lax.broadcasted_iota(jnp.int32, (size, 2 * size), 1)
    neutral = jnp.where(row == column, 1.0, 0.0).astype(BF16)
    for j in range(heads):
        earlier_block, later_block = pick(later, own_ref[j], received_ref[j])
        total_ref[j] = joined(earlier_block, later_block).astype(BF16)
        if first:
            before_ref[j] = jnp.where(later, received_ref[j], neutral)
        else:
            before = refs[2][j]
            before_ref[j] = jnp.where(later, joined(received_ref[j], before).astype(BF16), before)


def doubling(where, bit, own, received, before):
    first = before is None
    arrays = (own, received) if first else (own, received, before)
    spec = pl.BlockSpec(own.shape, lambda i, w: (0, 0, 0))
    return pl.pallas_call(
        functools.partial(doubling_kernel, bit, first),
        out_shape=(jax.ShapeDtypeStruct(own.shape, BF16),) * 2,
        grid_spec=pltpu.PrefetchScalarGridSpec(
            num_scalar_prefetch=1,
            grid=(1,),
            in_specs=[spec] * len(arrays),
            out_specs=(spec, spec),
        ),
        compiler_params=params(),
        cost_estimate=cost(own.size * 256, own.size * 8),
        name="doubling",
    )(where, *arrays)


def descend_kernel(bits, top, where_ref, *refs):
    count = len(bits)
    start = 2 if top is not None else 1
    blocks = refs[start : start + 2 * count]
    sends = refs[start + 2 * count : start + 3 * count]
    kept_ref = refs[-1]
    size = kept_ref.shape[-1]
    for j in range(kept_ref.shape[0]):
        if top is None:
            state = refs[0][j]
        else:
            before = refs[1][j]
            carried = dot(before[:, :size], refs[0][j]) + before[:, size:].astype(F32)
            state = jnp.where(where_ref[top] == 1, carried.astype(BF16), before[:, size:])
        for level, bit in enumerate(bits):
            later = where_ref[bit] == 1
            earlier = jnp.where(later, blocks[2 * level + 1][j], blocks[2 * level][j])
            after = (dot(earlier[:, :size], state) + earlier[:, size:].astype(F32)).astype(BF16)
            sends[level][j] = jnp.where(later, state, after)
            state = jnp.where(later, after, state)
        kept_ref[j] = state


def descend(where, bits, top, sources, blocks):
    arrays, specs = [], []
    heads, size = sources[0].shape[0], sources[0].shape[1]
    for array in sources:
        arrays.append(array)
        specs.append(pl.BlockSpec(array.shape, lambda i, w: (0, 0, 0)))
    for pair in blocks:
        for array, index in pair:
            arrays.append(array)
            lead = (None,) * len(index)
            specs.append(
                pl.BlockSpec(lead + array.shape[len(index) :], lambda i, w, index=index: index + (0, 0, 0))
            )
    spec = pl.BlockSpec((heads, size, size), lambda i, w: (0, 0, 0))
    outs = len(bits) + 1
    return pl.pallas_call(
        functools.partial(descend_kernel, bits, top),
        out_shape=(jax.ShapeDtypeStruct((heads, size, size), BF16),) * outs,
        grid_spec=pltpu.PrefetchScalarGridSpec(
            num_scalar_prefetch=1,
            grid=(1,),
            in_specs=specs,
            out_specs=(spec,) * outs,
        ),
        compiler_params=params(),
        cost_estimate=cost(outs * heads * 2 * size**3, outs * heads * 2**17),
        name="descend",
    )(where, *arrays)


def finish_kernel(has_previous, where_ref, state_ref, qo_ref, gate_ref, gain_ref, *rest):
    out_ref = rest[-1]
    size = state_ref.shape[-1]
    for j in range(state_ref.shape[0]):
        span = slice(j * size, (j + 1) * size)
        core = dot(qo_ref[j, :, :size], state_ref[j]) + qo_ref[j, :, size:].astype(F32)
        core = core.astype(BF16).astype(F32)
        scaled = core * lax.rsqrt(jnp.mean(core * core, axis=-1, keepdims=True) + 1e-06)
        gate = gate_ref[:, span].astype(F32)
        out_ref[:, span] = (scaled * gain_ref[...] * (gate / (1.0 + jnp.exp(-gate)))).astype(BF16)


def finish(where, part, turn, place, state, qo, gate, gain, previous):
    half, tokens, size = state.shape[0], gate.shape[0], state.shape[-1]

    def strip(i, w):
        return 0, 2 * jnp.bitwise_xor(w[0], part) + jnp.bitwise_xor(w[1], turn)

    specs = [
        pl.BlockSpec(state.shape, lambda i, w: (0, 0, 0)),
        pl.BlockSpec((None, None) + qo.shape[2:], lambda i, w: (place, turn, 0, 0, 0)),
        pl.BlockSpec((tokens, half * size), strip),
        pl.BlockSpec(gain.shape, lambda i, w: (0, 0)),
    ]
    arrays = [state, qo, gate, gain]
    aliases = {}
    if previous is not None:
        specs.append(pl.BlockSpec(memory_space=pl.ANY))
        arrays.append(previous)
        aliases = {len(arrays): 0}
    return pl.pallas_call(
        functools.partial(finish_kernel, previous is not None),
        out_shape=jax.ShapeDtypeStruct(gate.shape, BF16),
        grid_spec=pltpu.PrefetchScalarGridSpec(
            num_scalar_prefetch=1,
            grid=(1,),
            in_specs=specs,
            out_specs=pl.BlockSpec((tokens, half * size), strip),
        ),
        input_output_aliases=aliases,
        compiler_params=params(),
        cost_estimate=cost(half * 2 * tokens * size * size, half * 2**17),
        name="finish",
    )(where, *arrays)


def body(
    head_count,
    context_count,
    queries,
    key_input,
    value_input,
    gate_input,
    decay_logit,
    beta_logit,
    decay_bias,
    norm_gain,
    doc_start,
):
    place = lax.axis_index("head")
    block = lax.axis_index("context")
    tokens, heads = decay_logit.shape
    width = heads // head_count
    groups = tokens // C
    head_bits = head_count.bit_length() - 1
    context_bits = context_count.bit_length() - 1

    def swap(array, axis, distance):
        count = head_count if axis == "head" else context_count
        return lax.ppermute(array, axis, [(i, i ^ distance) for i in range(count)])

    where = jnp.stack(
        [place, block & 1]
        + [(place >> bit) & 1 for bit in range(head_bits)]
        + [(block >> bit) & 1 for bit in range(context_bits)]
    ).astype(jnp.int32)
    head_bit = [2 + bit for bit in range(head_bits)]
    context_bit = [2 + head_bits + bit for bit in range(context_bits)]

    mine = jnp.where(
        lax.broadcasted_iota(jnp.int32, (head_count, width), 0) == place, decay_bias[None, :], 0.0
    ).reshape(1, heads)
    biases = [mine] + [swap(mine, "head", other) for other in range(1, head_count)]
    starts = lax.dynamic_slice(doc_start, (place * groups,), (groups,)).astype(F32)
    resets = jnp.repeat(jnp.cumsum(starts), C)
    col, rowt, gap = gates(decay_logit, beta_logit, resets, biases, head_count)

    odd = list(range(head_count - 1, 0, -2))
    even = [part - 1 for part in odd]
    qo = {}
    ab_odd, qo_odd = local(where, odd, col, rowt, gap, queries, key_input, value_input)
    ab_even, qo_even = local(where, even, col, rowt, gap, queries, key_input, value_input)
    for index, part in enumerate(odd):
        qo[part] = (qo_odd, index)
    for index, part in enumerate(even):
        qo[part] = (qo_even, index)

    half, size = ab_even.shape[2], ab_even.shape[3]
    flat = lambda a: a.reshape((-1,) + a.shape[-2:])
    levels = []
    own = {part: (ab_even, (index,)) for index, part in enumerate(even)}
    received = swap(ab_odd, "head", 1)
    got = {part: (received, (index,)) for index, part in enumerate(even)}
    levels.append((own, got))
    blocks = compose(where, head_bit[0], flat(ab_even), flat(received)).reshape(ab_even.shape)
    current = {part: blocks[index] for index, part in enumerate(even)}
    for bit in range(1, head_bits):
        own, got = {}, {}
        following = {}
        for part in sorted(current):
            if part >> bit & 1:
                continue
            arrived = swap(current[part | 1 << bit], "head", 1 << bit)
            own[part] = (current[part], ())
            got[part] = (arrived, ())
            following[part] = compose(
                where, head_bit[bit], flat(current[part]), flat(arrived)
            ).reshape(arrived.shape)
        levels.append((own, got))
        current = following
    mine = current[0]
    arrived = swap(mine[1], "context", 1)
    x_pair = ((mine[0], ()), (arrived, ()))
    total = compose(where, context_bit[0], mine[0], arrived)
    before = None
    for bit in range(1, context_bits - 1):
        other = swap(total, "context", 1 << bit)
        total, before = doubling(where, context_bit[bit], total, other, before)
    top = context_bit[-1]
    other = swap(total[:, :, size:], "context", 1 << (context_bits - 1))

    def pair(bit, part, turn):
        own, got = levels[bit]
        (a, ai), (b, bi) = own[part], got[part]
        return (a, ai + (turn,)), (b, bi + (turn,))

    states = {}
    waiting = {}
    bits = [context_bit[0]] + [head_bit[bit] for bit in reversed(range(head_bits))]
    outs = descend(
        where,
        bits,
        top,
        (other, before),
        [x_pair] + [pair(bit, 0, 0) for bit in reversed(range(head_bits))],
    )
    states[0, 0] = outs[-1]
    waiting[0, 1] = (head_bits, swap(outs[0], "context", 1))
    for level, bit in enumerate(reversed(range(head_bits))):
        waiting[1 << bit, 0] = (bit, swap(outs[1 + level], "head", 1 << bit))
    while waiting:
        key = max(waiting, key=lambda entry: (waiting[entry][0], entry[1]))
        part, turn = key
        below, state = waiting.pop(key)
        if below == 0:
            states[key] = state
            continue
        bits = [head_bit[bit] for bit in reversed(range(below))]
        outs = descend(where, bits, None, (state,), [pair(bit, part, turn) for bit in reversed(range(below))])
        states[key] = outs[-1]
        for level, bit in enumerate(reversed(range(below))):
            waiting[part | 1 << bit, turn] = (bit, swap(outs[level], "head", 1 << bit))

    result = None
    gain = norm_gain[None, :]
    order = sorted(states, key=lambda entry: (bin(entry[0]).count("1") + entry[1], entry))
    for part, turn in order:
        source, index = qo[part]
        result = finish(where, part, turn, index, states[part, turn], source, gate_input, gain, result)
    return result


def solution(mesh):
    return jax.shard_map(
        functools.partial(body, mesh.shape["head"], mesh.shape["context"]),
        mesh=mesh,
        in_specs=(
            P(("context", "head"), None),
            P(("context", "head"), None),
            P(("context", "head"), None),
            P(("context", "head"), None),
            P(("context", "head"), None),
            P(("context", "head"), None),
            P("head"),
            P(),
            P("context"),
        ),
        out_specs=P(("context", "head"), None),
        check_vma=False,
    )
```

```python
import functools

import jax
import jax.numpy as jnp
from jax import lax
from jax.experimental import pallas as pl
from jax.experimental.pallas import tpu as pltpu
from jax.sharding import PartitionSpec as P

C = 64
F32 = jnp.float32
BF16 = jnp.bfloat16
EXACT = lax.Precision.HIGHEST
VMEM_BYTES = 40 * 1024 * 1024
FETCH_BYTES = 51 * 1024 * 1024
REFETCH_BYTES = 47 * 1024 * 1024
MASKED = -1e30
BASE = 16


def params(limit=VMEM_BYTES):
    return pltpu.CompilerParams(vmem_limit_bytes=limit)


def cost():
    return pl.CostEstimate(flops=10**10, bytes_accessed=10**8, transcendentals=0)


def is_later(bit):
    axis, number = bit
    return jnp.bitwise_and(lax.shift_right_logical(lax.axis_index(axis), number), 1) == 1


def chunk_of(part):
    return jnp.bitwise_xor(lax.axis_index("head"), lax.axis_size("head") - 1 - part)


def parity():
    return jnp.bitwise_and(lax.axis_index("context"), 1)


def dot(a, b):
    return jnp.dot(a, b, preferred_element_type=F32)


def dot_t(a, b):
    return lax.dot_general(a, b, (((1,), (1,)), ((), ())), preferred_element_type=F32)


def whole_vmem():
    return pl.BlockSpec(memory_space=pltpu.VMEM)


def whole_smem():
    return pl.BlockSpec(memory_space=pltpu.SMEM)


def in_hbm():
    return pl.BlockSpec(memory_space=pltpu.HBM)


def masks(tokens):
    row = lax.broadcasted_iota(jnp.int32, (tokens, tokens), 0)
    column = lax.broadcasted_iota(jnp.int32, (tokens, tokens), 1)
    return row, column


def gates_kernel(parts, width, doc_ref, decay_ref, beta_ref, *rest):
    bias_refs, (col_ref, row_ref, gap_ref) = rest[:-3], rest[-3:]
    tokens = decay_ref.shape[1]
    half = width // 2
    row, column = masks(tokens)
    groups = tokens // C
    row_resets = jnp.zeros_like(row)
    column_resets = jnp.zeros_like(row)
    for group in range(groups):
        flag = doc_ref[lax.axis_index("head") * groups + group]
        row_resets = row_resets + jnp.where(row >= group * C, flag, 0)
        column_resets = column_resets + jnp.where(column >= group * C, flag, 0)
    gap_ref[...] = jnp.where(jnp.logical_and(row >= column, row_resets == column_resets), 0.0, MASKED)
    resets = column_resets[: parts * width]
    final = row_resets[tokens - 1 :]
    decay, beta = [], []
    for part in range(parts):
        rows = pl.ds(pl.multiple_of(chunk_of(part) * width, width), width)
        diagonal = row[:width, :width] == column[:width, :width]
        bias = jnp.sum(jnp.where(diagonal, bias_refs[part][...], 0.0), axis=1, keepdims=True)
        decay.append(decay_ref[rows, :] + bias)
        beta.append(beta_ref[rows, :])
    z = jnp.concatenate(decay, axis=0)
    beta = 1.0 / (1.0 + jnp.exp(-jnp.concatenate(beta, axis=0)))
    log_decay = -(jnp.maximum(z, 0.0) + jnp.log1p(jnp.exp(-jnp.abs(z))))
    upper = jnp.where(row <= column, 1.0, 0.0)
    cum = jnp.dot(log_decay, upper, precision=EXACT, preferred_element_type=F32)
    last = jnp.broadcast_to(cum[:, tokens - 1 :], cum.shape)
    gamma = jnp.where(resets == 0, jnp.exp(cum), 0.0)
    back = jnp.where(resets == final, jnp.exp(last - cum), 0.0)
    whole = jnp.where(final == 0, jnp.exp(last), 0.0)
    swapped = parity() == 1
    tall = []
    for part in range(parts):
        sides = [slice(part * width + side * half, part * width + (side + 1) * half) for side in range(2)]
        for turn in range(2):
            same, other = sides[turn], sides[1 - turn]
            for table in (cum, beta, beta * gamma, gamma):
                tall.append(jnp.where(swapped, table[other], table[same]))
            for place, table in enumerate((cum, back, whole)):
                row_ref[part, turn, place * half : (place + 1) * half, :] = jnp.where(
                    swapped, table[other], table[same]
                )
    col_ref[...] = jnp.transpose(jnp.concatenate(tall, axis=0))


def gates(doc_start, decay_rows, beta_rows, biases):
    heads, tokens = decay_rows.shape
    parts = len(biases)
    width = heads // parts
    half = width // 2
    return pl.pallas_call(
        functools.partial(gates_kernel, parts, width),
        out_shape=(
            jax.ShapeDtypeStruct((tokens, 4 * heads), F32),
            jax.ShapeDtypeStruct((parts, 2, 3 * half, tokens), F32),
            jax.ShapeDtypeStruct((tokens, tokens), F32),
        ),
        in_specs=[whole_smem()] + [whole_vmem()] * (2 + parts),
        out_specs=(whole_vmem(),) * 3,
        compiler_params=params(),
        cost_estimate=cost(),
        name="gates",
    )(doc_start, decay_rows, beta_rows, *biases)


def fetch_kernel(parts, half, q_hbm, k_hbm, v_hbm, *rest):
    normed_ref, turned_ref, q_ref, v_ref, k_ref, sems = rest[-6:]
    span = q_ref.shape[-1]
    size = span // half
    copies = {}
    for number, (source, target) in enumerate(((k_hbm, k_ref), (q_hbm, q_ref), (v_hbm, v_ref))):
        for turn in (1, 0):
            for place, part in enumerate(parts):
                at = 2 * chunk_of(part) + jnp.bitwise_xor(turn, parity())
                strip = pl.ds(pl.multiple_of(at * span, span), span)
                copy = pltpu.make_async_copy(
                    source.at[:, strip], target.at[place, turn], sems.at[number, place, turn]
                )
                copy.start()
                copies[number, place, turn] = copy
    for turn in (1, 0):
        for place in range(len(parts)):
            copies[0, place, turn].wait()
            for j in range(half):
                keys = k_ref[place, turn, :, j * size : (j + 1) * size].astype(F32)
                keys = (keys * lax.rsqrt(jnp.sum(keys * keys, axis=-1, keepdims=True) + 1e-06)).astype(BF16)
                normed_ref[place, turn, j] = keys
                turned_ref[place, turn, j] = jnp.transpose(keys)
    for number in (1, 2):
        for turn in (1, 0):
            for place in range(len(parts)):
                copies[number, place, turn].wait()


def fetch(parts, half, size, queries, keys, values, *after):
    tokens = queries.shape[0]
    count = len(parts)
    strips = jax.ShapeDtypeStruct((count, 2, tokens, half * size), BF16)
    return pl.pallas_call(
        functools.partial(fetch_kernel, parts, half),
        out_shape=(
            jax.ShapeDtypeStruct((count, 2, half, tokens, size), BF16),
            jax.ShapeDtypeStruct((count, 2, half, size, tokens), BF16),
            strips,
            strips,
        ),
        in_specs=[in_hbm()] * 3 + [whole_vmem()] * len(after),
        out_specs=(whole_vmem(),) * 4,
        scratch_shapes=[pltpu.VMEM(strips.shape, BF16), pltpu.SemaphoreType.DMA((3, count, 2))],
        compiler_params=params(REFETCH_BYTES if after else FETCH_BYTES),
        cost_estimate=cost(),
        name="fetch",
    )(queries, keys, values, *after)


def local_kernel(part, at, turn, *refs):
    normed_ref, turned_ref, q_ref, v_ref, col_ref, row_ref, gap_ref = refs[:7]
    ab_ref, qo_ref = refs[-2:]
    tokens = gap_ref.shape[0]
    half = ab_ref.shape[0]
    size = ab_ref.shape[1]
    row, column = masks(tokens)
    apart = jnp.bitwise_xor(row, column)
    eye = jnp.where(row == column, 1.0, 0.0)
    strict = row > column
    lane_block = lax.shift_right_logical(column[:BASE], BASE.bit_length() - 1)
    inside = jnp.bitwise_and(column[:BASE], BASE - 1)
    small_eye = jnp.where(row[:BASE] == inside, 1.0, 0.0)
    gap = gap_ref[...]
    every = range(half)

    def tall_of(table, j):
        at = ((2 * part + turn) * 4 + table) * half + j
        return col_ref[:, at : at + 1]

    def wide_of(table, j):
        return row_ref[part, turn, table * half + j : table * half + j + 1, :]

    lower, mix, inverse = [], [], []
    for j in every:
        decay = jnp.exp(tall_of(0, j) - wide_of(0, j) + gap)
        queries = q_ref[at, turn, :, j * size : (j + 1) * size]
        grams = dot(jnp.concatenate([normed_ref[at, turn, j], queries], axis=0), turned_ref[at, turn, j])
        low = jnp.where(strict, tall_of(1, j) * decay * grams[:tokens], 0.0)
        mix.append((decay * grams[tokens:]).astype(BF16))
        packed = jnp.zeros((BASE, tokens), F32)
        for top in range(0, tokens, BASE):
            packed = jnp.where(lane_block == top // BASE, low[top : top + BASE], packed)
        solution_rows = small_eye
        for k in range(BASE - 1):
            factor = jnp.take_along_axis(packed, column[:BASE] - inside + k, axis=1, mode="promise_in_bounds")
            solution_rows = solution_rows - factor * solution_rows[k : k + 1]
        inverse.append(
            jnp.concatenate(
                [jnp.where(lane_block == at_block, solution_rows, 0.0) for at_block in range(tokens // BASE)],
                axis=0,
            )
        )
        lower.append(low.astype(BF16))
    nothing = jnp.zeros((tokens, tokens), BF16)
    block = BASE
    while block < tokens:
        small = [inverse[j].astype(BF16) for j in every]
        step = jnp.logical_and(apart >= block, apart < 2 * block)
        masked = [jnp.where(step, lower[j], nothing) for j in every]
        spans = [slice(top, top + block) for top in range(block, tokens, 2 * block)]

        def odd(array):
            return jnp.concatenate([array[s] for s in spans], axis=0)

        def spread(array, evens):
            pieces = []
            for i, s in enumerate(spans):
                pieces.append(evens[s.start - block : s.start])
                pieces.append(array[i * block : (i + 1) * block])
            return jnp.concatenate(pieces, axis=0)

        inner = [spread(dot(odd(masked[j]), small[j]).astype(BF16), nothing) for j in every]
        inverse = [
            spread(odd(inverse[j]) - dot(odd(small[j]), inner[j]), inverse[j]) for j in every
        ]
        block *= 2
    solved = []
    for j in every:
        lanes = slice(j * size, (j + 1) * size)
        keys = tall_of(2, j) * normed_ref[at, turn, j].astype(F32)
        values = tall_of(1, j) * v_ref[at, turn, :, lanes].astype(F32)
        right = jnp.concatenate([keys.astype(BF16), values.astype(BF16)], axis=1)
        solved.append(dot(inverse[j].astype(BF16), right).astype(BF16))
    for j in every:
        lanes = slice(j * size, (j + 1) * size)
        after = turned_ref[at, turn, j].astype(F32) * wide_of(1, j)
        both = dot(jnp.concatenate([after.astype(BF16), mix[j]], axis=0), solved[j])
        through = tall_of(3, j) * q_ref[at, turn, :, lanes].astype(F32)
        ab_ref[j, :, :size] = (eye * wide_of(2, j) - both[:size, :size]).astype(BF16)
        ab_ref[j, :, size:] = both[:size, size:].astype(BF16)
        qo_ref[j, :, :size] = (through - both[size:, :size]).astype(BF16)
        qo_ref[j, :, size:] = both[size:, size:].astype(BF16)


def local(part, at, turn, prepared, tables, *after):
    half, tokens, size = prepared[0].shape[2:]
    result = jax.ShapeDtypeStruct((half, tokens, 2 * size), BF16)
    arrays = tuple(prepared) + tuple(tables) + after
    return pl.pallas_call(
        functools.partial(local_kernel, part, at, turn),
        out_shape=(result, result),
        in_specs=[whole_vmem()] * len(arrays),
        out_specs=(whole_vmem(), whole_vmem()),
        compiler_params=params(),
        cost_estimate=cost(),
        name="local_tokens",
    )(*arrays)


def joined(earlier, later):
    size = earlier.shape[0]
    product = dot(later[:, :size], earlier)
    return jnp.concatenate([product[:, :size], product[:, size:] + later[:, size:].astype(F32)], axis=1)


def pick(later, own, received):
    return jnp.where(later, received, own), jnp.where(later, own, received)


def compose_kernel(bit, own_ref, got_ref, out_ref):
    later = is_later(bit)
    for j in range(out_ref.shape[0]):
        earlier_block, later_block = pick(later, own_ref[j], got_ref[j])
        out_ref[j] = joined(earlier_block, later_block).astype(BF16)


def compose(bit, own, got):
    return pl.pallas_call(
        functools.partial(compose_kernel, bit),
        out_shape=jax.ShapeDtypeStruct(own.shape, BF16),
        in_specs=[whole_vmem(), whole_vmem()],
        out_specs=whole_vmem(),
        compiler_params=params(),
        cost_estimate=cost(),
        name="compose",
    )(own, got)


def doubling_kernel(bit, first, last, *refs):
    later = is_later(bit)
    own_ref, got_ref = refs[:2]
    total_ref, before_ref = refs[-2:]
    heads, size = own_ref.shape[:2]
    row = lax.broadcasted_iota(jnp.int32, (size, 2 * size), 0)
    column = lax.broadcasted_iota(jnp.int32, (size, 2 * size), 1)
    neutral = jnp.where(row == column, 1.0, 0.0).astype(BF16)
    for j in range(heads):
        earlier_block, later_block = pick(later, own_ref[j], got_ref[j])
        total = joined(earlier_block, later_block).astype(BF16)
        total_ref[j] = total[:, size:] if last else total
        if first:
            before_ref[j] = jnp.where(later, got_ref[j], neutral)
        else:
            before = refs[2][j]
            before_ref[j] = jnp.where(later, joined(got_ref[j], before).astype(BF16), before)


def doubling(bit, last, own, got, before):
    first = before is None
    arrays = (own, got) if first else (own, got, before)
    heads, size = own.shape[:2]
    total = jax.ShapeDtypeStruct((heads, size, size if last else 2 * size), BF16)
    return pl.pallas_call(
        functools.partial(doubling_kernel, bit, first, last),
        out_shape=(total, jax.ShapeDtypeStruct(own.shape, BF16)),
        in_specs=[whole_vmem()] * len(arrays),
        out_specs=(whole_vmem(), whole_vmem()),
        compiler_params=params(),
        cost_estimate=cost(),
        name="doubling",
    )(*arrays)


def descend_kernel(bits, top, threaded, *refs):
    count = len(bits)
    start = 2 if top is not None else 1
    blocks = refs[start : start + 2 * count]
    outs = refs[start + 2 * count + threaded :]
    sends, kept_ref = outs[:count], outs[count]
    size = kept_ref.shape[-1]
    for j in range(kept_ref.shape[0]):
        if top is None:
            state = refs[0][j]
        else:
            before = refs[1][j]
            carried = dot(before[:, :size], refs[0][j]) + before[:, size:].astype(F32)
            state = jnp.where(is_later(top), carried.astype(BF16), before[:, size:])
        for level, bit in enumerate(bits):
            later = is_later(bit)
            earlier = jnp.where(later, blocks[2 * level + 1][j], blocks[2 * level][j])
            after = (dot(earlier[:, :size], state) + earlier[:, size:].astype(F32)).astype(BF16)
            sends[level][j] = jnp.where(later, state, after)
            state = jnp.where(later, after, state)
        kept_ref[j] = state


def descend(bits, top, sources, blocks, thread):
    heads, size = sources[0].shape[0], sources[0].shape[1]
    arrays = list(sources) + [array for pair in blocks for array in pair]
    specs = [whole_vmem()] * len(arrays)
    outs = len(bits) + 1
    shapes = [jax.ShapeDtypeStruct((heads, size, size), BF16)] * outs
    out_specs = [whole_vmem()] * outs
    aliases = {}
    if thread is not None:
        arrays.append(thread)
        specs.append(in_hbm())
        shapes.append(jax.ShapeDtypeStruct(thread.shape, thread.dtype))
        out_specs.append(in_hbm())
        aliases = {len(arrays) - 1: outs}
    return pl.pallas_call(
        functools.partial(descend_kernel, bits, top, int(thread is not None)),
        out_shape=tuple(shapes),
        in_specs=specs,
        out_specs=tuple(out_specs),
        input_output_aliases=aliases,
        compiler_params=params(),
        cost_estimate=cost(),
        name="descend",
    )(*arrays)


def finish_kernel(part, turn, gain_ref, state_ref, qo_ref, gate_hbm, *rest):
    out_hbm, gate_ref, out_ref, sems = rest[-4:]
    half, size = state_ref.shape[0], state_ref.shape[-1]
    span = half * size
    at = 2 * chunk_of(part) + jnp.bitwise_xor(parity(), turn)
    strip = pl.ds(pl.multiple_of(at * span, span), span)
    fetch = pltpu.make_async_copy(gate_hbm.at[:, strip], gate_ref, sems.at[0])
    fetch.start()
    scaled = []
    for j in range(half):
        core = dot(qo_ref[j, :, :size], state_ref[j]) + qo_ref[j, :, size:].astype(F32)
        core = core.astype(BF16).astype(F32)
        scaled.append(
            core * lax.rsqrt(jnp.mean(core * core, axis=-1, keepdims=True) + 1e-06) * gain_ref[...]
        )
    fetch.wait()
    stores = []
    for j in range(half):
        lanes = slice(j * size, (j + 1) * size)
        gate = gate_ref[:, lanes].astype(F32)
        out_ref[:, lanes] = (scaled[j] * (0.5 * gate) * (1.0 + jnp.tanh(0.5 * gate))).astype(BF16)
        there = pl.ds(pl.multiple_of(at * span + j * size, size), size)
        stores.append(pltpu.make_async_copy(out_ref.at[:, lanes], out_hbm.at[:, there], sems.at[1 + j]))
        stores[-1].start()
    for store in stores:
        store.wait()


def finish(part, turn, state, qo, gate, gain, previous):
    half, tokens, size = state.shape[0], gate.shape[0], state.shape[-1]
    specs = [whole_vmem()] * 3 + [in_hbm()]
    arrays = [gain, state, qo, gate]
    aliases = {}
    if previous is not None:
        specs.append(in_hbm())
        arrays.append(previous)
        aliases = {len(arrays) - 1: 0}
    return pl.pallas_call(
        functools.partial(finish_kernel, part, turn),
        out_shape=jax.ShapeDtypeStruct(gate.shape, BF16),
        in_specs=specs,
        out_specs=in_hbm(),
        scratch_shapes=[pltpu.VMEM((tokens, half * size), BF16)] * 2 + [pltpu.SemaphoreType.DMA((1 + half,))],
        input_output_aliases=aliases,
        compiler_params=params(),
        cost_estimate=cost(),
        name="finish",
    )(*arrays)


def body(
    head_count,
    context_count,
    queries,
    key_input,
    value_input,
    gate_input,
    decay_logit,
    beta_logit,
    decay_bias,
    norm_gain,
    doc_start,
):
    head_bits = head_count.bit_length() - 1
    context_bits = context_count.bit_length() - 1

    def swap(array, axis, distance):
        count = head_count if axis == "head" else context_count
        return lax.ppermute(array, axis, [(i, i ^ distance) for i in range(count)])

    head_bit = [("head", bit) for bit in range(head_bits)]
    context_bit = [("context", bit) for bit in range(context_bits)]
    own_bias = decay_bias[None, :]
    biases = [swap(own_bias, "head", head_count - 1 - part) for part in range(head_count - 1)] + [own_bias]
    half, size = decay_bias.shape[0] // 2, norm_gain.shape[0]
    inputs = (queries, key_input, value_input)

    qo = {}
    levels = [{} for _ in range(head_bits)]
    far_parts = list(reversed(range(head_count // 2, head_count)))
    near_parts = [part - head_count // 2 for part in far_parts]
    prepared = {}
    for at, part in enumerate(far_parts):
        if at == 0:
            fetched = fetch(far_parts, half, size, *inputs)
        prepared[part] = (at, fetched)
    tables = gates(doc_start, decay_logit.T, beta_logit.T, biases)

    def climb(part, turn, bit, *after):
        if bit == 0:
            at, fetched = prepared[part]
            block, qo[part, turn] = local(part, at, turn, fetched, tables, *after)
            return block
        far = climb(part | 1 << (bit - 1), turn, bit - 1, *after)
        got = swap(far, "head", 1 << (bit - 1))
        near = climb(part, turn, bit - 1, far)
        levels[bit - 1][part, turn] = (near, got)
        return compose(head_bit[bit - 1], near, got)

    under = head_bits - 1
    far, got, near = {}, {}, {}
    far[1] = climb(1 << under, 1, under)
    got[1] = swap(far[1], "head", 1 << under)
    far[0] = climb(1 << under, 0, under, far[1])
    got[0] = swap(far[0], "head", 1 << under)
    fetched = fetch(near_parts, half, size, *inputs, far[1], far[0])
    for at, part in enumerate(near_parts):
        prepared[part] = (at, fetched)
    near[1] = climb(0, 1, under)
    chip = {1: compose(head_bit[under], near[1], got[1])}
    across = swap(chip[1], "context", 1)
    near[0] = climb(0, 0, under, chip[1])
    chip[0] = compose(head_bit[under], near[0], got[0])
    for turn in (1, 0):
        levels[under][0, turn] = (near[turn], got[turn])

    x_pair = (chip[0], across)
    total = compose(context_bit[0], *x_pair)
    before = None
    for bit in range(1, context_bits - 1):
        other = swap(total, "context", 1 << bit)
        total, before = doubling(context_bit[bit], bit == context_bits - 2, total, other, before)
    other = swap(total, "context", 1 << (context_bits - 1))

    gain = norm_gain[None, :]
    states = {}
    result = None
    descending = list(reversed(range(head_bits)))
    outs = descend(
        [context_bit[0]] + [head_bit[bit] for bit in descending],
        context_bit[-1],
        (other, before),
        [x_pair] + [levels[bit][0, 0] for bit in descending],
        None,
    )
    states[0, 0] = outs[-1]
    arriving = [(0, 1, head_bits, swap(outs[0], "context", 1))]
    for level, bit in enumerate(descending):
        arriving.append((1 << bit, 0, bit, swap(outs[1 + level], "head", 1 << bit)))
    ready = [(0, 0)]
    while arriving or ready:
        for part, turn in ready:
            result = finish(part, turn, states[part, turn], qo[part, turn], gate_input, gain, result)
        ready = []
        leaves = [entry for entry in arriving if entry[2] == 0]
        inner = [entry for entry in arriving if entry[2] > 0]
        arriving = []
        for part, turn, _, state in leaves:
            result = finish(part, turn, state, qo[part, turn], gate_input, gain, result)
        for part, turn, below, state in inner:
            under = list(reversed(range(below)))
            outs = descend(
                        [head_bit[bit] for bit in under],
                None,
                (state,),
                [levels[bit][part, turn] for bit in under],
                result,
            )
            states[part, turn] = outs[below]
            result = outs[-1]
            ready.append((part, turn))
            for level, bit in enumerate(under):
                arriving.append((part | 1 << bit, turn, bit, swap(outs[level], "head", 1 << bit)))
    return result


def solution(mesh):
    return jax.shard_map(
        functools.partial(body, mesh.shape["head"], mesh.shape["context"]),
        mesh=mesh,
        in_specs=(
            P(("context", "head"), None),
            P(("context", "head"), None),
            P(("context", "head"), None),
            P(("context", "head"), None),
            P(("context", "head"), None),
            P(("context", "head"), None),
            P("head"),
            P(),
            P("context"),
        ),
        out_specs=P(("context", "head"), None),
        check_vma=False,
    )
```

```python
import functools

import jax
import jax.numpy as jnp
from jax import lax
from jax.experimental import pallas as pl
from jax.experimental.pallas import tpu as pltpu
from jax.sharding import PartitionSpec as P

C = 64
F32 = jnp.float32
BF16 = jnp.bfloat16
EXACT = lax.Precision.HIGHEST
VMEM_BYTES = 28 * 1024 * 1024
FETCH_BYTES = 52 * 1024 * 1024
REFETCH_BYTES = 47 * 1024 * 1024
MASKED = -1e30
BASE = 16


def params(limit=VMEM_BYTES):
    return pltpu.CompilerParams(vmem_limit_bytes=limit)


def cost(long=True):
    return pl.CostEstimate(flops=10**10 if long else 10**7, bytes_accessed=10**8 if long else 10**5, transcendentals=0)


def is_later(bit):
    axis, number = bit
    return jnp.bitwise_and(lax.shift_right_logical(lax.axis_index(axis), number), 1) == 1


def chunk_of(part):
    return jnp.bitwise_xor(lax.axis_index("head"), lax.axis_size("head") - 1 - part)


def parity():
    return jnp.bitwise_and(lax.axis_index("context"), 1)


def dot(a, b):
    return jnp.dot(a, b, preferred_element_type=F32)


def dot_t(a, b):
    return lax.dot_general(a, b, (((1,), (1,)), ((), ())), preferred_element_type=F32)


def whole_vmem():
    return pl.BlockSpec(memory_space=pltpu.VMEM)


def whole_smem():
    return pl.BlockSpec(memory_space=pltpu.SMEM)


def in_hbm():
    return pl.BlockSpec(memory_space=pltpu.HBM)


def masks(tokens):
    row = lax.broadcasted_iota(jnp.int32, (tokens, tokens), 0)
    column = lax.broadcasted_iota(jnp.int32, (tokens, tokens), 1)
    return row, column


def gates_kernel(parts, bias_rows, width, decay_ref, beta_ref, flag_ref, *rest):
    bias_refs, (col_ref, row_ref) = rest[: len(parts)], rest[-2:]
    tokens = decay_ref.shape[1]
    half = width // 2
    row, column = masks(tokens)
    decay, beta = [], []
    for place, part in enumerate(parts):
        rows = pl.ds(pl.multiple_of(chunk_of(part) * width, width), width)
        diagonal = row[:width, :width] == column[:width, :width]
        bias = bias_refs[place][bias_rows[place] : bias_rows[place] + 1, :width]
        bias = jnp.sum(jnp.where(diagonal, bias, 0.0), axis=1, keepdims=True)
        decay.append(decay_ref[rows, :] + bias)
        beta.append(beta_ref[rows, :])
    z = jnp.concatenate(decay, axis=0)
    beta = 1.0 / (1.0 + jnp.exp(-jnp.concatenate(beta, axis=0)))
    log_decay = -(jnp.maximum(z, 0.0) + jnp.log1p(jnp.exp(-jnp.abs(z))))
    upper = jnp.where(row <= column, 1.0, 0.0)
    cum = jnp.dot(log_decay, upper, precision=EXACT, preferred_element_type=F32)
    last = jnp.broadcast_to(cum[:, tokens - 1 :], cum.shape)
    gamma = jnp.exp(cum) * flag_ref[0, :1]
    back = jnp.exp(last - cum) * flag_ref[1, :1]
    whole = jnp.exp(last) * flag_ref[2, :1]
    swapped = parity() == 1
    tall = []
    for part in range(len(parts)):
        sides = [slice(part * width + side * half, part * width + (side + 1) * half) for side in range(2)]
        for turn in range(2):
            same, other = sides[turn], sides[1 - turn]
            for table in (cum, beta, beta * gamma, gamma):
                tall.append(jnp.where(swapped, table[other], table[same]))
            for place, table in enumerate((cum, back, whole)):
                row_ref[part, turn, place * half : (place + 1) * half, :] = jnp.where(
                    swapped, table[other], table[same]
                )
    col_ref[...] = jnp.transpose(jnp.concatenate(tall, axis=0))


def gates(parts, decay_rows, beta_rows, flags, biases, *after):
    heads, tokens = decay_rows.shape
    bias_rows = [row for _, row in biases]
    width = heads // lax.axis_size("head")
    half = width // 2
    count = len(parts)
    arrays = (decay_rows, beta_rows, flags) + tuple(array for array, _ in biases) + after
    return pl.pallas_call(
        functools.partial(gates_kernel, parts, bias_rows, width),
        out_shape=(
            jax.ShapeDtypeStruct((tokens, 4 * count * width), F32),
            jax.ShapeDtypeStruct((count, 2, 3 * half, tokens), F32),
        ),
        in_specs=[whole_vmem()] * len(arrays),
        out_specs=(whole_vmem(),) * 2,
        compiler_params=params(),
        cost_estimate=cost(),
        name="gates",
    )(*arrays)


def fetch_kernel(parts, half, with_resets, *refs):
    if with_resets:
        doc_ref, refs = refs[0], refs[1:]
    k_hbm, v_hbm = refs[:2]
    k_ref, sems = refs[-2:]
    normed_ref, turned_ref, v_ref = refs[-7:-4] if with_resets else refs[-5:-2]
    span = v_ref.shape[-1]
    size = span // half
    copies = {}
    for number, (source, target) in enumerate(((k_hbm, k_ref), (v_hbm, v_ref))):
        for turn in (1, 0):
            for place, part in enumerate(parts):
                at = 2 * chunk_of(part) + jnp.bitwise_xor(turn, parity())
                strip = pl.ds(pl.multiple_of(at * span, span), span)
                copy = pltpu.make_async_copy(
                    source.at[:, strip], target.at[place, turn], sems.at[number, place, turn]
                )
                copy.start()
                copies[number, place, turn] = copy
    if with_resets:
        gap_ref, flag_ref = refs[-4:-2]
        tokens = gap_ref.shape[0]
        row, column = masks(tokens)
        groups = tokens // C
        row_resets = jnp.zeros_like(row)
        column_resets = jnp.zeros_like(row)
        for group in range(groups):
            flag = doc_ref[lax.axis_index("head") * groups + group]
            row_resets = row_resets + jnp.where(row >= group * C, flag, 0)
            column_resets = column_resets + jnp.where(column >= group * C, flag, 0)
        gap_ref[...] = jnp.where(jnp.logical_and(row >= column, row_resets == column_resets), 0.0, MASKED)
        resets = column_resets[:8]
        final = row_resets[tokens - 8 :]
        flag_ref[0] = jnp.where(resets == 0, 1.0, 0.0)
        flag_ref[1] = jnp.where(resets == final, 1.0, 0.0)
        flag_ref[2] = jnp.where(final == 0, 1.0, 0.0)
    for turn in (1, 0):
        for place in range(len(parts)):
            copies[0, place, turn].wait()
            for j in range(half):
                keys = k_ref[place, turn, :, j * size : (j + 1) * size].astype(F32)
                keys = (keys * lax.rsqrt(jnp.sum(keys * keys, axis=-1, keepdims=True) + 1e-06)).astype(BF16)
                normed_ref[place, turn, j] = keys
                turned_ref[place, turn, j] = jnp.transpose(keys)
    for turn in (1, 0):
        for place in range(len(parts)):
            copies[1, place, turn].wait()


def fetch(parts, half, size, doc_start, keys, values, *after):
    tokens = keys.shape[0]
    count = len(parts)
    strips = jax.ShapeDtypeStruct((count, 2, tokens, half * size), BF16)
    outs = [
        jax.ShapeDtypeStruct((count, 2, half, tokens, size), BF16),
        jax.ShapeDtypeStruct((count, 2, half, size, tokens), BF16),
        strips,
    ]
    specs = [in_hbm()] * 2 + [whole_vmem()] * len(after)
    arrays = [keys, values, *after]
    if doc_start is not None:
        outs += [jax.ShapeDtypeStruct((tokens, tokens), F32), jax.ShapeDtypeStruct((3, 8, tokens), F32)]
        specs = [whole_smem()] + specs
        arrays = [doc_start] + arrays
    return pl.pallas_call(
        functools.partial(fetch_kernel, parts, half, doc_start is not None),
        out_shape=tuple(outs),
        in_specs=specs,
        out_specs=(whole_vmem(),) * len(outs),
        scratch_shapes=[pltpu.VMEM(strips.shape, BF16), pltpu.SemaphoreType.DMA((2, count, 2))],
        compiler_params=params(REFETCH_BYTES if after else FETCH_BYTES),
        cost_estimate=cost(),
        name="fetch",
    )(*arrays)


def local_kernel(units, *refs):
    normed_ref, turned_ref, v_ref, gap_ref, col_ref, row_ref = refs[:6]
    outs = refs[-2 * len(units) :]
    tokens = gap_ref.shape[0]
    half, size = outs[0].shape[:2]
    row, column = masks(tokens)
    apart = jnp.bitwise_xor(row, column)
    eye = jnp.where(row == column, 1.0, 0.0)
    strict = row > column
    lane_block = lax.shift_right_logical(column[:BASE], BASE.bit_length() - 1)
    inside = jnp.bitwise_and(column[:BASE], BASE - 1)
    small_eye = jnp.where(row[:BASE] == inside, 1.0, 0.0)
    gap = gap_ref[...]
    every = range(len(units) * half)

    def unit_of(i):
        return units[i // half] + (i % half,)

    def tall_of(table, i):
        at, turn, j = unit_of(i)
        at = ((2 * at + turn) * 4 + table) * half + j
        return col_ref[:, at : at + 1]

    def wide_of(table, i):
        at, turn, j = unit_of(i)
        return row_ref[at, turn, table * half + j : table * half + j + 1, :]

    lower, inverse = [], []
    for i in every:
        at, turn, j = unit_of(i)
        decay = jnp.exp(tall_of(0, i) - wide_of(0, i) + gap)
        gram = dot(normed_ref[at, turn, j], turned_ref[at, turn, j])
        low = jnp.where(strict, tall_of(1, i) * decay * gram, 0.0)
        packed = jnp.zeros((BASE, tokens), F32)
        for top in range(0, tokens, BASE):
            packed = jnp.where(lane_block == top // BASE, low[top : top + BASE], packed)
        solution_rows = small_eye
        for k in range(BASE - 1):
            factor = jnp.take_along_axis(packed, column[:BASE] - inside + k, axis=1, mode="promise_in_bounds")
            solution_rows = solution_rows - factor * solution_rows[k : k + 1]
        inverse.append(
            jnp.concatenate(
                [jnp.where(lane_block == at_block, solution_rows, 0.0) for at_block in range(tokens // BASE)],
                axis=0,
            )
        )
        lower.append(low.astype(BF16))
    nothing = jnp.zeros((tokens, tokens), BF16)
    block = BASE
    while block < tokens:
        small = [inverse[j].astype(BF16) for j in every]
        step = jnp.logical_and(apart >= block, apart < 2 * block)
        masked = [jnp.where(step, lower[j], nothing) for j in every]
        spans = [slice(top, top + block) for top in range(block, tokens, 2 * block)]

        def odd(array):
            return jnp.concatenate([array[s] for s in spans], axis=0)

        def spread(array, evens):
            pieces = []
            for i, s in enumerate(spans):
                pieces.append(evens[s.start - block : s.start])
                pieces.append(array[i * block : (i + 1) * block])
            return jnp.concatenate(pieces, axis=0)

        inner = [spread(dot(odd(masked[j]), small[j]).astype(BF16), nothing) for j in every]
        inverse = [
            spread(odd(inverse[j]) - dot(odd(small[j]), inner[j]), inverse[j]) for j in every
        ]
        block *= 2
    solved = []
    for i in every:
        at, turn, j = unit_of(i)
        lanes = slice(j * size, (j + 1) * size)
        keys = tall_of(2, i) * normed_ref[at, turn, j].astype(F32)
        values = tall_of(1, i) * v_ref[at, turn, :, lanes].astype(F32)
        right = jnp.concatenate([keys.astype(BF16), values.astype(BF16)], axis=1)
        solved.append(dot(inverse[i].astype(BF16), right).astype(BF16))
    for i in every:
        at, turn, j = unit_of(i)
        ab_ref, solved_ref = outs[2 * (i // half) : 2 * (i // half) + 2]
        solved_ref[j] = solved[i]
        after = turned_ref[at, turn, j].astype(F32) * wide_of(1, i)
        both = dot(after.astype(BF16), solved[i])
        ab_ref[j, :, :size] = (eye * wide_of(2, i) - both[:, :size]).astype(BF16)
        ab_ref[j, :, size:] = both[:, size:].astype(BF16)


def local(units, fetched, gap, tables, *after):
    half, tokens, size = fetched[0].shape[2:]
    result = jax.ShapeDtypeStruct((half, tokens, 2 * size), BF16)
    arrays = tuple(fetched) + (gap,) + tuple(tables) + after
    outs = pl.pallas_call(
        functools.partial(local_kernel, units),
        out_shape=(result,) * (2 * len(units)),
        in_specs=[whole_vmem()] * len(arrays),
        out_specs=(whole_vmem(),) * (2 * len(units)),
        compiler_params=params(),
        cost_estimate=cost(),
        name="local_tokens",
    )(*arrays)
    return [(outs[2 * i], outs[2 * i + 1]) for i in range(len(units))]


def outlook_kernel(at, part, q_hbm, turned_ref, gap_ref, col_ref, row_ref, *refs):
    solved_refs = refs[:2]
    qo_refs = refs[-4:-2]
    q_ref, sems = refs[-2:]
    half, tokens = solved_refs[0].shape[:2]
    size = solved_refs[0].shape[2] // 2
    span = half * size
    copies = []
    for turn in range(2):
        start = (2 * chunk_of(part) + jnp.bitwise_xor(turn, parity())) * span
        strip = pl.ds(pl.multiple_of(start, span), span)
        copies.append(pltpu.make_async_copy(q_hbm.at[:, strip], q_ref.at[turn], sems.at[turn]))
        copies[-1].start()
    gap = gap_ref[...]
    every = [(turn, j) for turn in range(2) for j in range(half)]

    def tall_of(table, turn, j):
        place = ((2 * at + turn) * 4 + table) * half + j
        return col_ref[:, place : place + 1]

    decay = {}
    for turn, j in every:
        decay[turn, j] = jnp.exp(tall_of(0, turn, j) - row_ref[at, turn, j : j + 1, :] + gap)
    for copy in copies:
        copy.wait()
    mix = {}
    for turn, j in every:
        gram = dot(q_ref[turn, :, j * size : (j + 1) * size], turned_ref[at, turn, j])
        mix[turn, j] = (decay[turn, j] * gram).astype(BF16)
    for turn, j in every:
        both = dot(mix[turn, j], solved_refs[turn][j])
        through = tall_of(3, turn, j) * q_ref[turn, :, j * size : (j + 1) * size].astype(F32)
        qo_refs[turn][j, :, :size] = (through - both[:, :size]).astype(BF16)
        qo_refs[turn][j, :, size:] = both[:, size:].astype(BF16)


def outlook(at, part, queries, turned, gap, tables, solved, *after):
    half, tokens, wide = solved[0].shape
    arrays = (queries, turned, gap) + tuple(tables) + tuple(solved) + after
    return pl.pallas_call(
        functools.partial(outlook_kernel, at, part),
        out_shape=(jax.ShapeDtypeStruct(solved[0].shape, BF16),) * 2,
        in_specs=[in_hbm()] + [whole_vmem()] * (len(arrays) - 1),
        out_specs=(whole_vmem(),) * 2,
        scratch_shapes=[pltpu.VMEM((2, tokens, half * wide // 2), BF16), pltpu.SemaphoreType.DMA((2,))],
        compiler_params=params(),
        cost_estimate=cost(),
        name="outlook",
    )(*arrays)


def joined(earlier, later):
    size = earlier.shape[0]
    product = dot(later[:, :size], earlier)
    return jnp.concatenate([product[:, :size], product[:, size:] + later[:, size:].astype(F32)], axis=1)


def pick(later, own, received):
    return jnp.where(later, received, own), jnp.where(later, own, received)


def compose_kernel(bit, with_token, carried, own_ref, got_ref, *rest):
    out_ref = rest[-1]
    if with_token:
        out_ref, token_ref = rest[-2:]
        token_ref[...] = jnp.zeros_like(token_ref)
        for row in range(carried):
            token_ref[row : row + 1, : rest[row].shape[1]] = rest[row][...]
    later = is_later(bit)
    for j in range(out_ref.shape[0]):
        earlier_block, later_block = pick(later, own_ref[j], got_ref[j])
        out_ref[j] = joined(earlier_block, later_block).astype(BF16)


def compose(bit, own, got, *after, with_token=False, carried=0):
    outs = (jax.ShapeDtypeStruct(own.shape, BF16),)
    if with_token:
        outs += (jax.ShapeDtypeStruct((8, 128), F32),)
    done = pl.pallas_call(
        functools.partial(compose_kernel, bit, with_token, carried),
        out_shape=outs,
        in_specs=[whole_vmem()] * (2 + len(after)),
        out_specs=(whole_vmem(),) * len(outs),
        compiler_params=params(),
        cost_estimate=cost(),
        name="compose",
    )(own, got, *after)
    return done if with_token else done[0]


def doubling_kernel(bit, first, last, *refs):
    later = is_later(bit)
    own_ref, got_ref = refs[:2]
    total_ref, before_ref = refs[-2:]
    heads, size = own_ref.shape[:2]
    row = lax.broadcasted_iota(jnp.int32, (size, 2 * size), 0)
    column = lax.broadcasted_iota(jnp.int32, (size, 2 * size), 1)
    neutral = jnp.where(row == column, 1.0, 0.0).astype(BF16)
    for j in range(heads):
        earlier_block, later_block = pick(later, own_ref[j], got_ref[j])
        total = joined(earlier_block, later_block).astype(BF16)
        total_ref[j] = total[:, size:] if last else total
        if first:
            before_ref[j] = jnp.where(later, got_ref[j], neutral)
        else:
            before = refs[2][j]
            before_ref[j] = jnp.where(later, joined(got_ref[j], before).astype(BF16), before)


def doubling(bit, last, own, got, before, *after):
    first = before is None
    arrays = (own, got) if first else (own, got, before)
    arrays += after
    heads, size = own.shape[:2]
    total = jax.ShapeDtypeStruct((heads, size, size if last else 2 * size), BF16)
    return pl.pallas_call(
        functools.partial(doubling_kernel, bit, first, last),
        out_shape=(total, jax.ShapeDtypeStruct(own.shape, BF16)),
        in_specs=[whole_vmem()] * len(arrays),
        out_specs=(whole_vmem(), whole_vmem()),
        compiler_params=params(),
        cost_estimate=cost(),
        name="doubling",
    )(*arrays)


def descend_kernel(bits, top, threaded, with_token, *refs):
    count = len(bits)
    start = 2 if top is not None else 1
    blocks = refs[start : start + 2 * count]
    outs = refs[start + 2 * count + threaded :]
    sends, kept_ref = outs[:count], outs[count]
    if with_token:
        outs[-1][...] = jnp.zeros_like(outs[-1])
    size = kept_ref.shape[-1]
    every = range(kept_ref.shape[0])
    if top is None:
        state = [refs[0][j] for j in every]
    else:
        carried = [dot(refs[1][j, :, :size], refs[0][j]) + refs[1][j, :, size:].astype(F32) for j in every]
        state = [jnp.where(is_later(top), carried[j].astype(BF16), refs[1][j, :, size:]) for j in every]
    for level, bit in enumerate(bits):
        later = is_later(bit)
        own_ref, got_ref = blocks[2 * level : 2 * level + 2]
        earlier = [jnp.where(later, got_ref[j], own_ref[j]) for j in every]
        after = [
            (dot(earlier[j][:, :size], state[j]) + earlier[j][:, size:].astype(F32)).astype(BF16) for j in every
        ]
        for j in every:
            sends[level][j] = jnp.where(later, state[j], after[j])
        state = [jnp.where(later, after[j], state[j]) for j in every]
    for j in every:
        kept_ref[j] = state[j]


def descend(bits, top, sources, blocks, thread, *after, with_token=False):
    heads, size = sources[0].shape[0], sources[0].shape[1]
    arrays = list(sources) + [array for pair in blocks for array in pair]
    specs = [whole_vmem()] * len(arrays)
    outs = len(bits) + 1
    shapes = [jax.ShapeDtypeStruct((heads, size, size), BF16)] * outs
    out_specs = [whole_vmem()] * outs
    aliases = {}
    if thread is not None:
        arrays.append(thread)
        specs.append(whole_vmem())
        shapes.append(jax.ShapeDtypeStruct(thread.shape, thread.dtype))
        out_specs.append(whole_vmem())
        aliases = {len(arrays) - 1: outs}
    if with_token:
        shapes.append(jax.ShapeDtypeStruct((8, 128), F32))
        out_specs.append(whole_vmem())
    arrays += after
    specs += [whole_vmem()] * len(after)
    return pl.pallas_call(
        functools.partial(descend_kernel, bits, top, int(thread is not None) + len(after), with_token),
        out_shape=tuple(shapes),
        in_specs=specs,
        out_specs=tuple(out_specs),
        input_output_aliases=aliases,
        compiler_params=params(),
        cost_estimate=cost(),
        name="descend",
    )(*arrays)


def finish_kernel(unit, earlier_unit, is_last, gain_ref, state_ref, qo_ref, gate_ref, *rest):
    sems = rest[-1]
    strip_ref = rest[-2]
    out_hbm = rest[-3]
    half, size = state_ref.shape[0], state_ref.shape[-1]
    span = half * size

    def start_of(part, turn):
        return (2 * chunk_of(part) + jnp.bitwise_xor(turn, parity())) * span

    stores = []
    if earlier_unit is not None:
        there = pl.ds(pl.multiple_of(start_of(*earlier_unit), span), span)
        stores.append(pltpu.make_async_copy(rest[0], out_hbm.at[:, there], sems.at[half]))
        stores[-1].start()
    cores = []
    for j in range(half):
        core = dot(qo_ref[j, :, :size], state_ref[j]) + qo_ref[j, :, size:].astype(F32)
        cores.append(core.astype(BF16).astype(F32))
    for j in range(half):
        core = cores[j]
        scaled = core * lax.rsqrt(jnp.mean(core * core, axis=-1, keepdims=True) + 1e-06) * gain_ref[...]
        there = pl.ds(pl.multiple_of(start_of(*unit) + j * size, size), size)
        gate = gate_ref[:, there].astype(F32)
        lanes = slice(j * size, (j + 1) * size)
        strip_ref[:, lanes] = (scaled * (0.5 * gate) * (1.0 + jnp.tanh(0.5 * gate))).astype(BF16)
        if is_last:
            stores.append(pltpu.make_async_copy(strip_ref.at[:, lanes], out_hbm.at[:, there], sems.at[j]))
            stores[-1].start()
    for store in stores:
        store.wait()


def finish(unit, is_last, state, qo, gate, gain, previous):
    half, tokens, size = state.shape[0], gate.shape[0], state.shape[-1]
    specs = [whole_vmem()] * 4
    arrays = [gain, state, qo, gate]
    aliases = {}
    earlier_unit = None
    if previous is not None:
        result, strip, earlier_unit = previous
        specs += [whole_vmem()]
        arrays += [strip]
        if result is not None:
            specs += [in_hbm()]
            arrays += [result]
            aliases = {len(arrays) - 1: 0}
    strip_shape = (tokens, half * size)
    outs = (jax.ShapeDtypeStruct(gate.shape, BF16),)
    out_specs = (in_hbm(),)
    scratch = [pltpu.SemaphoreType.DMA((1 + half,))]
    if is_last:
        scratch = [pltpu.VMEM(strip_shape, BF16)] + scratch
    else:
        outs += (jax.ShapeDtypeStruct(strip_shape, BF16),)
        out_specs += (whole_vmem(),)
    done = pl.pallas_call(
        functools.partial(finish_kernel, unit, earlier_unit, is_last),
        out_shape=outs,
        in_specs=specs,
        out_specs=out_specs,
        scratch_shapes=scratch,
        input_output_aliases=aliases,
        compiler_params=params(),
        cost_estimate=cost(),
        name="finish",
    )(*arrays)
    return done[0] if is_last else (done[0], done[1], unit)


def body(
    head_count,
    context_count,
    queries,
    key_input,
    value_input,
    gate_input,
    decay_logit,
    beta_logit,
    decay_bias,
    norm_gain,
    doc_start,
):
    head_bits = head_count.bit_length() - 1
    context_bits = context_count.bit_length() - 1

    def swap(array, axis, distance):
        count = head_count if axis == "head" else context_count
        return lax.ppermute(array, axis, [(i, i ^ distance) for i in range(count)])

    head_bit = [("head", bit) for bit in range(head_bits)]
    context_bit = [("context", bit) for bit in range(context_bits)]
    own_bias = decay_bias[None, :]
    far_biases = [own_bias] + [swap(own_bias, "head", other) for other in range(1, head_count // 2)]
    half, size = decay_bias.shape[0] // 2, norm_gain.shape[0]
    inputs = (key_input, value_input)
    decay_rows, beta_rows = decay_logit.T, beta_logit.T

    ab, solved, qo = {}, {}, {}
    levels = [{} for _ in range(head_bits)]
    far_parts = list(reversed(range(head_count // 2, head_count)))
    near_parts = [part - head_count // 2 for part in far_parts]

    def work(parts, turn, fetched, gap, tables, *after):
        names = far_parts if parts[0] in far_parts else near_parts
        units = [(names.index(part), turn) for part in parts]
        for part, (block, out) in zip(parts, local(units, fetched, gap, tables, *after)):
            ab[part, turn], solved[part, turn] = block, out

    def fold(part, turn, bit, *after, **options):
        if bit == 0:
            return ab[part, turn]
        got = swap(fold(part | 1 << (bit - 1), turn, bit - 1), "head", 1 << (bit - 1))
        near = fold(part, turn, bit - 1)
        levels[bit - 1][part, turn] = (near, got)
        return compose(head_bit[bit - 1], near, got, *after, **options)

    under = head_bits - 1
    *fetched, gap, flags = fetch(far_parts, half, size, doc_start, *inputs)
    tables = gates(far_parts, decay_rows, beta_rows, flags, [(array, 0) for array in far_biases])
    work(far_parts, 1, fetched, gap, tables)
    far, got, near, chip = {}, {}, {}, {}
    first_done = ab[far_parts[-1], 1]
    fetched_near = fetch(near_parts, half, size, None, *inputs, first_done)
    far[1], token = fold(
        1 << under, 1, under, *far_biases, fetched_near[0], with_token=True, carried=len(far_biases)
    )
    near_bias = swap(token, "head", 1 << under)
    got[1] = swap(far[1], "head", 1 << under)
    work(far_parts, 0, fetched, gap, tables, swap(token, "head", 1))
    near_biases = [(near_bias, row) for row in range(len(near_parts))]
    near_tables = gates(near_parts, decay_rows, beta_rows, flags, near_biases, ab[far_parts[-1], 0])
    work(near_parts, 1, fetched_near, gap, near_tables)
    far[0] = fold(1 << under, 0, under)
    got[0] = swap(far[0], "head", 1 << under)
    near[1] = fold(0, 1, under, far[0])
    chip[1], token = compose(head_bit[under], near[1], got[1], with_token=True)
    across = swap(chip[1], "context", 1)
    work(near_parts, 0, fetched_near, gap, near_tables, swap(token, "head", 1))

    def look(part, *after):
        names, data, known = (
            (far_parts, fetched, tables) if part in far_parts else (near_parts, fetched_near, near_tables)
        )
        qo[part, 0], qo[part, 1] = outlook(
            names.index(part), part, queries, data[1], gap, known, (solved[part, 0], solved[part, 1]), *after
        )

    every_part = far_parts + near_parts
    look(every_part[0], ab[near_parts[-1], 0])
    near[0] = fold(0, 0, under, qo[every_part[0], 0])
    chip[0] = compose(head_bit[under], near[0], got[0])
    for turn in (1, 0):
        levels[under][0, turn] = (near[turn], got[turn])

    x_pair = (chip[0], across)
    total = compose(context_bit[0], *x_pair)
    before = None
    for part in every_part[1:]:
        look(part, chip[0])
    for bit in range(1, context_bits - 1):
        other = swap(total, "context", 1 << bit)
        done_by = tuple(qo[part, 0] for part in every_part[1:]) if bit == 1 else ()
        total, before = doubling(context_bit[bit], bit == context_bits - 2, total, other, before, *done_by)
    other = swap(total, "context", 1 << (context_bits - 1))

    gain = norm_gain[None, :]
    states = {}
    result = None
    descending = list(reversed(range(head_bits)))
    first = descend([context_bit[0]], context_bit[-1], (other, before), [x_pair], None, with_token=True)
    arriving = [(0, 1, head_bits, swap(first[0], "context", 1))]
    outs = descend(
        [head_bit[bit] for bit in descending],
        None,
        (first[1],),
        [levels[bit][0, 0] for bit in descending],
        None,
        swap(first[-1], "head", 1),
    )
    states[0, 0] = outs[-1]
    for level, bit in enumerate(descending):
        arriving.append((1 << bit, 0, bit, swap(outs[level], "head", 1 << bit)))
    ready = [(0, 0)]
    total_units = 2 * head_count

    def write(part, turn, result):
        done.append((part, turn))
        return finish(
            (part, turn),
            len(done) == total_units,
            states[part, turn],
            qo[part, turn],
            gate_input,
            gain,
            result,
        )

    done = []
    while arriving or ready:
        for part, turn in ready:
            result = write(part, turn, result)
        ready = []
        leaves = [entry for entry in arriving if entry[2] == 0]
        inner = [entry for entry in arriving if entry[2] > 0]
        arriving = []
        for part, turn, _, state in leaves:
            states[part, turn] = state
            result = write(part, turn, result)
        tokens = ()
        for number, (part, turn, below, state) in enumerate(inner):
            down = list(reversed(range(below)))
            more = number + 1 < len(inner)
            outs = descend(
                [head_bit[bit] for bit in down],
                None,
                (state,),
                [levels[bit][part, turn] for bit in down],
                result[1],
                *tokens,
                with_token=more,
            )
            states[part, turn] = outs[below]
            result = (result[0], outs[below + 1], result[2])
            ready.append((part, turn))
            for level, bit in enumerate(down):
                arriving.append((part | 1 << bit, turn, bit, swap(outs[level], "head", 1 << bit)))
            tokens = (swap(outs[-1], "head", 1),) if more else ()
    return result


def solution(mesh):
    return jax.shard_map(
        functools.partial(body, mesh.shape["head"], mesh.shape["context"]),
        mesh=mesh,
        in_specs=(
            P(("context", "head"), None),
            P(("context", "head"), None),
            P(("context", "head"), None),
            P(("context", "head"), None),
            P(("context", "head"), None),
            P(("context", "head"), None),
            P("head"),
            P(),
            P("context"),
        ),
        out_specs=P(("context", "head"), None),
        check_vma=False,
    )
```

```python
import functools

import jax
import jax.numpy as jnp
from jax import lax
from jax.experimental import pallas as pl
from jax.experimental.pallas import tpu as pltpu
from jax.sharding import PartitionSpec as P

C = 64
F32 = jnp.float32
BF16 = jnp.bfloat16
EXACT = lax.Precision.HIGHEST
VMEM_BYTES = 28 * 1024 * 1024
FETCH_BYTES = 52 * 1024 * 1024
REFETCH_BYTES = 47 * 1024 * 1024
MASKED = -1e30
BASE = 16


def params(limit=VMEM_BYTES):
    return pltpu.CompilerParams(vmem_limit_bytes=limit)


def cost(long=True):
    return pl.CostEstimate(flops=10**10 if long else 10**7, bytes_accessed=10**8 if long else 10**5, transcendentals=0)


def is_later(bit):
    axis, number = bit
    return jnp.bitwise_and(lax.shift_right_logical(lax.axis_index(axis), number), 1) == 1


def chunk_of(part):
    return jnp.bitwise_xor(lax.axis_index("head"), lax.axis_size("head") - 1 - part)


def parity():
    return jnp.bitwise_and(lax.axis_index("context"), 1)


def dot(a, b):
    return jnp.dot(a, b, preferred_element_type=F32)


def dot_t(a, b):
    return lax.dot_general(a, b, (((1,), (1,)), ((), ())), preferred_element_type=F32)


def whole_vmem():
    return pl.BlockSpec(memory_space=pltpu.VMEM)


def whole_smem():
    return pl.BlockSpec(memory_space=pltpu.SMEM)


def in_hbm():
    return pl.BlockSpec(memory_space=pltpu.HBM)


def masks(tokens):
    row = lax.broadcasted_iota(jnp.int32, (tokens, tokens), 0)
    column = lax.broadcasted_iota(jnp.int32, (tokens, tokens), 1)
    return row, column


def gates_kernel(parts, bias_rows, width, decay_ref, beta_ref, flag_ref, *rest):
    bias_refs, (col_ref, row_ref) = rest[: len(parts)], rest[-2:]
    tokens = decay_ref.shape[1]
    half = width // 2
    row, column = masks(tokens)
    decay, beta = [], []
    for place, part in enumerate(parts):
        rows = pl.ds(pl.multiple_of(chunk_of(part) * width, width), width)
        diagonal = row[:width, :width] == column[:width, :width]
        bias = bias_refs[place][bias_rows[place] : bias_rows[place] + 1, :width]
        bias = jnp.sum(jnp.where(diagonal, bias, 0.0), axis=1, keepdims=True)
        decay.append(decay_ref[rows, :] + bias)
        beta.append(beta_ref[rows, :])
    z = jnp.concatenate(decay, axis=0)
    logit = jnp.concatenate(beta, axis=0)
    beta = 1.0 / (1.0 + jnp.exp(-logit))
    log_beta = jnp.minimum(logit, 0.0) - jnp.log1p(jnp.exp(-jnp.abs(logit)))
    log_decay = -(jnp.maximum(z, 0.0) + jnp.log1p(jnp.exp(-jnp.abs(z))))
    upper = jnp.where(row <= column, 1.0, 0.0)
    cum = jnp.dot(log_decay, upper, precision=EXACT, preferred_element_type=F32)
    last = jnp.broadcast_to(cum[:, tokens - 1 :], cum.shape)
    gamma = jnp.exp(cum) * flag_ref[0, :1]
    back = jnp.exp(last - cum) * flag_ref[1, :1]
    whole = jnp.exp(last) * flag_ref[2, :1]
    swapped = parity() == 1
    tall = []
    for part in range(len(parts)):
        sides = [slice(part * width + side * half, part * width + (side + 1) * half) for side in range(2)]
        for turn in range(2):
            same, other = sides[turn], sides[1 - turn]
            for table in (cum, cum + log_beta, gamma):
                tall.append(jnp.where(swapped, table[other], table[same]))
            for place, table in enumerate((cum, back, whole, beta, beta * gamma)):
                row_ref[part, turn, place * half : (place + 1) * half, :] = jnp.where(
                    swapped, table[other], table[same]
                )
    col_ref[...] = jnp.transpose(jnp.concatenate(tall, axis=0))


def gates(parts, decay_rows, beta_rows, flags, biases, *after):
    heads, tokens = decay_rows.shape
    bias_rows = [row for _, row in biases]
    width = heads // lax.axis_size("head")
    half = width // 2
    count = len(parts)
    arrays = (decay_rows, beta_rows, flags) + tuple(array for array, _ in biases) + after
    return pl.pallas_call(
        functools.partial(gates_kernel, parts, bias_rows, width),
        out_shape=(
            jax.ShapeDtypeStruct((tokens, 3 * count * width), F32),
            jax.ShapeDtypeStruct((count, 2, 5 * half, tokens), F32),
        ),
        in_specs=[whole_vmem()] * len(arrays),
        out_specs=(whole_vmem(),) * 2,
        compiler_params=params(),
        cost_estimate=cost(),
        name="gates",
    )(*arrays)


def fetch_kernel(parts, half, with_resets, *refs):
    if with_resets:
        doc_ref, refs = refs[0], refs[1:]
    k_hbm, v_hbm = refs[:2]
    k_ref, sems = refs[-2:]
    normed_ref, turned_ref, v_ref = refs[-7:-4] if with_resets else refs[-5:-2]
    span = v_ref.shape[-1]
    size = span // half
    copies = {}
    for number, (source, target) in enumerate(((k_hbm, k_ref), (v_hbm, v_ref))):
        for turn in (1, 0):
            for place, part in enumerate(parts):
                at = 2 * chunk_of(part) + jnp.bitwise_xor(turn, parity())
                strip = pl.ds(pl.multiple_of(at * span, span), span)
                copy = pltpu.make_async_copy(
                    source.at[:, strip], target.at[place, turn], sems.at[number, place, turn]
                )
                copy.start()
                copies[number, place, turn] = copy
    if with_resets:
        gap_ref, flag_ref = refs[-4:-2]
        tokens = gap_ref.shape[0]
        row, column = masks(tokens)
        groups = tokens // C
        row_resets = jnp.zeros_like(row)
        column_resets = jnp.zeros_like(row)
        for group in range(groups):
            flag = doc_ref[lax.axis_index("head") * groups + group]
            row_resets = row_resets + jnp.where(row >= group * C, flag, 0)
            column_resets = column_resets + jnp.where(column >= group * C, flag, 0)
        gap_ref[...] = jnp.where(jnp.logical_and(row >= column, row_resets == column_resets), 0.0, MASKED)
        resets = column_resets[:8]
        final = row_resets[tokens - 8 :]
        flag_ref[0] = jnp.where(resets == 0, 1.0, 0.0)
        flag_ref[1] = jnp.where(resets == final, 1.0, 0.0)
        flag_ref[2] = jnp.where(final == 0, 1.0, 0.0)
    for turn in (1, 0):
        for place in range(len(parts)):
            copies[0, place, turn].wait()
            for j in range(half):
                keys = k_ref[place, turn, :, j * size : (j + 1) * size].astype(F32)
                keys = (keys * lax.rsqrt(jnp.sum(keys * keys, axis=-1, keepdims=True) + 1e-06)).astype(BF16)
                normed_ref[place, turn, j] = keys
                turned_ref[place, turn, j] = jnp.transpose(keys)
    for turn in (1, 0):
        for place in range(len(parts)):
            copies[1, place, turn].wait()


def fetch(parts, half, size, doc_start, keys, values, *after):
    tokens = keys.shape[0]
    count = len(parts)
    strips = jax.ShapeDtypeStruct((count, 2, tokens, half * size), BF16)
    outs = [
        jax.ShapeDtypeStruct((count, 2, half, tokens, size), BF16),
        jax.ShapeDtypeStruct((count, 2, half, size, tokens), BF16),
        strips,
    ]
    specs = [in_hbm()] * 2 + [whole_vmem()] * len(after)
    arrays = [keys, values, *after]
    if doc_start is not None:
        outs += [jax.ShapeDtypeStruct((tokens, tokens), F32), jax.ShapeDtypeStruct((3, 8, tokens), F32)]
        specs = [whole_smem()] + specs
        arrays = [doc_start] + arrays
    return pl.pallas_call(
        functools.partial(fetch_kernel, parts, half, doc_start is not None),
        out_shape=tuple(outs),
        in_specs=specs,
        out_specs=(whole_vmem(),) * len(outs),
        scratch_shapes=[pltpu.VMEM(strips.shape, BF16), pltpu.SemaphoreType.DMA((2, count, 2))],
        compiler_params=params(REFETCH_BYTES if after else FETCH_BYTES),
        cost_estimate=cost(),
        name="fetch",
    )(*arrays)


def local_kernel(units, *refs):
    normed_ref, turned_ref, v_ref, gap_ref, col_ref, row_ref = refs[:6]
    outs = refs[-2 * len(units) :]
    tokens = gap_ref.shape[0]
    half, size = outs[0].shape[:2]
    row, column = masks(tokens)
    apart = jnp.bitwise_xor(row, column)
    eye = jnp.where(row == column, 1.0, 0.0)
    lane_block = lax.shift_right_logical(column[:BASE], BASE.bit_length() - 1)
    inside = jnp.bitwise_and(column[:BASE], BASE - 1)
    small_eye = jnp.where(row[:BASE] == inside, 1.0, 0.0)
    first_lane = column[:BASE] - inside
    gap = jnp.where(row > column, gap_ref[...], MASKED)
    every = range(len(units) * half)

    def unit_of(i):
        return units[i // half] + (i % half,)

    def tall_of(table, i):
        at, turn, j = unit_of(i)
        at = ((2 * at + turn) * 3 + table) * half + j
        return col_ref[:, at : at + 1]

    def wide_of(table, i):
        at, turn, j = unit_of(i)
        return row_ref[at, turn, table * half + j : table * half + j + 1, :]

    lower, packed = [], []
    for i in every:
        at, turn, j = unit_of(i)
        decay = jnp.exp(tall_of(1, i) - wide_of(0, i) + gap)
        low = decay * dot(normed_ref[at, turn, j], turned_ref[at, turn, j])
        blocks = jnp.zeros((BASE, tokens), F32)
        for top in range(0, tokens, BASE):
            blocks = jnp.where(lane_block == top // BASE, low[top : top + BASE], blocks)
        packed.append(blocks)
        lower.append(low.astype(BF16))
    rows = [[small_eye[top : top + 8] for top in range(0, BASE, 8)] for _ in every]
    for k in range(BASE - 1):
        for i in every:
            pivot = rows[i][k // 8][k % 8 : k % 8 + 1]
            for group in range((k + 1) // 8, BASE // 8):
                block_rows = slice(group * 8, group * 8 + 8)
                factor = jnp.take_along_axis(
                    packed[i][block_rows], first_lane[block_rows] + k, axis=1, mode="promise_in_bounds"
                )
                rows[i][group] = rows[i][group] - factor * pivot
    inverse = []
    for i in every:
        joint = jnp.concatenate(rows[i], axis=0)
        inverse.append(
            jnp.concatenate(
                [jnp.where(lane_block == at_block, joint, 0.0) for at_block in range(tokens // BASE)], axis=0
            )
        )
    nothing = jnp.zeros((tokens, tokens), BF16)
    block = BASE
    while block < tokens:
        small = [inverse[j].astype(BF16) for j in every]
        step = jnp.logical_and(apart >= block, apart < 2 * block)
        masked = [jnp.where(step, lower[j], nothing) for j in every]
        spans = [slice(top, top + block) for top in range(block, tokens, 2 * block)]

        def odd(array):
            return jnp.concatenate([array[s] for s in spans], axis=0)

        def spread(array, evens):
            pieces = []
            for i, s in enumerate(spans):
                pieces.append(evens[s.start - block : s.start])
                pieces.append(array[i * block : (i + 1) * block])
            return jnp.concatenate(pieces, axis=0)

        inner = [spread(dot(odd(masked[j]), small[j]).astype(BF16), nothing) for j in every]
        inverse = [
            spread(odd(inverse[j]) - dot(odd(small[j]), inner[j]), inverse[j]) for j in every
        ]
        block *= 2
    solved = []
    for i in every:
        at, turn, j = unit_of(i)
        lanes = slice(j * size, (j + 1) * size)
        keys = dot((inverse[i] * wide_of(4, i)).astype(BF16), normed_ref[at, turn, j])
        values = dot((inverse[i] * wide_of(3, i)).astype(BF16), v_ref[at, turn, :, lanes])
        solved.append(jnp.concatenate([keys.astype(BF16), values.astype(BF16)], axis=1))
    for i in every:
        at, turn, j = unit_of(i)
        ab_ref, solved_ref = outs[2 * (i // half) : 2 * (i // half) + 2]
        solved_ref[j] = solved[i]
        after = turned_ref[at, turn, j].astype(F32) * wide_of(1, i)
        both = dot(after.astype(BF16), solved[i])
        ab_ref[j, :, :size] = (eye * wide_of(2, i) - both[:, :size]).astype(BF16)
        ab_ref[j, :, size:] = both[:, size:].astype(BF16)


def local(units, fetched, gap, tables, *after):
    half, tokens, size = fetched[0].shape[2:]
    result = jax.ShapeDtypeStruct((half, tokens, 2 * size), BF16)
    arrays = tuple(fetched) + (gap,) + tuple(tables) + after
    outs = pl.pallas_call(
        functools.partial(local_kernel, units),
        out_shape=(result,) * (2 * len(units)),
        in_specs=[whole_vmem()] * len(arrays),
        out_specs=(whole_vmem(),) * (2 * len(units)),
        compiler_params=params(),
        cost_estimate=cost(),
        name="local_tokens",
    )(*arrays)
    return [(outs[2 * i], outs[2 * i + 1]) for i in range(len(units))]


def outlook_kernel(at, part, q_hbm, turned_ref, gap_ref, col_ref, row_ref, gain_ref, *refs):
    solved_refs = refs[:2]
    qo_refs = refs[-5:-3]
    refs[-3][...] = gain_ref[...]
    q_ref, sems = refs[-2:]
    half, tokens = solved_refs[0].shape[:2]
    size = solved_refs[0].shape[2] // 2
    span = half * size
    copies = []
    for turn in range(2):
        start = (2 * chunk_of(part) + jnp.bitwise_xor(turn, parity())) * span
        strip = pl.ds(pl.multiple_of(start, span), span)
        copies.append(pltpu.make_async_copy(q_hbm.at[:, strip], q_ref.at[turn], sems.at[turn]))
        copies[-1].start()
    gap = gap_ref[...]
    every = [(turn, j) for turn in range(2) for j in range(half)]

    def tall_of(table, turn, j):
        place = ((2 * at + turn) * 3 + table) * half + j
        return col_ref[:, place : place + 1]

    decay = {}
    for turn, j in every:
        decay[turn, j] = jnp.exp(tall_of(0, turn, j) - row_ref[at, turn, j : j + 1, :] + gap)
    for copy in copies:
        copy.wait()
    mix = {}
    for turn, j in every:
        gram = dot(q_ref[turn, :, j * size : (j + 1) * size], turned_ref[at, turn, j])
        mix[turn, j] = (decay[turn, j] * gram).astype(BF16)
    for turn, j in every:
        both = dot(mix[turn, j], solved_refs[turn][j])
        through = tall_of(2, turn, j) * q_ref[turn, :, j * size : (j + 1) * size].astype(F32)
        qo_refs[turn][j, :, :size] = (through - both[:, :size]).astype(BF16)
        qo_refs[turn][j, :, size:] = both[:, size:].astype(BF16)


def outlook(at, part, queries, turned, gap, tables, gain, solved, *after):
    half, tokens, wide = solved[0].shape
    arrays = (queries, turned, gap) + tuple(tables) + (gain,) + tuple(solved) + after
    return pl.pallas_call(
        functools.partial(outlook_kernel, at, part),
        out_shape=(jax.ShapeDtypeStruct(solved[0].shape, BF16),) * 2 + (jax.ShapeDtypeStruct(gain.shape, F32),),
        in_specs=[in_hbm()] + [whole_vmem()] * (len(arrays) - 1),
        out_specs=(whole_vmem(),) * 3,
        scratch_shapes=[pltpu.VMEM((2, tokens, half * wide // 2), BF16), pltpu.SemaphoreType.DMA((2,))],
        compiler_params=params(),
        cost_estimate=cost(),
        name="outlook",
    )(*arrays)


def joined(earlier, later):
    size = earlier.shape[0]
    product = dot(later[:, :size], earlier)
    return jnp.concatenate([product[:, :size], product[:, size:] + later[:, size:].astype(F32)], axis=1)


def pick(later, own, received):
    return jnp.where(later, received, own), jnp.where(later, own, received)


def compose_kernel(bit, with_token, carried, own_ref, got_ref, *rest):
    out_ref = rest[-1]
    if with_token:
        out_ref, token_ref = rest[-2:]
        token_ref[...] = jnp.zeros_like(token_ref)
        for row in range(carried):
            token_ref[row : row + 1, : rest[row].shape[1]] = rest[row][...]
    later = is_later(bit)
    for j in range(out_ref.shape[0]):
        earlier_block, later_block = pick(later, own_ref[j], got_ref[j])
        out_ref[j] = joined(earlier_block, later_block).astype(BF16)


def compose(bit, own, got, *after, with_token=False, carried=0):
    outs = (jax.ShapeDtypeStruct(own.shape, BF16),)
    if with_token:
        outs += (jax.ShapeDtypeStruct((8, 128), F32),)
    done = pl.pallas_call(
        functools.partial(compose_kernel, bit, with_token, carried),
        out_shape=outs,
        in_specs=[whole_vmem()] * (2 + len(after)),
        out_specs=(whole_vmem(),) * len(outs),
        compiler_params=params(),
        cost_estimate=cost(),
        name="compose",
    )(own, got, *after)
    return done if with_token else done[0]


def doubling_kernel(bit, first, last, *refs):
    later = is_later(bit)
    own_ref, got_ref = refs[:2]
    total_ref, before_ref = refs[-2:]
    heads, size = own_ref.shape[:2]
    row = lax.broadcasted_iota(jnp.int32, (size, 2 * size), 0)
    column = lax.broadcasted_iota(jnp.int32, (size, 2 * size), 1)
    neutral = jnp.where(row == column, 1.0, 0.0).astype(BF16)
    for j in range(heads):
        earlier_block, later_block = pick(later, own_ref[j], got_ref[j])
        total = joined(earlier_block, later_block).astype(BF16)
        total_ref[j] = total[:, size:] if last else total
        if first:
            before_ref[j] = jnp.where(later, got_ref[j], neutral)
        else:
            before = refs[2][j]
            before_ref[j] = jnp.where(later, joined(got_ref[j], before).astype(BF16), before)


def doubling(bit, last, own, got, before, *after):
    first = before is None
    arrays = (own, got) if first else (own, got, before)
    arrays += after
    heads, size = own.shape[:2]
    total = jax.ShapeDtypeStruct((heads, size, size if last else 2 * size), BF16)
    return pl.pallas_call(
        functools.partial(doubling_kernel, bit, first, last),
        out_shape=(total, jax.ShapeDtypeStruct(own.shape, BF16)),
        in_specs=[whole_vmem()] * len(arrays),
        out_specs=(whole_vmem(), whole_vmem()),
        compiler_params=params(),
        cost_estimate=cost(),
        name="doubling",
    )(*arrays)


def descend_kernel(bits, top, threaded, with_token, *refs):
    count = len(bits)
    start = 2 if top is not None else 1
    blocks = refs[start : start + 2 * count]
    outs = refs[start + 2 * count + threaded :]
    sends, kept_ref = outs[:count], outs[count]
    if with_token:
        outs[-1][...] = jnp.zeros_like(outs[-1])
    size = kept_ref.shape[-1]
    every = range(kept_ref.shape[0])
    if top is None:
        state = [refs[0][j] for j in every]
    else:
        carried = [dot(refs[1][j, :, :size], refs[0][j]) + refs[1][j, :, size:].astype(F32) for j in every]
        state = [jnp.where(is_later(top), carried[j].astype(BF16), refs[1][j, :, size:]) for j in every]
    for level, bit in enumerate(bits):
        later = is_later(bit)
        own_ref, got_ref = blocks[2 * level : 2 * level + 2]
        earlier = [jnp.where(later, got_ref[j], own_ref[j]) for j in every]
        after = [
            (dot(earlier[j][:, :size], state[j]) + earlier[j][:, size:].astype(F32)).astype(BF16) for j in every
        ]
        for j in every:
            sends[level][j] = jnp.where(later, state[j], after[j])
        state = [jnp.where(later, after[j], state[j]) for j in every]
    for j in every:
        kept_ref[j] = state[j]


def descend(bits, top, sources, blocks, thread, *after, with_token=False):
    heads, size = sources[0].shape[0], sources[0].shape[1]
    arrays = list(sources) + [array for pair in blocks for array in pair]
    specs = [whole_vmem()] * len(arrays)
    outs = len(bits) + 1
    shapes = [jax.ShapeDtypeStruct((heads, size, size), BF16)] * outs
    out_specs = [whole_vmem()] * outs
    aliases = {}
    if thread is not None:
        arrays.append(thread)
        specs.append(whole_vmem())
        shapes.append(jax.ShapeDtypeStruct(thread.shape, thread.dtype))
        out_specs.append(whole_vmem())
        aliases = {len(arrays) - 1: outs}
    if with_token:
        shapes.append(jax.ShapeDtypeStruct((8, 128), F32))
        out_specs.append(whole_vmem())
    arrays += after
    specs += [whole_vmem()] * len(after)
    return pl.pallas_call(
        functools.partial(descend_kernel, bits, top, int(thread is not None) + len(after), with_token),
        out_shape=tuple(shapes),
        in_specs=specs,
        out_specs=tuple(out_specs),
        input_output_aliases=aliases,
        compiler_params=params(),
        cost_estimate=cost(),
        name="descend",
    )(*arrays)


def finish_kernel(unit, stored, is_last, gain_ref, state_ref, qo_ref, gate_ref, *rest):
    half, size = state_ref.shape[0], state_ref.shape[-1]
    span = half * size
    strip_ref = rest[-2] if is_last or stored else rest[-1]

    def start_of(part, turn):
        return (2 * chunk_of(part) + jnp.bitwise_xor(turn, parity())) * span

    stores = []
    if stored or is_last:
        out_hbm, sems = rest[-3], rest[-1]
    for number, earlier in enumerate(stored):
        there = pl.ds(pl.multiple_of(start_of(*earlier), span), span)
        stores.append(pltpu.make_async_copy(rest[number], out_hbm.at[:, there], sems.at[half + number]))
        stores[-1].start()
    cores = []
    for j in range(half):
        core = dot(qo_ref[j, :, :size], state_ref[j]) + qo_ref[j, :, size:].astype(F32)
        cores.append(core.astype(BF16).astype(F32))
    for j in range(half):
        core = cores[j]
        scaled = core * lax.rsqrt(jnp.mean(core * core, axis=-1, keepdims=True) + 1e-06) * gain_ref[...]
        there = pl.ds(pl.multiple_of(start_of(*unit) + j * size, size), size)
        gate = gate_ref[:, there].astype(F32)
        lanes = slice(j * size, (j + 1) * size)
        strip_ref[:, lanes] = (scaled * (0.5 * gate) * (1.0 + jnp.tanh(0.5 * gate))).astype(BF16)
        if is_last:
            stores.append(pltpu.make_async_copy(strip_ref.at[:, lanes], out_hbm.at[:, there], sems.at[j]))
            stores[-1].start()
    for store in stores:
        store.wait()


def finish(unit, is_last, state, qo, gate, gain, result, stored, *after):
    half, tokens, size = state.shape[0], gate.shape[0], state.shape[-1]
    arrays = [gain, state, qo, gate] + [strip for strip, _ in stored] + list(after)
    specs = [whole_vmem()] * len(arrays)
    aliases = {}
    if result is not None:
        aliases = {len(arrays): 0}
        arrays.append(result)
        specs.append(in_hbm())
    strip = jax.ShapeDtypeStruct((tokens, half * size), BF16)
    outs, out_specs, scratch = [], [], []
    if stored or is_last:
        outs.append(jax.ShapeDtypeStruct(gate.shape, BF16))
        out_specs.append(in_hbm())
        scratch.append(pltpu.SemaphoreType.DMA((half + len(stored),)))
    if is_last:
        scratch = [pltpu.VMEM(strip.shape, BF16)] + scratch
    else:
        outs.append(strip)
        out_specs.append(whole_vmem())
    done = pl.pallas_call(
        functools.partial(finish_kernel, unit, [earlier for _, earlier in stored], is_last),
        out_shape=tuple(outs),
        in_specs=specs,
        out_specs=tuple(out_specs),
        scratch_shapes=scratch,
        input_output_aliases=aliases,
        compiler_params=params(),
        cost_estimate=cost(),
        name="finish",
    )(*arrays)
    if is_last:
        return done[0], None
    return (done[0], done[1]) if stored else (result, done[0])


def body(
    head_count,
    context_count,
    queries,
    key_input,
    value_input,
    gate_input,
    decay_logit,
    beta_logit,
    decay_bias,
    norm_gain,
    doc_start,
):
    head_bits = head_count.bit_length() - 1
    context_bits = context_count.bit_length() - 1

    def swap(array, axis, distance):
        count = head_count if axis == "head" else context_count
        return lax.ppermute(array, axis, [(i, i ^ distance) for i in range(count)])

    head_bit = [("head", bit) for bit in range(head_bits)]
    context_bit = [("context", bit) for bit in range(context_bits)]
    own_bias = decay_bias[None, :]
    far_biases = [own_bias] + [swap(own_bias, "head", other) for other in range(1, head_count // 2)]
    half, size = decay_bias.shape[0] // 2, norm_gain.shape[0]
    inputs = (key_input, value_input)
    decay_rows, beta_rows = decay_logit.T, beta_logit.T

    ab, solved, qo = {}, {}, {}
    levels = [{} for _ in range(head_bits)]
    far_parts = list(reversed(range(head_count // 2, head_count)))
    near_parts = [part - head_count // 2 for part in far_parts]

    def work(parts, turn, fetched, gap, tables, *after):
        names = far_parts if parts[0] in far_parts else near_parts
        units = [(names.index(part), turn) for part in parts]
        for part, (block, out) in zip(parts, local(units, fetched, gap, tables, *after)):
            ab[part, turn], solved[part, turn] = block, out

    def fold(part, turn, bit, *after, **options):
        if bit == 0:
            return ab[part, turn]
        got = swap(fold(part | 1 << (bit - 1), turn, bit - 1), "head", 1 << (bit - 1))
        near = fold(part, turn, bit - 1)
        levels[bit - 1][part, turn] = (near, got)
        return compose(head_bit[bit - 1], near, got, *after, **options)

    under = head_bits - 1
    *fetched, gap, flags = fetch(far_parts, half, size, doc_start, *inputs)
    tables = gates(far_parts, decay_rows, beta_rows, flags, [(array, 0) for array in far_biases])
    work(far_parts, 1, fetched, gap, tables)
    far, got, near, chip = {}, {}, {}, {}
    first_done = ab[far_parts[-1], 1]
    fetched_near = fetch(near_parts, half, size, None, *inputs, first_done)
    early = swap(flags, "head", 1)
    far[1], token = fold(
        1 << under, 1, under, *far_biases, fetched_near[0], with_token=True, carried=len(far_biases)
    )
    near_bias = swap(token, "head", 1 << under)
    got[1] = swap(far[1], "head", 1 << under)
    work(far_parts, 0, fetched, gap, tables, swap(token, "head", 1))
    near_biases = [(near_bias, row) for row in range(len(near_parts))]
    near_tables = gates(near_parts, decay_rows, beta_rows, flags, near_biases, ab[far_parts[-1], 0])
    work(near_parts, 1, fetched_near, gap, near_tables)
    far[0] = fold(1 << under, 0, under)
    got[0] = swap(far[0], "head", 1 << under)
    near[1] = fold(0, 1, under, far[0])
    chip[1] = compose(head_bit[under], near[1], got[1])
    across = swap(chip[1], "context", 1)
    work(near_parts, 0, fetched_near, gap, near_tables, chip[1], early)

    def look(part, *after):
        names, data, known = (
            (far_parts, fetched, tables) if part in far_parts else (near_parts, fetched_near, near_tables)
        )
        qo[part, 0], qo[part, 1], gain = outlook(
            names.index(part), part, queries, data[1], gap, known, norm_gain[None, :], (solved[part, 0], solved[part, 1]), *after
        )
        return gain

    every_part = far_parts + near_parts
    look(every_part[0], ab[near_parts[-1], 0])
    near[0] = fold(0, 0, under, qo[every_part[0], 0])
    chip[0] = compose(head_bit[under], near[0], got[0])
    for turn in (1, 0):
        levels[under][0, turn] = (near[turn], got[turn])

    x_pair = (chip[0], across)
    total = compose(context_bit[0], *x_pair)
    before = None
    held = [array for level in levels[:under] for pair in level.values() for array in pair]
    for part in every_part[1:]:
        gain = look(part, chip[0], *held)
    for bit in range(1, context_bits - 1):
        other = swap(total, "context", 1 << bit)
        done_by = tuple(qo[part, turn] for part in every_part for turn in (0, 1)) + tuple(held) if bit == 1 else ()
        total, before = doubling(context_bit[bit], bit == context_bits - 2, total, other, before, *done_by)
    other = swap(total, "context", 1 << (context_bits - 1))

    states = {}
    result = None
    descending = list(reversed(range(head_bits)))
    first = descend([context_bit[0]], context_bit[-1], (other, before), [x_pair], None, with_token=True)
    arriving = [(0, 1, head_bits, swap(first[0], "context", 1))]
    outs = descend(
        [head_bit[bit] for bit in descending],
        None,
        (first[1],),
        [levels[bit][0, 0] for bit in descending],
        None,
        swap(first[-1], "head", 1),
    )
    states[0, 0] = outs[-1]
    for level, bit in enumerate(descending):
        arriving.append((1 << bit, 0, bit, swap(outs[level], "head", 1 << bit)))
    ready = [(0, 0)]
    total_units = 2 * head_count

    strips = []

    def write(part, turn, result):
        number = len(strips) + 1
        stored = strips if number == total_units - 1 else strips[-1:] if number == total_units else []
        chained = [strips[-1][0]] if strips and not stored else []
        result, strip = finish(
            (part, turn),
            number == total_units,
            states[part, turn],
            qo[part, turn],
            gate_input,
            gain,
            result,
            list(stored),
            *chained,
        )
        strips.append((strip, (part, turn)))
        return result

    while arriving or ready:
        for part, turn in ready:
            result = write(part, turn, result)
        ready = []
        leaves = [entry for entry in arriving if entry[2] == 0]
        inner = [entry for entry in arriving if entry[2] > 0]
        arriving = []
        for part, turn, _, state in leaves:
            states[part, turn] = state
            result = write(part, turn, result)
        tokens = ()
        for number, (part, turn, below, state) in enumerate(inner):
            down = list(reversed(range(below)))
            more = number + 1 < len(inner)
            outs = descend(
                [head_bit[bit] for bit in down],
                None,
                (state,),
                [levels[bit][part, turn] for bit in down],
                strips[-1][0],
                *tokens,
                with_token=more,
            )
            states[part, turn] = outs[below]
            strips[-1] = (outs[below + 1], strips[-1][1])
            ready.append((part, turn))
            for level, bit in enumerate(down):
                arriving.append((part | 1 << bit, turn, bit, swap(outs[level], "head", 1 << bit)))
            tokens = (swap(outs[-1], "head", 1),) if more else ()
    return result


def solution(mesh):
    return jax.shard_map(
        functools.partial(body, mesh.shape["head"], mesh.shape["context"]),
        mesh=mesh,
        in_specs=(
            P(("context", "head"), None),
            P(("context", "head"), None),
            P(("context", "head"), None),
            P(("context", "head"), None),
            P(("context", "head"), None),
            P(("context", "head"), None),
            P("head"),
            P(),
            P("context"),
        ),
        out_specs=P(("context", "head"), None),
        check_vma=False,
    )
```

```python
import functools

import jax
import jax.numpy as jnp
from jax import lax
from jax.experimental import pallas as pl
from jax.experimental.pallas import tpu as pltpu
from jax.sharding import PartitionSpec as P

C = 64
F32 = jnp.float32
BF16 = jnp.bfloat16
EXACT = lax.Precision.HIGHEST
VMEM_BYTES = 28 * 1024 * 1024
FETCH_BYTES = 52 * 1024 * 1024
REFETCH_BYTES = 47 * 1024 * 1024
MASKED = -1e30
BASE = 16


def params(limit=VMEM_BYTES):
    return pltpu.CompilerParams(vmem_limit_bytes=limit)


def cost(long=True):
    return pl.CostEstimate(flops=10**10 if long else 10**7, bytes_accessed=10**8 if long else 10**5, transcendentals=0)


def is_later(bit):
    axis, number = bit
    return jnp.bitwise_and(lax.shift_right_logical(lax.axis_index(axis), number), 1) == 1


def chunk_of(part):
    return jnp.bitwise_xor(lax.axis_index("head"), lax.axis_size("head") - 1 - part)


def parity():
    return jnp.bitwise_and(lax.shift_right_logical(lax.axis_index("context"), 1), 1)


def quarter_parity():
    return jnp.bitwise_and(lax.axis_index("context"), 1)


def dot(a, b):
    return jnp.dot(a, b, preferred_element_type=F32)


def dot_t(a, b):
    return lax.dot_general(a, b, (((1,), (1,)), ((), ())), preferred_element_type=F32)


def whole_vmem():
    return pl.BlockSpec(memory_space=pltpu.VMEM)


def whole_smem():
    return pl.BlockSpec(memory_space=pltpu.SMEM)


def in_hbm():
    return pl.BlockSpec(memory_space=pltpu.HBM)


def masks(tokens):
    row = lax.broadcasted_iota(jnp.int32, (tokens, tokens), 0)
    column = lax.broadcasted_iota(jnp.int32, (tokens, tokens), 1)
    return row, column


def gates_kernel(parts, bias_rows, width, decay_ref, beta_ref, flag_ref, *rest):
    bias_refs, (col_ref, row_ref) = rest[: len(parts)], rest[-2:]
    tokens = decay_ref.shape[1]
    half = width // 2
    row, column = masks(tokens)
    decay, beta = [], []
    for place, part in enumerate(parts):
        rows = pl.ds(pl.multiple_of(chunk_of(part) * width, width), width)
        diagonal = row[:width, :width] == column[:width, :width]
        bias = bias_refs[place][bias_rows[place] : bias_rows[place] + 1, :width]
        bias = jnp.sum(jnp.where(diagonal, bias, 0.0), axis=1, keepdims=True)
        decay.append(decay_ref[rows, :] + bias)
        beta.append(beta_ref[rows, :])
    z = jnp.concatenate(decay, axis=0)
    logit = jnp.concatenate(beta, axis=0)
    beta = 1.0 / (1.0 + jnp.exp(-logit))
    log_beta = jnp.minimum(logit, 0.0) - jnp.log1p(jnp.exp(-jnp.abs(logit)))
    log_decay = -(jnp.maximum(z, 0.0) + jnp.log1p(jnp.exp(-jnp.abs(z))))
    upper = jnp.where(row <= column, 1.0, 0.0)
    cum = jnp.dot(log_decay, upper, precision=EXACT, preferred_element_type=F32)
    last = jnp.broadcast_to(cum[:, tokens - 1 :], cum.shape)
    gamma = jnp.exp(cum) * flag_ref[0, :1]
    back = jnp.exp(last - cum) * flag_ref[1, :1]
    whole = jnp.exp(last) * flag_ref[2, :1]
    swapped = parity() == 1
    tall = []
    for part in range(len(parts)):
        sides = [slice(part * width + side * half, part * width + (side + 1) * half) for side in range(2)]
        for turn in range(2):
            same, other = sides[turn], sides[1 - turn]
            for table in (cum, cum + log_beta, gamma):
                tall.append(jnp.where(swapped, table[other], table[same]))
            for place, table in enumerate((cum, back, whole, beta, beta * gamma)):
                row_ref[part, turn, place * half : (place + 1) * half, :] = jnp.where(
                    swapped, table[other], table[same]
                )
    col_ref[...] = jnp.transpose(jnp.concatenate(tall, axis=0))


def gates(parts, decay_rows, beta_rows, flags, biases, *after):
    heads, tokens = decay_rows.shape
    bias_rows = [row for _, row in biases]
    width = heads // lax.axis_size("head")
    half = width // 2
    count = len(parts)
    arrays = (decay_rows, beta_rows, flags) + tuple(array for array, _ in biases) + after
    return pl.pallas_call(
        functools.partial(gates_kernel, parts, bias_rows, width),
        out_shape=(
            jax.ShapeDtypeStruct((tokens, 3 * count * width), F32),
            jax.ShapeDtypeStruct((count, 2, 5 * half, tokens), F32),
        ),
        in_specs=[whole_vmem()] * len(arrays),
        out_specs=(whole_vmem(),) * 2,
        compiler_params=params(),
        cost_estimate=cost(),
        name="gates",
    )(*arrays)


def fetch_kernel(parts, half, with_resets, *refs):
    if with_resets:
        doc_ref, refs = refs[0], refs[1:]
    k_hbm, v_hbm = refs[:2]
    k_ref, sems = refs[-2:]
    normed_ref, turned_ref, v_ref = refs[-7:-4] if with_resets else refs[-5:-2]
    span = v_ref.shape[-1]
    size = span // half
    copies = {}
    for number, (source, target) in enumerate(((k_hbm, k_ref), (v_hbm, v_ref))):
        for turn in (1, 0):
            for place, part in enumerate(parts):
                at = 2 * chunk_of(part) + jnp.bitwise_xor(turn, parity())
                strip = pl.ds(pl.multiple_of(at * span, span), span)
                copy = pltpu.make_async_copy(
                    source.at[:, strip], target.at[place, turn], sems.at[number, place, turn]
                )
                copy.start()
                copies[number, place, turn] = copy
    if with_resets:
        gap_ref, flag_ref = refs[-4:-2]
        tokens = gap_ref.shape[0]
        row, column = masks(tokens)
        groups = tokens // C
        row_resets = jnp.zeros_like(row)
        column_resets = jnp.zeros_like(row)
        for group in range(groups):
            flag = doc_ref[lax.axis_index("head") * groups + group]
            row_resets = row_resets + jnp.where(row >= group * C, flag, 0)
            column_resets = column_resets + jnp.where(column >= group * C, flag, 0)
        gap_ref[...] = jnp.where(jnp.logical_and(row >= column, row_resets == column_resets), 0.0, MASKED)
        resets = column_resets[:8]
        final = row_resets[tokens - 8 :]
        flag_ref[0] = jnp.where(resets == 0, 1.0, 0.0)
        flag_ref[1] = jnp.where(resets == final, 1.0, 0.0)
        flag_ref[2] = jnp.where(final == 0, 1.0, 0.0)
    for turn in (1, 0):
        for place in range(len(parts)):
            copies[0, place, turn].wait()
            for j in range(half):
                keys = k_ref[place, turn, :, j * size : (j + 1) * size].astype(F32)
                keys = (keys * lax.rsqrt(jnp.sum(keys * keys, axis=-1, keepdims=True) + 1e-06)).astype(BF16)
                normed_ref[place, turn, j] = keys
                turned_ref[place, turn, j] = jnp.transpose(keys)
    for turn in (1, 0):
        for place in range(len(parts)):
            copies[1, place, turn].wait()


def fetch(parts, half, size, doc_start, keys, values, *after):
    tokens = keys.shape[0]
    count = len(parts)
    strips = jax.ShapeDtypeStruct((count, 2, tokens, half * size), BF16)
    outs = [
        jax.ShapeDtypeStruct((count, 2, half, tokens, size), BF16),
        jax.ShapeDtypeStruct((count, 2, half, size, tokens), BF16),
        strips,
    ]
    specs = [in_hbm()] * 2 + [whole_vmem()] * len(after)
    arrays = [keys, values, *after]
    if doc_start is not None:
        outs += [jax.ShapeDtypeStruct((tokens, tokens), F32), jax.ShapeDtypeStruct((3, 8, tokens), F32)]
        specs = [whole_smem()] + specs
        arrays = [doc_start] + arrays
    return pl.pallas_call(
        functools.partial(fetch_kernel, parts, half, doc_start is not None),
        out_shape=tuple(outs),
        in_specs=specs,
        out_specs=(whole_vmem(),) * len(outs),
        scratch_shapes=[pltpu.VMEM(strips.shape, BF16), pltpu.SemaphoreType.DMA((2, count, 2))],
        compiler_params=params(REFETCH_BYTES if after else FETCH_BYTES),
        cost_estimate=cost(),
        name="fetch",
    )(*arrays)


def local_kernel(units, *refs):
    normed_ref, turned_ref, v_ref, gap_ref, col_ref, row_ref = refs[:6]
    outs = refs[-2 * len(units) :]
    tokens = gap_ref.shape[0]
    half, size = outs[0].shape[:2]
    row, column = masks(tokens)
    apart = jnp.bitwise_xor(row, column)
    eye = jnp.where(row == column, 1.0, 0.0)
    lane_block = lax.shift_right_logical(column[:BASE], BASE.bit_length() - 1)
    inside = jnp.bitwise_and(column[:BASE], BASE - 1)
    small_eye = jnp.where(row[:BASE] == inside, 1.0, 0.0)
    first_lane = column[:BASE] - inside
    gap = jnp.where(row > column, gap_ref[...], MASKED)
    every = range(len(units) * half)

    def unit_of(i):
        return units[i // half] + (i % half,)

    def tall_of(table, i):
        at, turn, j = unit_of(i)
        at = ((2 * at + turn) * 3 + table) * half + j
        return col_ref[:, at : at + 1]

    def wide_of(table, i):
        at, turn, j = unit_of(i)
        return row_ref[at, turn, table * half + j : table * half + j + 1, :]

    lower, packed = [], []
    for i in every:
        at, turn, j = unit_of(i)
        decay = jnp.exp(tall_of(1, i) - wide_of(0, i) + gap)
        low = decay * dot(normed_ref[at, turn, j], turned_ref[at, turn, j])
        blocks = jnp.zeros((BASE, tokens), F32)
        for top in range(0, tokens, BASE):
            blocks = jnp.where(lane_block == top // BASE, low[top : top + BASE], blocks)
        packed.append(blocks)
        lower.append(low.astype(BF16))
    rows = [[small_eye[top : top + 8] for top in range(0, BASE, 8)] for _ in every]
    for k in range(BASE - 1):
        for i in every:
            pivot = rows[i][k // 8][k % 8 : k % 8 + 1]
            for group in range((k + 1) // 8, BASE // 8):
                block_rows = slice(group * 8, group * 8 + 8)
                factor = jnp.take_along_axis(
                    packed[i][block_rows], first_lane[block_rows] + k, axis=1, mode="promise_in_bounds"
                )
                rows[i][group] = rows[i][group] - factor * pivot
    inverse = []
    for i in every:
        joint = jnp.concatenate(rows[i], axis=0)
        inverse.append(
            jnp.concatenate(
                [jnp.where(lane_block == at_block, joint, 0.0) for at_block in range(tokens // BASE)], axis=0
            )
        )
    nothing = jnp.zeros((tokens, tokens), BF16)
    block = BASE
    while block < tokens:
        small = [inverse[j].astype(BF16) for j in every]
        step = jnp.logical_and(apart >= block, apart < 2 * block)
        masked = [jnp.where(step, lower[j], nothing) for j in every]
        spans = [slice(top, top + block) for top in range(block, tokens, 2 * block)]

        def odd(array):
            return jnp.concatenate([array[s] for s in spans], axis=0)

        def spread(array, evens):
            pieces = []
            for i, s in enumerate(spans):
                pieces.append(evens[s.start - block : s.start])
                pieces.append(array[i * block : (i + 1) * block])
            return jnp.concatenate(pieces, axis=0)

        inner = [spread(dot(odd(masked[j]), small[j]).astype(BF16), nothing) for j in every]
        inverse = [
            spread(odd(inverse[j]) - dot(odd(small[j]), inner[j]), inverse[j]) for j in every
        ]
        block *= 2
    solved = []
    for i in every:
        at, turn, j = unit_of(i)
        lanes = slice(j * size, (j + 1) * size)
        keys = dot((inverse[i] * wide_of(4, i)).astype(BF16), normed_ref[at, turn, j])
        values = dot((inverse[i] * wide_of(3, i)).astype(BF16), v_ref[at, turn, :, lanes])
        solved.append(jnp.concatenate([keys.astype(BF16), values.astype(BF16)], axis=1))
    for i in every:
        at, turn, j = unit_of(i)
        ab_ref, solved_ref = outs[2 * (i // half) : 2 * (i // half) + 2]
        solved_ref[j] = solved[i]
        after = turned_ref[at, turn, j].astype(F32) * wide_of(1, i)
        both = dot(after.astype(BF16), solved[i])
        ab_ref[j, :, :size] = (eye * wide_of(2, i) - both[:, :size]).astype(BF16)
        ab_ref[j, :, size:] = both[:, size:].astype(BF16)


def local(units, fetched, gap, tables, *after):
    half, tokens, size = fetched[0].shape[2:]
    result = jax.ShapeDtypeStruct((half, tokens, 2 * size), BF16)
    arrays = tuple(fetched) + (gap,) + tuple(tables) + after
    outs = pl.pallas_call(
        functools.partial(local_kernel, units),
        out_shape=(result,) * (2 * len(units)),
        in_specs=[whole_vmem()] * len(arrays),
        out_specs=(whole_vmem(),) * (2 * len(units)),
        compiler_params=params(),
        cost_estimate=cost(),
        name="local_tokens",
    )(*arrays)
    return [(outs[2 * i], outs[2 * i + 1]) for i in range(len(units))]


def outlook_kernel(at, part, q_hbm, turned_ref, gap_ref, col_ref, row_ref, gain_ref, *refs):
    solved_refs = refs[:2]
    qo_refs = refs[-5:-3]
    refs[-3][...] = gain_ref[...]
    q_ref, sems = refs[-2:]
    half, tokens = solved_refs[0].shape[:2]
    size = solved_refs[0].shape[2] // 2
    span = half * size
    copies = []
    for turn in range(2):
        start = (2 * chunk_of(part) + jnp.bitwise_xor(turn, parity())) * span
        strip = pl.ds(pl.multiple_of(start, span), span)
        copies.append(pltpu.make_async_copy(q_hbm.at[:, strip], q_ref.at[turn], sems.at[turn]))
        copies[-1].start()
    gap = gap_ref[...]
    every = [(turn, j) for turn in range(2) for j in range(half)]

    def tall_of(table, turn, j):
        place = ((2 * at + turn) * 3 + table) * half + j
        return col_ref[:, place : place + 1]

    decay = {}
    for turn, j in every:
        decay[turn, j] = jnp.exp(tall_of(0, turn, j) - row_ref[at, turn, j : j + 1, :] + gap)
    for copy in copies:
        copy.wait()
    mix = {}
    for turn, j in every:
        gram = dot(q_ref[turn, :, j * size : (j + 1) * size], turned_ref[at, turn, j])
        mix[turn, j] = (decay[turn, j] * gram).astype(BF16)
    for turn, j in every:
        both = dot(mix[turn, j], solved_refs[turn][j])
        through = tall_of(2, turn, j) * q_ref[turn, :, j * size : (j + 1) * size].astype(F32)
        qo_refs[turn][j, :, :size] = (through - both[:, :size]).astype(BF16)
        qo_refs[turn][j, :, size:] = both[:, size:].astype(BF16)


def outlook(at, part, queries, turned, gap, tables, gain, solved, *after):
    half, tokens, wide = solved[0].shape
    arrays = (queries, turned, gap) + tuple(tables) + (gain,) + tuple(solved) + after
    return pl.pallas_call(
        functools.partial(outlook_kernel, at, part),
        out_shape=(jax.ShapeDtypeStruct(solved[0].shape, BF16),) * 2 + (jax.ShapeDtypeStruct(gain.shape, F32),),
        in_specs=[in_hbm()] + [whole_vmem()] * (len(arrays) - 1),
        out_specs=(whole_vmem(),) * 3,
        scratch_shapes=[pltpu.VMEM((2, tokens, half * wide // 2), BF16), pltpu.SemaphoreType.DMA((2,))],
        compiler_params=params(),
        cost_estimate=cost(),
        name="outlook",
    )(*arrays)


def joined(earlier, later):
    size = earlier.shape[0]
    product = dot(later[:, :size], earlier)
    return jnp.concatenate([product[:, :size], product[:, size:] + later[:, size:].astype(F32)], axis=1)


def pick(later, own, received):
    return jnp.where(later, received, own), jnp.where(later, own, received)


def compose_kernel(bit, with_token, carried, own_ref, got_ref, *rest):
    out_ref = rest[-1]
    if with_token:
        out_ref, token_ref = rest[-2:]
        token_ref[...] = jnp.zeros_like(token_ref)
        for row in range(carried):
            token_ref[row : row + 1, : rest[row].shape[1]] = rest[row][...]
    later = is_later(bit)
    for j in range(out_ref.shape[0]):
        earlier_block, later_block = pick(later, own_ref[j], got_ref[j])
        out_ref[j] = joined(earlier_block, later_block).astype(BF16)


def compose(bit, own, got, *after, with_token=False, carried=0):
    outs = (jax.ShapeDtypeStruct(own.shape, BF16),)
    if with_token:
        outs += (jax.ShapeDtypeStruct((8, 128), F32),)
    done = pl.pallas_call(
        functools.partial(compose_kernel, bit, with_token, carried),
        out_shape=outs,
        in_specs=[whole_vmem()] * (2 + len(after)),
        out_specs=(whole_vmem(),) * len(outs),
        compiler_params=params(),
        cost_estimate=cost(),
        name="compose",
    )(own, got, *after)
    return done if with_token else done[0]


def split_kernel(bit, own_ref, got_ref, *rest):
    later = is_later(bit)
    quarter = own_ref.shape[0] // 2
    for number, out_ref in enumerate(rest[-2:]):
        first = jnp.bitwise_xor(1 - number, quarter_parity()) * quarter
        for j in range(quarter):
            earlier_block, later_block = pick(later, own_ref[first + j], got_ref[first + j])
            out_ref[j] = joined(earlier_block, later_block).astype(BF16)


def compose_split(bit, own, got, *after):
    part = jax.ShapeDtypeStruct((own.shape[0] // 2,) + own.shape[1:], BF16)
    return pl.pallas_call(
        functools.partial(split_kernel, bit),
        out_shape=(part, part),
        in_specs=[whole_vmem()] * (2 + len(after)),
        out_specs=(whole_vmem(),) * 2,
        compiler_params=params(),
        cost_estimate=cost(),
        name="compose",
    )(own, got, *after)


def place_in_four():
    return jnp.bitwise_and(lax.axis_index("context"), 3)


def choose(index, values):
    chosen = values[0]
    for number in range(1, len(values)):
        chosen = jnp.where(index == number, values[number], chosen)
    return chosen


def four_kernel(last, *refs):
    blocks, (total_ref, before_ref) = refs[:4], refs[-2:]
    heads, size = blocks[0].shape[:2]
    every = range(heads)
    own = place_in_four()
    ordered = [
        [choose(jnp.bitwise_xor(own, place), [ref[j] for ref in blocks]) for j in every] for place in range(4)
    ]
    running = ordered[0]
    for place in range(1, 4):
        for j in every:
            before_ref[place - 1, j] = running[j]
        running = [joined(running[j], ordered[place][j]).astype(BF16) for j in every]
    for j in every:
        total_ref[j] = running[j][:, size:] if last else running[j]


def four(last, blocks, *after):
    heads, size = blocks[0].shape[:2]
    arrays = tuple(blocks) + after
    return pl.pallas_call(
        functools.partial(four_kernel, last),
        out_shape=(
            jax.ShapeDtypeStruct((heads, size, size if last else 2 * size), BF16),
            jax.ShapeDtypeStruct((3,) + blocks[0].shape, BF16),
        ),
        in_specs=[whole_vmem()] * len(arrays),
        out_specs=(whole_vmem(),) * 2,
        compiler_params=params(),
        cost_estimate=cost(),
        name="four",
    )(*arrays)


def spread_kernel(top, with_outer, carried_ref, before_ref, *rest):
    outs = rest[-4:]
    heads, size = carried_ref.shape[:2]
    every = range(heads)
    own = place_in_four()

    def through(block, state):
        return (dot(block[:, :size], state) + block[:, size:].astype(F32)).astype(BF16)

    later = is_later(top)
    if with_outer:
        outer = rest[0]
        state = [
            jnp.where(later, through(outer[j], carried_ref[j]), outer[j, :, size:]) for j in every
        ]
    else:
        state = [jnp.where(later, carried_ref[j], jnp.zeros_like(carried_ref[j])) for j in every]
    entering = [state] + [[through(before_ref[place, j], state[j]) for j in every] for place in range(3)]
    for distance in (3, 2, 1, 0):
        there = jnp.bitwise_xor(own, distance)
        for j in every:
            outs[distance][j] = choose(there, [entering[place][j] for place in range(4)])


def spread(top, carried, before, outer, *after):
    arrays = (carried, before) + (() if outer is None else (outer,)) + after
    return pl.pallas_call(
        functools.partial(spread_kernel, top, outer is not None),
        out_shape=(jax.ShapeDtypeStruct(carried.shape, BF16),) * 4,
        in_specs=[whole_vmem()] * len(arrays),
        out_specs=(whole_vmem(),) * 4,
        compiler_params=params(),
        cost_estimate=cost(),
        name="spread",
    )(*arrays)


def doubling_kernel(bit, first, last, *refs):
    later = is_later(bit)
    own_ref, got_ref = refs[:2]
    total_ref, before_ref = refs[-2:]
    heads, size = own_ref.shape[:2]
    row = lax.broadcasted_iota(jnp.int32, (size, 2 * size), 0)
    column = lax.broadcasted_iota(jnp.int32, (size, 2 * size), 1)
    neutral = jnp.where(row == column, 1.0, 0.0).astype(BF16)
    for j in range(heads):
        earlier_block, later_block = pick(later, own_ref[j], got_ref[j])
        total = joined(earlier_block, later_block).astype(BF16)
        total_ref[j] = total[:, size:] if last else total
        if first:
            before_ref[j] = jnp.where(later, got_ref[j], neutral)
        else:
            before = refs[2][j]
            before_ref[j] = jnp.where(later, joined(got_ref[j], before).astype(BF16), before)


def doubling(bit, last, own, got, before, *after):
    first = before is None
    arrays = (own, got) if first else (own, got, before)
    arrays += after
    heads, size = own.shape[:2]
    total = jax.ShapeDtypeStruct((heads, size, size if last else 2 * size), BF16)
    return pl.pallas_call(
        functools.partial(doubling_kernel, bit, first, last),
        out_shape=(total, jax.ShapeDtypeStruct(own.shape, BF16)),
        in_specs=[whole_vmem()] * len(arrays),
        out_specs=(whole_vmem(), whole_vmem()),
        compiler_params=params(),
        cost_estimate=cost(),
        name="doubling",
    )(*arrays)


def descend_kernel(bits, joint, threaded, with_token, *refs):
    count = len(bits)
    start = 2 if joint else 1
    blocks = refs[start : start + 2 * count]
    outs = refs[start + 2 * count + threaded :]
    sends, kept_ref = outs[:count], outs[count]
    if with_token:
        outs[-1][...] = jnp.zeros_like(outs[-1])
    size = kept_ref.shape[-1]
    every = range(kept_ref.shape[0])
    if joint:
        quarter = refs[0].shape[0]
        flip = quarter_parity() == 1
        state = []
        for j in every:
            same, other = refs[j // quarter], refs[1 - j // quarter]
            state.append(jnp.where(flip, other[j % quarter], same[j % quarter]))
    else:
        state = [refs[0][j] for j in every]
    for level, bit in enumerate(bits):
        later = is_later(bit)
        own_ref, got_ref = blocks[2 * level : 2 * level + 2]
        earlier = [jnp.where(later, got_ref[j], own_ref[j]) for j in every]
        after = [
            (dot(earlier[j][:, :size], state[j]) + earlier[j][:, size:].astype(F32)).astype(BF16) for j in every
        ]
        for j in every:
            sends[level][j] = jnp.where(later, state[j], after[j])
        state = [jnp.where(later, after[j], state[j]) for j in every]
    for j in every:
        kept_ref[j] = state[j]


def descend(bits, sources, blocks, thread, *after, with_token=False):
    heads, size = sum(array.shape[0] for array in sources), sources[0].shape[1]
    arrays = list(sources) + [array for pair in blocks for array in pair]
    specs = [whole_vmem()] * len(arrays)
    outs = len(bits) + 1
    shapes = [jax.ShapeDtypeStruct((heads, size, size), BF16)] * outs
    out_specs = [whole_vmem()] * outs
    aliases = {}
    if thread is not None:
        arrays.append(thread)
        specs.append(whole_vmem())
        shapes.append(jax.ShapeDtypeStruct(thread.shape, thread.dtype))
        out_specs.append(whole_vmem())
        aliases = {len(arrays) - 1: outs}
    if with_token:
        shapes.append(jax.ShapeDtypeStruct((8, 128), F32))
        out_specs.append(whole_vmem())
    arrays += after
    specs += [whole_vmem()] * len(after)
    return pl.pallas_call(
        functools.partial(descend_kernel, bits, len(sources) > 1, int(thread is not None) + len(after), with_token),
        out_shape=tuple(shapes),
        in_specs=specs,
        out_specs=tuple(out_specs),
        input_output_aliases=aliases,
        compiler_params=params(),
        cost_estimate=cost(),
        name="descend",
    )(*arrays)


def finish_kernel(unit, stored, is_last, gain_ref, state_ref, qo_ref, gate_ref, *rest):
    half, size = state_ref.shape[0], state_ref.shape[-1]
    span = half * size
    strip_ref = rest[-2] if is_last or stored else rest[-1]

    def start_of(part, turn):
        return (2 * chunk_of(part) + jnp.bitwise_xor(turn, parity())) * span

    stores = []
    if stored or is_last:
        out_hbm, sems = rest[-3], rest[-1]
    for number, earlier in enumerate(stored):
        there = pl.ds(pl.multiple_of(start_of(*earlier), span), span)
        stores.append(pltpu.make_async_copy(rest[number], out_hbm.at[:, there], sems.at[half + number]))
        stores[-1].start()
    cores = []
    for j in range(half):
        core = dot(qo_ref[j, :, :size], state_ref[j]) + qo_ref[j, :, size:].astype(F32)
        cores.append(core.astype(BF16).astype(F32))
    for j in range(half):
        core = cores[j]
        scaled = core * lax.rsqrt(jnp.mean(core * core, axis=-1, keepdims=True) + 1e-06) * gain_ref[...]
        there = pl.ds(pl.multiple_of(start_of(*unit) + j * size, size), size)
        gate = gate_ref[:, there].astype(F32)
        lanes = slice(j * size, (j + 1) * size)
        strip_ref[:, lanes] = (scaled * (0.5 * gate) * (1.0 + jnp.tanh(0.5 * gate))).astype(BF16)
        if is_last:
            stores.append(pltpu.make_async_copy(strip_ref.at[:, lanes], out_hbm.at[:, there], sems.at[j]))
            stores[-1].start()
    for store in stores:
        store.wait()


def finish(unit, is_last, state, qo, gate, gain, result, stored, *after):
    half, tokens, size = state.shape[0], gate.shape[0], state.shape[-1]
    arrays = [gain, state, qo, gate] + [strip for strip, _ in stored] + list(after)
    specs = [whole_vmem()] * len(arrays)
    aliases = {}
    if result is not None and (stored or is_last):
        aliases = {len(arrays): 0}
        arrays.append(result)
        specs.append(in_hbm())
    strip = jax.ShapeDtypeStruct((tokens, half * size), BF16)
    outs, out_specs, scratch = [], [], []
    if stored or is_last:
        outs.append(jax.ShapeDtypeStruct(gate.shape, BF16))
        out_specs.append(in_hbm())
        scratch.append(pltpu.SemaphoreType.DMA((half + len(stored),)))
    if is_last:
        scratch = [pltpu.VMEM(strip.shape, BF16)] + scratch
    else:
        outs.append(strip)
        out_specs.append(whole_vmem())
    done = pl.pallas_call(
        functools.partial(finish_kernel, unit, [earlier for _, earlier in stored], is_last),
        out_shape=tuple(outs),
        in_specs=specs,
        out_specs=tuple(out_specs),
        scratch_shapes=scratch,
        input_output_aliases=aliases,
        compiler_params=params(),
        cost_estimate=cost(),
        name="finish",
    )(*arrays)
    if is_last:
        return done[0], None
    return (done[0], done[1]) if stored else (result, done[0])


def body(
    head_count,
    context_count,
    queries,
    key_input,
    value_input,
    gate_input,
    decay_logit,
    beta_logit,
    decay_bias,
    norm_gain,
    doc_start,
):
    head_bits = head_count.bit_length() - 1
    context_bits = context_count.bit_length() - 1

    def swap(array, axis, distance):
        count = head_count if axis == "head" else context_count
        return lax.ppermute(array, axis, [(i, i ^ distance) for i in range(count)])

    head_bit = [("head", bit) for bit in range(head_bits)]
    context_bit = [("context", bit) for bit in range(context_bits)]
    own_bias = decay_bias[None, :]
    far_biases = [own_bias] + [swap(own_bias, "head", other) for other in range(1, head_count // 2)]
    half, size = decay_bias.shape[0] // 2, norm_gain.shape[0]
    inputs = (key_input, value_input)
    decay_rows, beta_rows = decay_logit.T, beta_logit.T

    ab, solved, qo = {}, {}, {}
    levels = [{} for _ in range(head_bits)]
    far_parts = list(reversed(range(head_count // 2, head_count)))
    near_parts = [part - head_count // 2 for part in far_parts]

    def work(parts, turn, fetched, gap, tables, *after):
        names = far_parts if parts[0] in far_parts else near_parts
        units = [(names.index(part), turn) for part in parts]
        for part, (block, out) in zip(parts, local(units, fetched, gap, tables, *after)):
            ab[part, turn], solved[part, turn] = block, out

    def fold(part, turn, bit, *after, **options):
        if bit == 0:
            return ab[part, turn]
        got = swap(fold(part | 1 << (bit - 1), turn, bit - 1), "head", 1 << (bit - 1))
        near = fold(part, turn, bit - 1)
        levels[bit - 1][part, turn] = (near, got)
        return compose(head_bit[bit - 1], near, got, *after, **options)

    under = head_bits - 1
    *fetched, gap, flags = fetch(far_parts, half, size, doc_start, *inputs)
    tables = gates(far_parts, decay_rows, beta_rows, flags, [(array, 0) for array in far_biases])
    work(far_parts, 1, fetched, gap, tables)
    far, got, near, chip = {}, {}, {}, {}
    first_done = ab[far_parts[-1], 1]
    fetched_near = fetch(near_parts, half, size, None, *inputs, first_done)
    far[1], token = fold(
        1 << under, 1, under, *far_biases, fetched_near[0], with_token=True, carried=len(far_biases)
    )
    near_bias = swap(token, "head", 1 << under)
    got[1] = swap(far[1], "head", 1 << under)
    work(far_parts, 0, fetched, gap, tables, swap(token, "head", 1))
    near_biases = [(near_bias, row) for row in range(len(near_parts))]
    near_tables = gates(near_parts, decay_rows, beta_rows, flags, near_biases, ab[far_parts[-1], 0])
    work(near_parts, 1, fetched_near, gap, near_tables)
    far[0] = fold(1 << under, 0, under)
    got[0] = swap(far[0], "head", 1 << under)
    near[1] = fold(0, 1, under, far[0])
    to_three, to_two = compose_split(head_bit[under], near[1], got[1])
    from_three = swap(to_three, "context", 3)
    from_two = swap(to_two, "context", 2)
    work(near_parts, 0, fetched_near, gap, near_tables, ab[near_parts[-1], 1], far[0])

    def look(part, *after):
        names, data, known = (
            (far_parts, fetched, tables) if part in far_parts else (near_parts, fetched_near, near_tables)
        )
        qo[part, 0], qo[part, 1], gain = outlook(
            names.index(part), part, queries, data[1], gap, known, norm_gain[None, :], (solved[part, 0], solved[part, 1]), *after
        )
        return gain

    every_part = far_parts + near_parts
    near[0] = fold(0, 0, under)
    to_one, mine = compose_split(head_bit[under], near[0], got[0])
    from_one = swap(to_one, "context", 1)
    for turn in (1, 0):
        levels[under][0, turn] = (near[turn], got[turn])

    for part in every_part[:2]:
        look(part, mine)
    only_last = context_bits == 3
    outlooks = [qo[part, 0] for part in every_part[:2]]
    total, before = four(only_last, (mine, from_one, from_two, from_three), *outlooks)
    outer = None
    held = [array for level in levels[:under] for pair in level.values() for array in pair]
    for part in every_part[2:]:
        gain = look(part, total, *held)
    done_by = [qo[part, turn] for part in every_part for turn in (0, 1)] + held
    for bit in range(2, context_bits - 1):
        other = swap(total, "context", 1 << bit)
        total, outer = doubling(context_bit[bit], bit == context_bits - 2, total, other, outer)
    other = swap(total, "context", 1 << (context_bits - 1))

    states = {}
    entering = spread(context_bit[-1], other, before, outer, gate_input, *done_by)
    from_far = {distance: swap(entering[distance], "context", distance) for distance in (3, 2, 1)}
    total_units = 2 * head_count
    strips, waiting, results = [], [], [None]

    def write(part, turn):
        number = len(strips) + 1
        stored = []
        if number in (total_units // 2, total_units - 1, total_units):
            stored, waiting[:] = waiting[:], []
        chained = [strips[-1][0]] if strips and not stored else []
        result, strip = finish(
            (part, turn),
            number == total_units,
            states[part, turn],
            qo[part, turn],
            gate_input,
            gain,
            results[-1],
            [(strips[entry][0], strips[entry][1]) for entry in stored],
            *chained,
        )
        results.append(result)
        waiting.append(len(strips))
        strips.append((strip, (part, turn)))

    leaves = []
    inner = [
        (0, 0, head_bits, (entering[0], from_far[1])),
        (0, 1, head_bits, (from_far[2], from_far[3])),
    ]

    def pass_on(part, turn, below, sources):
        down = list(reversed(range(below)))
        outs = descend(
            [head_bit[bit] for bit in down],
            sources,
            [levels[bit][part, turn] for bit in down],
            strips[-1][0] if strips else None,
        )
        states[part, turn] = outs[below]
        if strips:
            strips[-1] = (outs[below + 1], strips[-1][1])
        for level, bit in enumerate(down):
            entry = (part | 1 << bit, turn, bit, (swap(outs[level], "head", 1 << bit),))
            (inner if bit else leaves).append(entry)

    def write_leaves(entries):
        for part, turn, _, (state,) in entries:
            states[part, turn] = state
            write(part, turn)

    depth = head_bits
    while inner:
        inner.sort(key=lambda entry: (-entry[2], entry[1]))
        part, turn, below, sources = inner.pop(0)
        if below < depth or turn and below == head_bits:
            write_leaves(leaves)
            leaves.clear()
            depth = below
        known = len(leaves)
        pass_on(part, turn, below, sources)
        if not inner:
            write_leaves(leaves[:known])
            del leaves[:known]
        write(part, turn)
    write_leaves(leaves)
    return results[-1]


def solution(mesh):
    return jax.shard_map(
        functools.partial(body, mesh.shape["head"], mesh.shape["context"]),
        mesh=mesh,
        in_specs=(
            P(("context", "head"), None),
            P(("context", "head"), None),
            P(("context", "head"), None),
            P(("context", "head"), None),
            P(("context", "head"), None),
            P(("context", "head"), None),
            P("head"),
            P(),
            P("context"),
        ),
        out_specs=P(("context", "head"), None),
        check_vma=False,
    )
```

```python
import functools

import jax
import jax.numpy as jnp
from jax import lax
from jax.experimental import pallas as pl
from jax.experimental.pallas import tpu as pltpu
from jax.sharding import PartitionSpec as P

C = 64
F32 = jnp.float32
BF16 = jnp.bfloat16
EXACT = lax.Precision.HIGHEST
VMEM_BYTES = 28 * 1024 * 1024
FETCH_BYTES = 52 * 1024 * 1024
REFETCH_BYTES = 47 * 1024 * 1024
MASKED = -1e30
BASE = 16


def params(limit=VMEM_BYTES):
    return pltpu.CompilerParams(vmem_limit_bytes=limit)


def cost(long=True):
    return pl.CostEstimate(flops=10**10 if long else 10**7, bytes_accessed=10**8 if long else 10**5, transcendentals=0)


def is_later(bit):
    axis, number = bit
    return jnp.bitwise_and(lax.shift_right_logical(lax.axis_index(axis), number), 1) == 1


def chunk_of(part):
    return jnp.bitwise_xor(lax.axis_index("head"), lax.axis_size("head") - 1 - part)


def parity():
    return jnp.bitwise_and(lax.shift_right_logical(lax.axis_index("context"), 1), 1)


def quarter_parity():
    return jnp.bitwise_and(lax.axis_index("context"), 1)


def dot(a, b):
    return jnp.dot(a, b, preferred_element_type=F32)


def dot_t(a, b):
    return lax.dot_general(a, b, (((1,), (1,)), ((), ())), preferred_element_type=F32)


def whole_vmem():
    return pl.BlockSpec(memory_space=pltpu.VMEM)


def whole_smem():
    return pl.BlockSpec(memory_space=pltpu.SMEM)


def in_hbm():
    return pl.BlockSpec(memory_space=pltpu.HBM)


def masks(tokens):
    row = lax.broadcasted_iota(jnp.int32, (tokens, tokens), 0)
    column = lax.broadcasted_iota(jnp.int32, (tokens, tokens), 1)
    return row, column


def gates_kernel(parts, bias_rows, width, decay_ref, beta_ref, flag_ref, *rest):
    bias_refs, (col_ref, row_ref) = rest[: len(parts)], rest[-2:]
    tokens = decay_ref.shape[1]
    half = width // 2
    row, column = masks(tokens)
    decay, beta = [], []
    for place, part in enumerate(parts):
        rows = pl.ds(pl.multiple_of(chunk_of(part) * width, width), width)
        diagonal = row[:width, :width] == column[:width, :width]
        bias = bias_refs[place][bias_rows[place] : bias_rows[place] + 1, :width]
        bias = jnp.sum(jnp.where(diagonal, bias, 0.0), axis=1, keepdims=True)
        decay.append(decay_ref[rows, :] + bias)
        beta.append(beta_ref[rows, :])
    z = jnp.concatenate(decay, axis=0)
    logit = jnp.concatenate(beta, axis=0)
    beta = 1.0 / (1.0 + jnp.exp(-logit))
    log_beta = jnp.minimum(logit, 0.0) - jnp.log1p(jnp.exp(-jnp.abs(logit)))
    log_decay = -(jnp.maximum(z, 0.0) + jnp.log1p(jnp.exp(-jnp.abs(z))))
    upper = jnp.where(row <= column, 1.0, 0.0)
    cum = jnp.dot(log_decay, upper, precision=EXACT, preferred_element_type=F32)
    last = jnp.broadcast_to(cum[:, tokens - 1 :], cum.shape)
    gamma = jnp.exp(cum) * flag_ref[0, :1]
    back = jnp.exp(last - cum) * flag_ref[1, :1]
    whole = jnp.exp(last) * flag_ref[2, :1]
    swapped = parity() == 1
    tall = []
    for part in range(len(parts)):
        sides = [slice(part * width + side * half, part * width + (side + 1) * half) for side in range(2)]
        for turn in range(2):
            same, other = sides[turn], sides[1 - turn]
            for table in (cum, cum + log_beta, gamma):
                tall.append(jnp.where(swapped, table[other], table[same]))
            for place, table in enumerate((cum, back, whole, beta, beta * gamma)):
                row_ref[part, turn, place * half : (place + 1) * half, :] = jnp.where(
                    swapped, table[other], table[same]
                )
    col_ref[...] = jnp.transpose(jnp.concatenate(tall, axis=0))


def gates(parts, decay_rows, beta_rows, flags, biases, *after):
    heads, tokens = decay_rows.shape
    bias_rows = [row for _, row in biases]
    width = heads // lax.axis_size("head")
    half = width // 2
    count = len(parts)
    arrays = (decay_rows, beta_rows, flags) + tuple(array for array, _ in biases) + after
    return pl.pallas_call(
        functools.partial(gates_kernel, parts, bias_rows, width),
        out_shape=(
            jax.ShapeDtypeStruct((tokens, 3 * count * width), F32),
            jax.ShapeDtypeStruct((count, 2, 5 * half, tokens), F32),
        ),
        in_specs=[whole_vmem()] * len(arrays),
        out_specs=(whole_vmem(),) * 2,
        compiler_params=params(),
        cost_estimate=cost(False),
        name="gates",
    )(*arrays)


def fetch_kernel(parts, half, with_resets, *refs):
    if with_resets:
        doc_ref, refs = refs[0], refs[1:]
    k_hbm, v_hbm = refs[:2]
    k_ref, sems = refs[-2:]
    normed_ref, turned_ref, v_ref = refs[-7:-4] if with_resets else refs[-5:-2]
    span = v_ref.shape[-1]
    size = span // half
    copies = {}
    for number, (source, target) in enumerate(((k_hbm, k_ref), (v_hbm, v_ref))):
        for turn in (1, 0):
            for place, part in enumerate(parts):
                at = 2 * chunk_of(part) + jnp.bitwise_xor(turn, parity())
                strip = pl.ds(pl.multiple_of(at * span, span), span)
                copy = pltpu.make_async_copy(
                    source.at[:, strip], target.at[place, turn], sems.at[number, place, turn]
                )
                copy.start()
                copies[number, place, turn] = copy
    if with_resets:
        gap_ref, flag_ref = refs[-4:-2]
        tokens = gap_ref.shape[0]
        row, column = masks(tokens)
        groups = tokens // C
        row_resets = jnp.zeros_like(row)
        column_resets = jnp.zeros_like(row)
        for group in range(groups):
            flag = doc_ref[lax.axis_index("head") * groups + group]
            row_resets = row_resets + jnp.where(row >= group * C, flag, 0)
            column_resets = column_resets + jnp.where(column >= group * C, flag, 0)
        gap_ref[...] = jnp.where(jnp.logical_and(row >= column, row_resets == column_resets), 0.0, MASKED)
        resets = column_resets[:8]
        final = row_resets[tokens - 8 :]
        flag_ref[0] = jnp.where(resets == 0, 1.0, 0.0)
        flag_ref[1] = jnp.where(resets == final, 1.0, 0.0)
        flag_ref[2] = jnp.where(final == 0, 1.0, 0.0)
    for turn in (1, 0):
        for place in range(len(parts)):
            copies[0, place, turn].wait()
            for j in range(half):
                keys = k_ref[place, turn, :, j * size : (j + 1) * size].astype(F32)
                keys = (keys * lax.rsqrt(jnp.sum(keys * keys, axis=-1, keepdims=True) + 1e-06)).astype(BF16)
                normed_ref[place, turn, j] = keys
                turned_ref[place, turn, j] = jnp.transpose(keys)
    for turn in (1, 0):
        for place in range(len(parts)):
            copies[1, place, turn].wait()


def fetch(parts, half, size, doc_start, keys, values, *after):
    tokens = keys.shape[0]
    count = len(parts)
    strips = jax.ShapeDtypeStruct((count, 2, tokens, half * size), BF16)
    outs = [
        jax.ShapeDtypeStruct((count, 2, half, tokens, size), BF16),
        jax.ShapeDtypeStruct((count, 2, half, size, tokens), BF16),
        strips,
    ]
    specs = [in_hbm()] * 2 + [whole_vmem()] * len(after)
    arrays = [keys, values, *after]
    if doc_start is not None:
        outs += [jax.ShapeDtypeStruct((tokens, tokens), F32), jax.ShapeDtypeStruct((3, 8, tokens), F32)]
        specs = [whole_smem()] + specs
        arrays = [doc_start] + arrays
    return pl.pallas_call(
        functools.partial(fetch_kernel, parts, half, doc_start is not None),
        out_shape=tuple(outs),
        in_specs=specs,
        out_specs=(whole_vmem(),) * len(outs),
        scratch_shapes=[pltpu.VMEM(strips.shape, BF16), pltpu.SemaphoreType.DMA((2, count, 2))],
        compiler_params=params(REFETCH_BYTES if after else FETCH_BYTES),
        cost_estimate=cost(),
        name="fetch",
    )(*arrays)


def local_kernel(units, *refs):
    normed_ref, turned_ref, v_ref, gap_ref, col_ref, row_ref = refs[:6]
    outs = refs[-2 * len(units) :]
    tokens = gap_ref.shape[0]
    half, size = outs[0].shape[:2]
    row, column = masks(tokens)
    apart = jnp.bitwise_xor(row, column)
    eye = jnp.where(row == column, 1.0, 0.0)
    lane_block = lax.shift_right_logical(column[:BASE], BASE.bit_length() - 1)
    inside = jnp.bitwise_and(column[:BASE], BASE - 1)
    small_eye = jnp.where(row[:BASE] == inside, 1.0, 0.0)
    first_lane = column[:BASE] - inside
    gap = jnp.where(row > column, gap_ref[...], MASKED)
    every = range(len(units) * half)

    def unit_of(i):
        return units[i // half] + (i % half,)

    def tall_of(table, i):
        at, turn, j = unit_of(i)
        at = ((2 * at + turn) * 3 + table) * half + j
        return col_ref[:, at : at + 1]

    def wide_of(table, i):
        at, turn, j = unit_of(i)
        return row_ref[at, turn, table * half + j : table * half + j + 1, :]

    lower, packed = [], []
    for i in every:
        at, turn, j = unit_of(i)
        decay = jnp.exp(tall_of(1, i) - wide_of(0, i) + gap)
        low = decay * dot(normed_ref[at, turn, j], turned_ref[at, turn, j])
        blocks = jnp.zeros((BASE, tokens), F32)
        for top in range(0, tokens, BASE):
            blocks = jnp.where(lane_block == top // BASE, low[top : top + BASE], blocks)
        packed.append(blocks)
        lower.append(low.astype(BF16))
    rows = [[small_eye[top : top + 8] for top in range(0, BASE, 8)] for _ in every]
    for k in range(BASE - 1):
        for i in every:
            pivot = rows[i][k // 8][k % 8 : k % 8 + 1]
            for group in range((k + 1) // 8, BASE // 8):
                block_rows = slice(group * 8, group * 8 + 8)
                factor = jnp.take_along_axis(
                    packed[i][block_rows], first_lane[block_rows] + k, axis=1, mode="promise_in_bounds"
                )
                rows[i][group] = rows[i][group] - factor * pivot
    inverse = []
    for i in every:
        joint = jnp.concatenate(rows[i], axis=0)
        inverse.append(
            jnp.concatenate(
                [jnp.where(lane_block == at_block, joint, 0.0) for at_block in range(tokens // BASE)], axis=0
            )
        )
    nothing = jnp.zeros((tokens, tokens), BF16)
    block = BASE
    while block < tokens:
        small = [inverse[j].astype(BF16) for j in every]
        step = jnp.logical_and(apart >= block, apart < 2 * block)
        masked = [jnp.where(step, lower[j], nothing) for j in every]
        spans = [slice(top, top + block) for top in range(block, tokens, 2 * block)]

        def odd(array):
            return jnp.concatenate([array[s] for s in spans], axis=0)

        def spread(array, evens):
            pieces = []
            for i, s in enumerate(spans):
                pieces.append(evens[s.start - block : s.start])
                pieces.append(array[i * block : (i + 1) * block])
            return jnp.concatenate(pieces, axis=0)

        inner = [spread(dot(odd(masked[j]), small[j]).astype(BF16), nothing) for j in every]
        inverse = [
            spread(odd(inverse[j]) - dot(odd(small[j]), inner[j]), inverse[j]) for j in every
        ]
        block *= 2
    solved = []
    for i in every:
        at, turn, j = unit_of(i)
        lanes = slice(j * size, (j + 1) * size)
        keys = dot((inverse[i] * wide_of(4, i)).astype(BF16), normed_ref[at, turn, j])
        values = dot((inverse[i] * wide_of(3, i)).astype(BF16), v_ref[at, turn, :, lanes])
        solved.append(jnp.concatenate([keys.astype(BF16), values.astype(BF16)], axis=1))
    for i in every:
        at, turn, j = unit_of(i)
        ab_ref, solved_ref = outs[2 * (i // half) : 2 * (i // half) + 2]
        solved_ref[j] = solved[i]
        after = turned_ref[at, turn, j].astype(F32) * wide_of(1, i)
        both = dot(after.astype(BF16), solved[i])
        ab_ref[j, :, :size] = (eye * wide_of(2, i) - both[:, :size]).astype(BF16)
        ab_ref[j, :, size:] = both[:, size:].astype(BF16)


def local(units, fetched, gap, tables, *after):
    half, tokens, size = fetched[0].shape[2:]
    result = jax.ShapeDtypeStruct((half, tokens, 2 * size), BF16)
    arrays = tuple(fetched) + (gap,) + tuple(tables) + after
    outs = pl.pallas_call(
        functools.partial(local_kernel, units),
        out_shape=(result,) * (2 * len(units)),
        in_specs=[whole_vmem()] * len(arrays),
        out_specs=(whole_vmem(),) * (2 * len(units)),
        compiler_params=params(),
        cost_estimate=cost(),
        name="local_tokens",
    )(*arrays)
    return [(outs[2 * i], outs[2 * i + 1]) for i in range(len(units))]


def outlook_kernel(at, part, q_hbm, turned_ref, gap_ref, col_ref, row_ref, gain_ref, *refs):
    solved_refs = refs[:2]
    qo_refs = refs[-5:-3]
    refs[-3][...] = gain_ref[...]
    q_ref, sems = refs[-2:]
    half, tokens = solved_refs[0].shape[:2]
    size = solved_refs[0].shape[2] // 2
    span = half * size
    copies = []
    for turn in range(2):
        start = (2 * chunk_of(part) + jnp.bitwise_xor(turn, parity())) * span
        strip = pl.ds(pl.multiple_of(start, span), span)
        copies.append(pltpu.make_async_copy(q_hbm.at[:, strip], q_ref.at[turn], sems.at[turn]))
        copies[-1].start()
    gap = gap_ref[...]
    every = [(turn, j) for turn in range(2) for j in range(half)]

    def tall_of(table, turn, j):
        place = ((2 * at + turn) * 3 + table) * half + j
        return col_ref[:, place : place + 1]

    decay = {}
    for turn, j in every:
        decay[turn, j] = jnp.exp(tall_of(0, turn, j) - row_ref[at, turn, j : j + 1, :] + gap)
    for copy in copies:
        copy.wait()
    mix = {}
    for turn, j in every:
        gram = dot(q_ref[turn, :, j * size : (j + 1) * size], turned_ref[at, turn, j])
        mix[turn, j] = (decay[turn, j] * gram).astype(BF16)
    for turn, j in every:
        both = dot(mix[turn, j], solved_refs[turn][j])
        through = tall_of(2, turn, j) * q_ref[turn, :, j * size : (j + 1) * size].astype(F32)
        qo_refs[turn][j, :, :size] = (through - both[:, :size]).astype(BF16)
        qo_refs[turn][j, :, size:] = both[:, size:].astype(BF16)


def outlook(at, part, queries, turned, gap, tables, gain, solved, *after):
    half, tokens, wide = solved[0].shape
    arrays = (queries, turned, gap) + tuple(tables) + (gain,) + tuple(solved) + after
    return pl.pallas_call(
        functools.partial(outlook_kernel, at, part),
        out_shape=(jax.ShapeDtypeStruct(solved[0].shape, BF16),) * 2 + (jax.ShapeDtypeStruct(gain.shape, F32),),
        in_specs=[in_hbm()] + [whole_vmem()] * (len(arrays) - 1),
        out_specs=(whole_vmem(),) * 3,
        scratch_shapes=[pltpu.VMEM((2, tokens, half * wide // 2), BF16), pltpu.SemaphoreType.DMA((2,))],
        compiler_params=params(),
        cost_estimate=cost(),
        name="outlook",
    )(*arrays)


def joined(earlier, later):
    size = earlier.shape[0]
    product = dot(later[:, :size], earlier)
    return jnp.concatenate([product[:, :size], product[:, size:] + later[:, size:].astype(F32)], axis=1)


def pick(later, own, received):
    return jnp.where(later, received, own), jnp.where(later, own, received)


def compose_kernel(bit, with_token, carried, own_ref, got_ref, *rest):
    out_ref = rest[-1]
    if with_token:
        out_ref, token_ref = rest[-2:]
        token_ref[...] = jnp.zeros_like(token_ref)
        for row in range(carried):
            token_ref[row : row + 1, : rest[row].shape[1]] = rest[row][...]
    later = is_later(bit)
    for j in range(out_ref.shape[0]):
        earlier_block, later_block = pick(later, own_ref[j], got_ref[j])
        out_ref[j] = joined(earlier_block, later_block).astype(BF16)


def compose(bit, own, got, *after, with_token=False, carried=0):
    outs = (jax.ShapeDtypeStruct(own.shape, BF16),)
    if with_token:
        outs += (jax.ShapeDtypeStruct((8, 128), F32),)
    done = pl.pallas_call(
        functools.partial(compose_kernel, bit, with_token, carried),
        out_shape=outs,
        in_specs=[whole_vmem()] * (2 + len(after)),
        out_specs=(whole_vmem(),) * len(outs),
        compiler_params=params(),
        cost_estimate=cost(),
        name="compose",
    )(own, got, *after)
    return done if with_token else done[0]


def split_kernel(bit, halves, own_ref, got_ref, *rest):
    later = is_later(bit)
    quarter = own_ref.shape[0] // 2
    for number, out_ref in zip(halves, rest[-len(halves) :]):
        first = jnp.bitwise_xor(number, quarter_parity()) * quarter
        for j in range(quarter):
            earlier_block, later_block = pick(later, own_ref[first + j], got_ref[first + j])
            out_ref[j] = joined(earlier_block, later_block).astype(BF16)


def compose_split(bit, halves, own, got, *after):
    part = jax.ShapeDtypeStruct((own.shape[0] // 2,) + own.shape[1:], BF16)
    return pl.pallas_call(
        functools.partial(split_kernel, bit, halves),
        out_shape=(part,) * len(halves),
        in_specs=[whole_vmem()] * (2 + len(after)),
        out_specs=(whole_vmem(),) * len(halves),
        compiler_params=params(),
        cost_estimate=cost(),
        name="compose",
    )(own, got, *after)


def place_in_four():
    return jnp.bitwise_and(lax.axis_index("context"), 3)


def choose(index, values):
    chosen = values[0]
    for number in range(1, len(values)):
        chosen = jnp.where(index == number, values[number], chosen)
    return chosen


def four_kernel(last, *refs):
    blocks, (total_ref, before_ref) = refs[:4], refs[-2:]
    heads, size = blocks[0].shape[:2]
    every = range(heads)
    own = place_in_four()
    ordered = [
        [choose(jnp.bitwise_xor(own, place), [ref[j] for ref in blocks]) for j in every] for place in range(4)
    ]
    running = ordered[0]
    for place in range(1, 4):
        for j in every:
            before_ref[place - 1, j] = running[j]
        running = [joined(running[j], ordered[place][j]).astype(BF16) for j in every]
    for j in every:
        total_ref[j] = running[j][:, size:] if last else running[j]


def four(last, blocks, *after):
    heads, size = blocks[0].shape[:2]
    arrays = tuple(blocks) + after
    return pl.pallas_call(
        functools.partial(four_kernel, last),
        out_shape=(
            jax.ShapeDtypeStruct((heads, size, size if last else 2 * size), BF16),
            jax.ShapeDtypeStruct((3,) + blocks[0].shape, BF16),
        ),
        in_specs=[whole_vmem()] * len(arrays),
        out_specs=(whole_vmem(),) * 2,
        compiler_params=params(),
        cost_estimate=cost(),
        name="four",
    )(*arrays)


def spread_kernel(top, with_outer, carried_ref, before_ref, *rest):
    outs = rest[-4:]
    heads, size = carried_ref.shape[:2]
    every = range(heads)
    own = place_in_four()

    def through(block, state):
        return (dot(block[:, :size], state) + block[:, size:].astype(F32)).astype(BF16)

    later = is_later(top)
    if with_outer:
        outer = rest[0]
        state = [
            jnp.where(later, through(outer[j], carried_ref[j]), outer[j, :, size:]) for j in every
        ]
    else:
        state = [jnp.where(later, carried_ref[j], jnp.zeros_like(carried_ref[j])) for j in every]
    entering = [state] + [[through(before_ref[place, j], state[j]) for j in every] for place in range(3)]
    for distance in (3, 2, 1, 0):
        there = jnp.bitwise_xor(own, distance)
        for j in every:
            outs[distance][j] = choose(there, [entering[place][j] for place in range(4)])


def spread(top, carried, before, outer, *after):
    arrays = (carried, before) + (() if outer is None else (outer,)) + after
    return pl.pallas_call(
        functools.partial(spread_kernel, top, outer is not None),
        out_shape=(jax.ShapeDtypeStruct(carried.shape, BF16),) * 4,
        in_specs=[whole_vmem()] * len(arrays),
        out_specs=(whole_vmem(),) * 4,
        compiler_params=params(),
        cost_estimate=cost(),
        name="spread",
    )(*arrays)


def doubling_kernel(bit, first, last, *refs):
    later = is_later(bit)
    own_ref, got_ref = refs[:2]
    total_ref, before_ref = refs[-2:]
    heads, size = own_ref.shape[:2]
    row = lax.broadcasted_iota(jnp.int32, (size, 2 * size), 0)
    column = lax.broadcasted_iota(jnp.int32, (size, 2 * size), 1)
    neutral = jnp.where(row == column, 1.0, 0.0).astype(BF16)
    for j in range(heads):
        earlier_block, later_block = pick(later, own_ref[j], got_ref[j])
        total = joined(earlier_block, later_block).astype(BF16)
        total_ref[j] = total[:, size:] if last else total
        if first:
            before_ref[j] = jnp.where(later, got_ref[j], neutral)
        else:
            before = refs[2][j]
            before_ref[j] = jnp.where(later, joined(got_ref[j], before).astype(BF16), before)


def doubling(bit, last, own, got, before, *after):
    first = before is None
    arrays = (own, got) if first else (own, got, before)
    arrays += after
    heads, size = own.shape[:2]
    total = jax.ShapeDtypeStruct((heads, size, size if last else 2 * size), BF16)
    return pl.pallas_call(
        functools.partial(doubling_kernel, bit, first, last),
        out_shape=(total, jax.ShapeDtypeStruct(own.shape, BF16)),
        in_specs=[whole_vmem()] * len(arrays),
        out_specs=(whole_vmem(), whole_vmem()),
        compiler_params=params(),
        cost_estimate=cost(),
        name="doubling",
    )(*arrays)


def descend_kernel(bits, joint, threaded, with_token, *refs):
    count = len(bits)
    start = 2 if joint else 1
    blocks = refs[start : start + 2 * count]
    outs = refs[start + 2 * count + threaded :]
    sends, kept_ref = outs[:count], outs[count]
    if with_token:
        outs[-1][...] = jnp.zeros_like(outs[-1])
    size = kept_ref.shape[-1]
    every = range(kept_ref.shape[0])
    if joint:
        quarter = refs[0].shape[0]
        flip = quarter_parity() == 1
        state = []
        for j in every:
            same, other = refs[j // quarter], refs[1 - j // quarter]
            state.append(jnp.where(flip, other[j % quarter], same[j % quarter]))
    else:
        state = [refs[0][j] for j in every]
    for level, bit in enumerate(bits):
        later = is_later(bit)
        own_ref, got_ref = blocks[2 * level : 2 * level + 2]
        earlier = [jnp.where(later, got_ref[j], own_ref[j]) for j in every]
        after = [
            (dot(earlier[j][:, :size], state[j]) + earlier[j][:, size:].astype(F32)).astype(BF16) for j in every
        ]
        for j in every:
            sends[level][j] = jnp.where(later, state[j], after[j])
        state = [jnp.where(later, after[j], state[j]) for j in every]
    for j in every:
        kept_ref[j] = state[j]


def descend(bits, sources, blocks, thread, *after, with_token=False):
    heads, size = sum(array.shape[0] for array in sources), sources[0].shape[1]
    arrays = list(sources) + [array for pair in blocks for array in pair]
    specs = [whole_vmem()] * len(arrays)
    outs = len(bits) + 1
    shapes = [jax.ShapeDtypeStruct((heads, size, size), BF16)] * outs
    out_specs = [whole_vmem()] * outs
    aliases = {}
    if thread is not None:
        arrays.append(thread)
        specs.append(whole_vmem())
        shapes.append(jax.ShapeDtypeStruct(thread.shape, thread.dtype))
        out_specs.append(whole_vmem())
        aliases = {len(arrays) - 1: outs}
    if with_token:
        shapes.append(jax.ShapeDtypeStruct((8, 128), F32))
        out_specs.append(whole_vmem())
    arrays += after
    specs += [whole_vmem()] * len(after)
    return pl.pallas_call(
        functools.partial(descend_kernel, bits, len(sources) > 1, int(thread is not None) + len(after), with_token),
        out_shape=tuple(shapes),
        in_specs=specs,
        out_specs=tuple(out_specs),
        input_output_aliases=aliases,
        compiler_params=params(),
        cost_estimate=cost(),
        name="descend",
    )(*arrays)


def finish_kernel(unit, stored, is_last, gain_ref, state_ref, qo_ref, gate_ref, *rest):
    half, size = state_ref.shape[0], state_ref.shape[-1]
    span = half * size
    strip_ref = rest[-2] if is_last or stored else rest[-1]

    def start_of(part, turn):
        return (2 * chunk_of(part) + jnp.bitwise_xor(turn, parity())) * span

    stores = []
    if stored or is_last:
        out_hbm, sems = rest[-3], rest[-1]
    for number, earlier in enumerate(stored):
        there = pl.ds(pl.multiple_of(start_of(*earlier), span), span)
        stores.append(pltpu.make_async_copy(rest[number], out_hbm.at[:, there], sems.at[half + number]))
        stores[-1].start()
    cores = []
    for j in range(half):
        core = dot(qo_ref[j, :, :size], state_ref[j]) + qo_ref[j, :, size:].astype(F32)
        cores.append(core.astype(BF16).astype(F32))
    for j in range(half):
        core = cores[j]
        scaled = core * lax.rsqrt(jnp.mean(core * core, axis=-1, keepdims=True) + 1e-06) * gain_ref[...]
        there = pl.ds(pl.multiple_of(start_of(*unit) + j * size, size), size)
        gate = gate_ref[:, there].astype(F32)
        lanes = slice(j * size, (j + 1) * size)
        strip_ref[:, lanes] = (scaled * (0.5 * gate) * (1.0 + jnp.tanh(0.5 * gate))).astype(BF16)
        if is_last:
            stores.append(pltpu.make_async_copy(strip_ref.at[:, lanes], out_hbm.at[:, there], sems.at[j]))
            stores[-1].start()
    for store in stores:
        store.wait()


def finish(unit, is_last, state, qo, gate, gain, result, stored, *after):
    half, tokens, size = state.shape[0], gate.shape[0], state.shape[-1]
    arrays = [gain, state, qo, gate] + [strip for strip, _ in stored] + list(after)
    specs = [whole_vmem()] * len(arrays)
    aliases = {}
    if result is not None and (stored or is_last):
        aliases = {len(arrays): 0}
        arrays.append(result)
        specs.append(in_hbm())
    strip = jax.ShapeDtypeStruct((tokens, half * size), BF16)
    outs, out_specs, scratch = [], [], []
    if stored or is_last:
        outs.append(jax.ShapeDtypeStruct(gate.shape, BF16))
        out_specs.append(in_hbm())
        scratch.append(pltpu.SemaphoreType.DMA((half + len(stored),)))
    if is_last:
        scratch = [pltpu.VMEM(strip.shape, BF16)] + scratch
    else:
        outs.append(strip)
        out_specs.append(whole_vmem())
    done = pl.pallas_call(
        functools.partial(finish_kernel, unit, [earlier for _, earlier in stored], is_last),
        out_shape=tuple(outs),
        in_specs=specs,
        out_specs=tuple(out_specs),
        scratch_shapes=scratch,
        input_output_aliases=aliases,
        compiler_params=params(),
        cost_estimate=cost(),
        name="finish",
    )(*arrays)
    if is_last:
        return done[0], None
    return (done[0], done[1]) if stored else (result, done[0])


def body(
    head_count,
    context_count,
    queries,
    key_input,
    value_input,
    gate_input,
    decay_logit,
    beta_logit,
    decay_bias,
    norm_gain,
    doc_start,
):
    head_bits = head_count.bit_length() - 1
    context_bits = context_count.bit_length() - 1

    def swap(array, axis, distance):
        count = head_count if axis == "head" else context_count
        return lax.ppermute(array, axis, [(i, i ^ distance) for i in range(count)])

    head_bit = [("head", bit) for bit in range(head_bits)]
    context_bit = [("context", bit) for bit in range(context_bits)]
    own_bias = decay_bias[None, :]
    far_biases = [own_bias] + [swap(own_bias, "head", other) for other in range(1, head_count // 2)]
    half, size = decay_bias.shape[0] // 2, norm_gain.shape[0]
    inputs = (key_input, value_input)
    decay_rows, beta_rows = decay_logit.T, beta_logit.T

    ab, solved, qo = {}, {}, {}
    levels = [{} for _ in range(head_bits)]
    far_parts = list(reversed(range(head_count // 2, head_count)))
    near_parts = [part - head_count // 2 for part in far_parts]

    def work(parts, turn, fetched, gap, tables, *after):
        names = far_parts if parts[0] in far_parts else near_parts
        units = [(names.index(part), turn) for part in parts]
        for part, (block, out) in zip(parts, local(units, fetched, gap, tables, *after)):
            ab[part, turn], solved[part, turn] = block, out

    def fold(part, turn, bit, *after, **options):
        if bit == 0:
            return ab[part, turn]
        got = swap(fold(part | 1 << (bit - 1), turn, bit - 1), "head", 1 << (bit - 1))
        near = fold(part, turn, bit - 1)
        levels[bit - 1][part, turn] = (near, got)
        return compose(head_bit[bit - 1], near, got, *after, **options)

    under = head_bits - 1
    *fetched, gap, flags = fetch(far_parts, half, size, doc_start, *inputs)
    tables = gates(far_parts, decay_rows, beta_rows, flags, [(array, 0) for array in far_biases])
    work(far_parts, 1, fetched, gap, tables)
    far, got, near, chip = {}, {}, {}, {}
    far[1], token = fold(
        1 << under, 1, under, *far_biases, with_token=True, carried=len(far_biases)
    )
    near_bias = swap(token, "head", 1 << under)
    got[1] = swap(far[1], "head", 1 << under)
    work(far_parts, 0, fetched, gap, tables, swap(token, "head", 1))
    fetched_near = fetch(near_parts, half, size, None, *inputs, ab[far_parts[-1], 0])
    near_biases = [(near_bias, row) for row in range(len(near_parts))]
    near_tables = gates(near_parts, decay_rows, beta_rows, flags, near_biases, ab[far_parts[-1], 0])
    early = swap(flags, "head", 1)
    far[0] = fold(1 << under, 0, under, fetched_near[0])
    got[0] = swap(far[0], "head", 1 << under)
    work(near_parts, 1, fetched_near, gap, near_tables, far[0], early)
    near[1] = fold(0, 1, under)
    (to_three,) = compose_split(head_bit[under], (1,), near[1], got[1])
    from_three = swap(to_three, "context", 3)
    work(near_parts, 0, fetched_near, gap, near_tables, ab[near_parts[-1], 1], early)

    def look(part, *after):
        names, data, known = (
            (far_parts, fetched, tables) if part in far_parts else (near_parts, fetched_near, near_tables)
        )
        qo[part, 0], qo[part, 1], gain = outlook(
            names.index(part), part, queries, data[1], gap, known, norm_gain[None, :], (solved[part, 0], solved[part, 1]), *after
        )
        return gain

    every_part = far_parts + near_parts
    near[0] = fold(0, 0, under)
    to_one, mine = compose_split(head_bit[under], (1, 0), near[0], got[0])
    from_one = swap(to_one, "context", 1)
    (to_two,) = compose_split(head_bit[under], (0,), near[1], got[1], mine)
    from_two = swap(to_two, "context", 2)
    for turn in (1, 0):
        levels[under][0, turn] = (near[turn], got[turn])

    for part in every_part[:2]:
        look(part, mine)
    only_last = context_bits == 3
    outlooks = [qo[part, 0] for part in every_part[:2]]
    total, before = four(only_last, (mine, from_one, from_two, from_three), *outlooks)
    outer = None
    held = [array for level in levels[:under] for pair in level.values() for array in pair]
    for part in every_part[2:]:
        gain = look(part, total, *held)
    done_by = [qo[part, turn] for part in every_part for turn in (0, 1)] + held
    for bit in range(2, context_bits - 1):
        other = swap(total, "context", 1 << bit)
        total, outer = doubling(context_bit[bit], bit == context_bits - 2, total, other, outer)
    other = swap(total, "context", 1 << (context_bits - 1))

    states = {}
    entering = spread(context_bit[-1], other, before, outer, gate_input, *done_by)
    from_far = {distance: swap(entering[distance], "context", distance) for distance in (3, 2, 1)}
    total_units = 2 * head_count
    strips, waiting, results = [], [], [None]

    def write(part, turn):
        number = len(strips) + 1
        stored = []
        if number in (total_units // 2, total_units - 1, total_units):
            stored, waiting[:] = waiting[:], []
        chained = [strips[-1][0]] if strips and not stored else []
        result, strip = finish(
            (part, turn),
            number == total_units,
            states[part, turn],
            qo[part, turn],
            gate_input,
            gain,
            results[-1],
            [(strips[entry][0], strips[entry][1]) for entry in stored],
            *chained,
        )
        results.append(result)
        waiting.append(len(strips))
        strips.append((strip, (part, turn)))

    leaves = []
    inner = [
        (0, 0, head_bits, (entering[0], from_far[1])),
        (0, 1, head_bits, (from_far[2], from_far[3])),
    ]

    def pass_on(part, turn, below, sources):
        down = list(reversed(range(below)))
        outs = descend(
            [head_bit[bit] for bit in down],
            sources,
            [levels[bit][part, turn] for bit in down],
            strips[-1][0] if strips else None,
        )
        states[part, turn] = outs[below]
        if strips:
            strips[-1] = (outs[below + 1], strips[-1][1])
        for level, bit in enumerate(down):
            entry = (part | 1 << bit, turn, bit, (swap(outs[level], "head", 1 << bit),))
            (inner if bit else leaves).append(entry)

    def write_leaves(entries):
        for part, turn, _, (state,) in entries:
            states[part, turn] = state
            write(part, turn)

    depth = head_bits
    while inner:
        inner.sort(key=lambda entry: (-entry[2], entry[1]))
        part, turn, below, sources = inner.pop(0)
        if below < depth or turn and below == head_bits:
            write_leaves(leaves)
            leaves.clear()
            depth = below
        known = len(leaves)
        pass_on(part, turn, below, sources)
        if not inner:
            write_leaves(leaves[:known])
            del leaves[:known]
        write(part, turn)
    write_leaves(leaves)
    return results[-1]


def solution(mesh):
    return jax.shard_map(
        functools.partial(body, mesh.shape["head"], mesh.shape["context"]),
        mesh=mesh,
        in_specs=(
            P(("context", "head"), None),
            P(("context", "head"), None),
            P(("context", "head"), None),
            P(("context", "head"), None),
            P(("context", "head"), None),
            P(("context", "head"), None),
            P("head"),
            P(),
            P("context"),
        ),
        out_specs=P(("context", "head"), None),
        check_vma=False,
    )
```

```python
import functools

import jax
import jax.numpy as jnp
from jax import lax
from jax.experimental import pallas as pl
from jax.experimental.pallas import tpu as pltpu
from jax.sharding import PartitionSpec as P

C = 64
F32 = jnp.float32
BF16 = jnp.bfloat16
EXACT = lax.Precision.HIGHEST
VMEM_BYTES = 28 * 1024 * 1024
FETCH_BYTES = 52 * 1024 * 1024
REFETCH_BYTES = 47 * 1024 * 1024
MASKED = -1e30
BASE = 16


def params(limit=VMEM_BYTES):
    return pltpu.CompilerParams(vmem_limit_bytes=limit)


def cost(long=True):
    return pl.CostEstimate(flops=10**10 if long else 10**7, bytes_accessed=10**8 if long else 10**5, transcendentals=0)


def is_later(bit):
    axis, number = bit
    return jnp.bitwise_and(lax.shift_right_logical(lax.axis_index(axis), number), 1) == 1


def chunk_of(part):
    return jnp.bitwise_xor(lax.axis_index("head"), lax.axis_size("head") - 1 - part)


def parity():
    return jnp.bitwise_and(lax.shift_right_logical(lax.axis_index("context"), 1), 1)


def quarter_parity():
    return jnp.bitwise_and(lax.axis_index("context"), 1)


def dot(a, b):
    return jnp.dot(a, b, preferred_element_type=F32)


def dot_t(a, b):
    return lax.dot_general(a, b, (((1,), (1,)), ((), ())), preferred_element_type=F32)


def whole_vmem():
    return pl.BlockSpec(memory_space=pltpu.VMEM)


def whole_smem():
    return pl.BlockSpec(memory_space=pltpu.SMEM)


def in_hbm():
    return pl.BlockSpec(memory_space=pltpu.HBM)


def masks(tokens):
    row = lax.broadcasted_iota(jnp.int32, (tokens, tokens), 0)
    column = lax.broadcasted_iota(jnp.int32, (tokens, tokens), 1)
    return row, column


def gates_kernel(parts, bias_rows, width, decay_ref, beta_ref, flag_ref, *rest):
    bias_refs, (col_ref, row_ref) = rest[: len(parts)], rest[-2:]
    tokens = decay_ref.shape[1]
    half = width // 2
    row, column = masks(tokens)
    decay, beta = [], []
    for place, part in enumerate(parts):
        rows = pl.ds(pl.multiple_of(chunk_of(part) * width, width), width)
        diagonal = row[:width, :width] == column[:width, :width]
        bias = bias_refs[place][bias_rows[place] : bias_rows[place] + 1, :width]
        bias = jnp.sum(jnp.where(diagonal, bias, 0.0), axis=1, keepdims=True)
        decay.append(decay_ref[rows, :] + bias)
        beta.append(beta_ref[rows, :])
    z = jnp.concatenate(decay, axis=0)
    logit = jnp.concatenate(beta, axis=0)
    beta = 1.0 / (1.0 + jnp.exp(-logit))
    log_beta = jnp.minimum(logit, 0.0) - jnp.log1p(jnp.exp(-jnp.abs(logit)))
    log_decay = -(jnp.maximum(z, 0.0) + jnp.log1p(jnp.exp(-jnp.abs(z))))
    upper = jnp.where(row <= column, 1.0, 0.0)
    cum = jnp.dot(log_decay, upper, precision=EXACT, preferred_element_type=F32)
    last = jnp.broadcast_to(cum[:, tokens - 1 :], cum.shape)
    gamma = jnp.exp(cum) * flag_ref[0, :1]
    back = jnp.exp(last - cum) * flag_ref[1, :1]
    whole = jnp.exp(last) * flag_ref[2, :1]
    swapped = parity() == 1
    tall = []
    for part in range(len(parts)):
        sides = [slice(part * width + side * half, part * width + (side + 1) * half) for side in range(2)]
        for turn in range(2):
            same, other = sides[turn], sides[1 - turn]
            for table in (cum, cum + log_beta, gamma):
                tall.append(jnp.where(swapped, table[other], table[same]))
            for place, table in enumerate((cum, back, whole, beta, beta * gamma)):
                row_ref[part, turn, place * half : (place + 1) * half, :] = jnp.where(
                    swapped, table[other], table[same]
                )
    col_ref[...] = jnp.transpose(jnp.concatenate(tall, axis=0))


def gates(parts, decay_rows, beta_rows, flags, biases, *after):
    heads, tokens = decay_rows.shape
    bias_rows = [row for _, row in biases]
    width = heads // lax.axis_size("head")
    half = width // 2
    count = len(parts)
    arrays = (decay_rows, beta_rows, flags) + tuple(array for array, _ in biases) + after
    return pl.pallas_call(
        functools.partial(gates_kernel, parts, bias_rows, width),
        out_shape=(
            jax.ShapeDtypeStruct((tokens, 3 * count * width), F32),
            jax.ShapeDtypeStruct((count, 2, 5 * half, tokens), F32),
        ),
        in_specs=[whole_vmem()] * len(arrays),
        out_specs=(whole_vmem(),) * 2,
        compiler_params=params(),
        cost_estimate=cost(False),
        name="gates",
    )(*arrays)


def fetch_kernel(parts, half, with_resets, *refs):
    if with_resets:
        doc_ref, refs = refs[0], refs[1:]
    k_hbm, v_hbm = refs[:2]
    k_ref, sems = refs[-2:]
    normed_ref, turned_ref, v_ref = refs[-7:-4] if with_resets else refs[-5:-2]
    span = v_ref.shape[-1]
    size = span // half
    copies = {}
    for number, (source, target) in enumerate(((k_hbm, k_ref), (v_hbm, v_ref))):
        for turn in (1, 0):
            for place, part in enumerate(parts):
                at = 2 * chunk_of(part) + jnp.bitwise_xor(turn, parity())
                strip = pl.ds(pl.multiple_of(at * span, span), span)
                copy = pltpu.make_async_copy(
                    source.at[:, strip], target.at[place, turn], sems.at[number, place, turn]
                )
                copy.start()
                copies[number, place, turn] = copy
    if with_resets:
        gap_ref, flag_ref = refs[-4:-2]
        tokens = gap_ref.shape[0]
        row, column = masks(tokens)
        groups = tokens // C
        row_resets = jnp.zeros_like(row)
        column_resets = jnp.zeros_like(row)
        for group in range(groups):
            flag = doc_ref[lax.axis_index("head") * groups + group]
            row_resets = row_resets + jnp.where(row >= group * C, flag, 0)
            column_resets = column_resets + jnp.where(column >= group * C, flag, 0)
        gap_ref[...] = jnp.where(jnp.logical_and(row >= column, row_resets == column_resets), 0.0, MASKED)
        resets = column_resets[:8]
        final = row_resets[tokens - 8 :]
        flag_ref[0] = jnp.where(resets == 0, 1.0, 0.0)
        flag_ref[1] = jnp.where(resets == final, 1.0, 0.0)
        flag_ref[2] = jnp.where(final == 0, 1.0, 0.0)
    for turn in (1, 0):
        for place in range(len(parts)):
            copies[0, place, turn].wait()
            for j in range(half):
                keys = k_ref[place, turn, :, j * size : (j + 1) * size].astype(F32)
                keys = (keys * lax.rsqrt(jnp.sum(keys * keys, axis=-1, keepdims=True) + 1e-06)).astype(BF16)
                normed_ref[place, turn, j] = keys
                turned_ref[place, turn, j] = jnp.transpose(keys)
    for turn in (1, 0):
        for place in range(len(parts)):
            copies[1, place, turn].wait()


def fetch(parts, half, size, doc_start, keys, values, *after):
    tokens = keys.shape[0]
    count = len(parts)
    strips = jax.ShapeDtypeStruct((count, 2, tokens, half * size), BF16)
    outs = [
        jax.ShapeDtypeStruct((count, 2, half, tokens, size), BF16),
        jax.ShapeDtypeStruct((count, 2, half, size, tokens), BF16),
        strips,
    ]
    specs = [in_hbm()] * 2 + [whole_vmem()] * len(after)
    arrays = [keys, values, *after]
    if doc_start is not None:
        outs += [jax.ShapeDtypeStruct((tokens, tokens), F32), jax.ShapeDtypeStruct((3, 8, tokens), F32)]
        specs = [whole_smem()] + specs
        arrays = [doc_start] + arrays
    return pl.pallas_call(
        functools.partial(fetch_kernel, parts, half, doc_start is not None),
        out_shape=tuple(outs),
        in_specs=specs,
        out_specs=(whole_vmem(),) * len(outs),
        scratch_shapes=[pltpu.VMEM(strips.shape, BF16), pltpu.SemaphoreType.DMA((2, count, 2))],
        compiler_params=params(REFETCH_BYTES if after else FETCH_BYTES),
        cost_estimate=cost(),
        name="fetch",
    )(*arrays)


def local_kernel(units, *refs):
    normed_ref, turned_ref, v_ref, gap_ref, col_ref, row_ref = refs[:6]
    outs = refs[-2 * len(units) :]
    tokens = gap_ref.shape[0]
    half, size = outs[0].shape[:2]
    row, column = masks(tokens)
    apart = jnp.bitwise_xor(row, column)
    eye = jnp.where(row == column, 1.0, 0.0)
    lane_block = lax.shift_right_logical(column[:BASE], BASE.bit_length() - 1)
    inside = jnp.bitwise_and(column[:BASE], BASE - 1)
    small_eye = jnp.where(row[:BASE] == inside, 1.0, 0.0)
    first_lane = column[:BASE] - inside
    gap = jnp.where(row > column, gap_ref[...], MASKED)
    every = range(len(units) * half)

    def unit_of(i):
        return units[i // half] + (i % half,)

    def tall_of(table, i):
        at, turn, j = unit_of(i)
        at = ((2 * at + turn) * 3 + table) * half + j
        return col_ref[:, at : at + 1]

    def wide_of(table, i):
        at, turn, j = unit_of(i)
        return row_ref[at, turn, table * half + j : table * half + j + 1, :]

    lower, packed = [], []
    for i in every:
        at, turn, j = unit_of(i)
        decay = jnp.exp(tall_of(1, i) - wide_of(0, i) + gap)
        low = decay * dot(normed_ref[at, turn, j], turned_ref[at, turn, j])
        blocks = jnp.zeros((BASE, tokens), F32)
        for top in range(0, tokens, BASE):
            blocks = jnp.where(lane_block == top // BASE, low[top : top + BASE], blocks)
        packed.append(blocks)
        lower.append(low.astype(BF16))
    rows = [[small_eye[top : top + 8] for top in range(0, BASE, 8)] for _ in every]
    for k in range(BASE - 1):
        for i in every:
            pivot = rows[i][k // 8][k % 8 : k % 8 + 1]
            for group in range((k + 1) // 8, BASE // 8):
                block_rows = slice(group * 8, group * 8 + 8)
                factor = jnp.take_along_axis(
                    packed[i][block_rows], first_lane[block_rows] + k, axis=1, mode="promise_in_bounds"
                )
                rows[i][group] = rows[i][group] - factor * pivot
    inverse = []
    for i in every:
        joint = jnp.concatenate(rows[i], axis=0)
        inverse.append(
            jnp.concatenate(
                [jnp.where(lane_block == at_block, joint, 0.0) for at_block in range(tokens // BASE)], axis=0
            )
        )
    nothing = jnp.zeros((tokens, tokens), BF16)
    block = BASE
    while block < tokens:
        small = [inverse[j].astype(BF16) for j in every]
        step = jnp.logical_and(apart >= block, apart < 2 * block)
        masked = [jnp.where(step, lower[j], nothing) for j in every]
        spans = [slice(top, top + block) for top in range(block, tokens, 2 * block)]

        def odd(array):
            return jnp.concatenate([array[s] for s in spans], axis=0)

        def spread(array, evens):
            pieces = []
            for i, s in enumerate(spans):
                pieces.append(evens[s.start - block : s.start])
                pieces.append(array[i * block : (i + 1) * block])
            return jnp.concatenate(pieces, axis=0)

        inner = [spread(dot(odd(masked[j]), small[j]).astype(BF16), nothing) for j in every]
        inverse = [
            spread(odd(inverse[j]) - dot(odd(small[j]), inner[j]), inverse[j]) for j in every
        ]
        block *= 2
    solved = []
    for i in every:
        at, turn, j = unit_of(i)
        lanes = slice(j * size, (j + 1) * size)
        keys = dot((inverse[i] * wide_of(4, i)).astype(BF16), normed_ref[at, turn, j])
        values = dot((inverse[i] * wide_of(3, i)).astype(BF16), v_ref[at, turn, :, lanes])
        solved.append(jnp.concatenate([keys.astype(BF16), values.astype(BF16)], axis=1))
    for i in every:
        at, turn, j = unit_of(i)
        ab_ref, solved_ref = outs[2 * (i // half) : 2 * (i // half) + 2]
        solved_ref[j] = solved[i]
        after = turned_ref[at, turn, j].astype(F32) * wide_of(1, i)
        both = dot(after.astype(BF16), solved[i])
        ab_ref[j, :, :size] = (eye * wide_of(2, i) - both[:, :size]).astype(BF16)
        ab_ref[j, :, size:] = both[:, size:].astype(BF16)


def local(units, fetched, gap, tables, *after):
    half, tokens, size = fetched[0].shape[2:]
    result = jax.ShapeDtypeStruct((half, tokens, 2 * size), BF16)
    arrays = tuple(fetched) + (gap,) + tuple(tables) + after
    outs = pl.pallas_call(
        functools.partial(local_kernel, units),
        out_shape=(result,) * (2 * len(units)),
        in_specs=[whole_vmem()] * len(arrays),
        out_specs=(whole_vmem(),) * (2 * len(units)),
        compiler_params=params(),
        cost_estimate=cost(),
        name="local_tokens",
    )(*arrays)
    return [(outs[2 * i], outs[2 * i + 1]) for i in range(len(units))]


def outlook_kernel(at, part, q_hbm, turned_ref, gap_ref, col_ref, row_ref, gain_ref, *refs):
    solved_refs = refs[:2]
    qo_refs = refs[-5:-3]
    refs[-3][...] = gain_ref[...]
    q_ref, sems = refs[-2:]
    half, tokens = solved_refs[0].shape[:2]
    size = solved_refs[0].shape[2] // 2
    span = half * size
    copies = []
    for turn in range(2):
        start = (2 * chunk_of(part) + jnp.bitwise_xor(turn, parity())) * span
        strip = pl.ds(pl.multiple_of(start, span), span)
        copies.append(pltpu.make_async_copy(q_hbm.at[:, strip], q_ref.at[turn], sems.at[turn]))
        copies[-1].start()
    gap = gap_ref[...]
    every = [(turn, j) for turn in range(2) for j in range(half)]

    def tall_of(table, turn, j):
        place = ((2 * at + turn) * 3 + table) * half + j
        return col_ref[:, place : place + 1]

    decay = {}
    for turn, j in every:
        decay[turn, j] = jnp.exp(tall_of(0, turn, j) - row_ref[at, turn, j : j + 1, :] + gap)
    for copy in copies:
        copy.wait()
    mix = {}
    for turn, j in every:
        gram = dot(q_ref[turn, :, j * size : (j + 1) * size], turned_ref[at, turn, j])
        mix[turn, j] = (decay[turn, j] * gram).astype(BF16)
    for turn, j in every:
        both = dot(mix[turn, j], solved_refs[turn][j])
        through = tall_of(2, turn, j) * q_ref[turn, :, j * size : (j + 1) * size].astype(F32)
        qo_refs[turn][j, :, :size] = (through - both[:, :size]).astype(BF16)
        qo_refs[turn][j, :, size:] = both[:, size:].astype(BF16)


def outlook(at, part, queries, turned, gap, tables, gain, solved, *after):
    half, tokens, wide = solved[0].shape
    arrays = (queries, turned, gap) + tuple(tables) + (gain,) + tuple(solved) + after
    return pl.pallas_call(
        functools.partial(outlook_kernel, at, part),
        out_shape=(jax.ShapeDtypeStruct(solved[0].shape, BF16),) * 2 + (jax.ShapeDtypeStruct(gain.shape, F32),),
        in_specs=[in_hbm()] + [whole_vmem()] * (len(arrays) - 1),
        out_specs=(whole_vmem(),) * 3,
        scratch_shapes=[pltpu.VMEM((2, tokens, half * wide // 2), BF16), pltpu.SemaphoreType.DMA((2,))],
        compiler_params=params(),
        cost_estimate=cost(),
        name="outlook",
    )(*arrays)


def joined(earlier, later):
    size = earlier.shape[0]
    product = dot(later[:, :size], earlier)
    return jnp.concatenate([product[:, :size], product[:, size:] + later[:, size:].astype(F32)], axis=1)


def pick(later, own, received):
    return jnp.where(later, received, own), jnp.where(later, own, received)


def compose_kernel(bit, with_token, carried, own_ref, got_ref, *rest):
    out_ref = rest[-1]
    if with_token:
        out_ref, token_ref = rest[-2:]
        token_ref[...] = jnp.zeros_like(token_ref)
        for row in range(carried):
            token_ref[row : row + 1, : rest[row].shape[1]] = rest[row][...]
    later = is_later(bit)
    for j in range(out_ref.shape[0]):
        earlier_block, later_block = pick(later, own_ref[j], got_ref[j])
        out_ref[j] = joined(earlier_block, later_block).astype(BF16)


def compose(bit, own, got, *after, with_token=False, carried=0):
    outs = (jax.ShapeDtypeStruct(own.shape, BF16),)
    if with_token:
        outs += (jax.ShapeDtypeStruct((8, 128), F32),)
    done = pl.pallas_call(
        functools.partial(compose_kernel, bit, with_token, carried),
        out_shape=outs,
        in_specs=[whole_vmem()] * (2 + len(after)),
        out_specs=(whole_vmem(),) * len(outs),
        compiler_params=params(),
        cost_estimate=cost(),
        name="compose",
    )(own, got, *after)
    return done if with_token else done[0]


def split_kernel(bit, halves, own_ref, got_ref, *rest):
    later = is_later(bit)
    quarter = own_ref.shape[0] // 2
    for number, out_ref in zip(halves, rest[-len(halves) :]):
        first = jnp.bitwise_xor(number, quarter_parity()) * quarter
        for j in range(quarter):
            earlier_block, later_block = pick(later, own_ref[first + j], got_ref[first + j])
            out_ref[j] = joined(earlier_block, later_block).astype(BF16)


def compose_split(bit, halves, own, got, *after):
    part = jax.ShapeDtypeStruct((own.shape[0] // 2,) + own.shape[1:], BF16)
    return pl.pallas_call(
        functools.partial(split_kernel, bit, halves),
        out_shape=(part,) * len(halves),
        in_specs=[whole_vmem()] * (2 + len(after)),
        out_specs=(whole_vmem(),) * len(halves),
        compiler_params=params(),
        cost_estimate=cost(),
        name="compose",
    )(own, got, *after)


def place_in_four():
    return jnp.bitwise_and(lax.axis_index("context"), 3)


def choose(index, values):
    chosen = values[0]
    for number in range(1, len(values)):
        chosen = jnp.where(index == number, values[number], chosen)
    return chosen


def four_kernel(last, *refs):
    blocks, (total_ref, before_ref) = refs[:4], refs[-2:]
    heads, size = blocks[0].shape[:2]
    every = range(heads)
    own = place_in_four()
    ordered = [
        [choose(jnp.bitwise_xor(own, place), [ref[j] for ref in blocks]) for j in every] for place in range(4)
    ]
    running = ordered[0]
    for place in range(1, 4):
        for j in every:
            before_ref[place - 1, j] = running[j]
        running = [joined(running[j], ordered[place][j]).astype(BF16) for j in every]
    for j in every:
        total_ref[j] = running[j][:, size:] if last else running[j]


def four(last, blocks, *after):
    heads, size = blocks[0].shape[:2]
    arrays = tuple(blocks) + after
    return pl.pallas_call(
        functools.partial(four_kernel, last),
        out_shape=(
            jax.ShapeDtypeStruct((heads, size, size if last else 2 * size), BF16),
            jax.ShapeDtypeStruct((3,) + blocks[0].shape, BF16),
        ),
        in_specs=[whole_vmem()] * len(arrays),
        out_specs=(whole_vmem(),) * 2,
        compiler_params=params(),
        cost_estimate=cost(),
        name="four",
    )(*arrays)


def spread_kernel(top, with_outer, carried_ref, before_ref, *rest):
    outs = rest[-4:]
    heads, size = carried_ref.shape[:2]
    every = range(heads)
    own = place_in_four()

    def through(block, state):
        return (dot(block[:, :size], state) + block[:, size:].astype(F32)).astype(BF16)

    later = is_later(top)
    if with_outer:
        outer = rest[0]
        state = [
            jnp.where(later, through(outer[j], carried_ref[j]), outer[j, :, size:]) for j in every
        ]
    else:
        state = [jnp.where(later, carried_ref[j], jnp.zeros_like(carried_ref[j])) for j in every]
    entering = [state] + [[through(before_ref[place, j], state[j]) for j in every] for place in range(3)]
    for distance in (3, 2, 1, 0):
        there = jnp.bitwise_xor(own, distance)
        for j in every:
            outs[distance][j] = choose(there, [entering[place][j] for place in range(4)])


def spread(top, carried, before, outer, *after):
    arrays = (carried, before) + (() if outer is None else (outer,)) + after
    return pl.pallas_call(
        functools.partial(spread_kernel, top, outer is not None),
        out_shape=(jax.ShapeDtypeStruct(carried.shape, BF16),) * 4,
        in_specs=[whole_vmem()] * len(arrays),
        out_specs=(whole_vmem(),) * 4,
        compiler_params=params(),
        cost_estimate=cost(),
        name="spread",
    )(*arrays)


def doubling_kernel(bit, first, last, *refs):
    later = is_later(bit)
    own_ref, got_ref = refs[:2]
    total_ref, before_ref = refs[-2:]
    heads, size = own_ref.shape[:2]
    row = lax.broadcasted_iota(jnp.int32, (size, 2 * size), 0)
    column = lax.broadcasted_iota(jnp.int32, (size, 2 * size), 1)
    neutral = jnp.where(row == column, 1.0, 0.0).astype(BF16)
    for j in range(heads):
        earlier_block, later_block = pick(later, own_ref[j], got_ref[j])
        total = joined(earlier_block, later_block).astype(BF16)
        total_ref[j] = total[:, size:] if last else total
        if first:
            before_ref[j] = jnp.where(later, got_ref[j], neutral)
        else:
            before = refs[2][j]
            before_ref[j] = jnp.where(later, joined(got_ref[j], before).astype(BF16), before)


def doubling(bit, last, own, got, before, *after):
    first = before is None
    arrays = (own, got) if first else (own, got, before)
    arrays += after
    heads, size = own.shape[:2]
    total = jax.ShapeDtypeStruct((heads, size, size if last else 2 * size), BF16)
    return pl.pallas_call(
        functools.partial(doubling_kernel, bit, first, last),
        out_shape=(total, jax.ShapeDtypeStruct(own.shape, BF16)),
        in_specs=[whole_vmem()] * len(arrays),
        out_specs=(whole_vmem(), whole_vmem()),
        compiler_params=params(),
        cost_estimate=cost(),
        name="doubling",
    )(*arrays)


def descend_kernel(bits, joint, threaded, with_token, *refs):
    count = len(bits)
    start = 2 if joint else 1
    blocks = refs[start : start + 2 * count]
    outs = refs[start + 2 * count + threaded :]
    sends, kept_ref = outs[:count], outs[count]
    if with_token:
        outs[-1][...] = jnp.zeros_like(outs[-1])
    size = kept_ref.shape[-1]
    every = range(kept_ref.shape[0])
    if joint:
        quarter = refs[0].shape[0]
        flip = quarter_parity() == 1
        state = []
        for j in every:
            same, other = refs[j // quarter], refs[1 - j // quarter]
            state.append(jnp.where(flip, other[j % quarter], same[j % quarter]))
    else:
        state = [refs[0][j] for j in every]
    for level, bit in enumerate(bits):
        later = is_later(bit)
        own_ref, got_ref = blocks[2 * level : 2 * level + 2]
        earlier = [jnp.where(later, got_ref[j], own_ref[j]) for j in every]
        after = [
            (dot(earlier[j][:, :size], state[j]) + earlier[j][:, size:].astype(F32)).astype(BF16) for j in every
        ]
        for j in every:
            sends[level][j] = jnp.where(later, state[j], after[j])
        state = [jnp.where(later, after[j], state[j]) for j in every]
    for j in every:
        kept_ref[j] = state[j]


def descend(bits, sources, blocks, thread, *after, with_token=False):
    heads, size = sum(array.shape[0] for array in sources), sources[0].shape[1]
    arrays = list(sources) + [array for pair in blocks for array in pair]
    specs = [whole_vmem()] * len(arrays)
    outs = len(bits) + 1
    shapes = [jax.ShapeDtypeStruct((heads, size, size), BF16)] * outs
    out_specs = [whole_vmem()] * outs
    aliases = {}
    if thread is not None:
        arrays.append(thread)
        specs.append(whole_vmem())
        shapes.append(jax.ShapeDtypeStruct(thread.shape, thread.dtype))
        out_specs.append(whole_vmem())
        aliases = {len(arrays) - 1: outs}
    if with_token:
        shapes.append(jax.ShapeDtypeStruct((8, 128), F32))
        out_specs.append(whole_vmem())
    arrays += after
    specs += [whole_vmem()] * len(after)
    return pl.pallas_call(
        functools.partial(descend_kernel, bits, len(sources) > 1, int(thread is not None) + len(after), with_token),
        out_shape=tuple(shapes),
        in_specs=specs,
        out_specs=tuple(out_specs),
        input_output_aliases=aliases,
        compiler_params=params(),
        cost_estimate=cost(),
        name="descend",
    )(*arrays)


def finish_kernel(unit, stored, is_last, gain_ref, state_ref, qo_ref, gate_ref, *rest):
    half, size = state_ref.shape[0], state_ref.shape[-1]
    span = half * size
    strip_ref = rest[-2] if is_last or stored else rest[-1]

    def start_of(part, turn):
        return (2 * chunk_of(part) + jnp.bitwise_xor(turn, parity())) * span

    stores = []
    if stored or is_last:
        out_hbm, sems = rest[-3], rest[-1]
    for number, earlier in enumerate(stored):
        there = pl.ds(pl.multiple_of(start_of(*earlier), span), span)
        stores.append(pltpu.make_async_copy(rest[number], out_hbm.at[:, there], sems.at[half + number]))
        stores[-1].start()
    cores = []
    for j in range(half):
        core = dot(qo_ref[j, :, :size], state_ref[j]) + qo_ref[j, :, size:].astype(F32)
        cores.append(core.astype(BF16).astype(F32))
    for j in range(half):
        core = cores[j]
        scaled = core * lax.rsqrt(jnp.mean(core * core, axis=-1, keepdims=True) + 1e-06) * gain_ref[...]
        there = pl.ds(pl.multiple_of(start_of(*unit) + j * size, size), size)
        gate = gate_ref[:, there].astype(F32)
        lanes = slice(j * size, (j + 1) * size)
        strip_ref[:, lanes] = (scaled * (0.5 * gate) * (1.0 + jnp.tanh(0.5 * gate))).astype(BF16)
        if is_last:
            stores.append(pltpu.make_async_copy(strip_ref.at[:, lanes], out_hbm.at[:, there], sems.at[j]))
            stores[-1].start()
    for store in stores:
        store.wait()


def finish(unit, is_last, state, qo, gate, gain, result, stored, *after):
    half, tokens, size = state.shape[0], gate.shape[0], state.shape[-1]
    arrays = [gain, state, qo, gate] + [strip for strip, _ in stored] + list(after)
    specs = [whole_vmem()] * len(arrays)
    aliases = {}
    if result is not None and (stored or is_last):
        aliases = {len(arrays): 0}
        arrays.append(result)
        specs.append(in_hbm())
    strip = jax.ShapeDtypeStruct((tokens, half * size), BF16)
    outs, out_specs, scratch = [], [], []
    if stored or is_last:
        outs.append(jax.ShapeDtypeStruct(gate.shape, BF16))
        out_specs.append(in_hbm())
        scratch.append(pltpu.SemaphoreType.DMA((half + len(stored),)))
    if is_last:
        scratch = [pltpu.VMEM(strip.shape, BF16)] + scratch
    else:
        outs.append(strip)
        out_specs.append(whole_vmem())
    done = pl.pallas_call(
        functools.partial(finish_kernel, unit, [earlier for _, earlier in stored], is_last),
        out_shape=tuple(outs),
        in_specs=specs,
        out_specs=tuple(out_specs),
        scratch_shapes=scratch,
        input_output_aliases=aliases,
        compiler_params=params(),
        cost_estimate=cost(),
        name="finish",
    )(*arrays)
    if is_last:
        return done[0], None
    return (done[0], done[1]) if stored else (result, done[0])


def body(
    head_count,
    context_count,
    queries,
    key_input,
    value_input,
    gate_input,
    decay_logit,
    beta_logit,
    decay_bias,
    norm_gain,
    doc_start,
):
    head_bits = head_count.bit_length() - 1
    context_bits = context_count.bit_length() - 1

    def swap(array, axis, distance):
        count = head_count if axis == "head" else context_count
        return lax.ppermute(array, axis, [(i, i ^ distance) for i in range(count)])

    head_bit = [("head", bit) for bit in range(head_bits)]
    context_bit = [("context", bit) for bit in range(context_bits)]
    own_bias = decay_bias[None, :]
    far_biases = [own_bias] + [swap(own_bias, "head", other) for other in range(1, head_count // 2)]
    half, size = decay_bias.shape[0] // 2, norm_gain.shape[0]
    inputs = (key_input, value_input)
    decay_rows, beta_rows = decay_logit.T, beta_logit.T

    ab, solved, qo = {}, {}, {}
    levels = [{} for _ in range(head_bits)]
    far_parts = list(reversed(range(head_count // 2, head_count)))
    near_parts = [part - head_count // 2 for part in far_parts]

    def work(parts, turn, fetched, gap, tables, *after):
        names = far_parts if parts[0] in far_parts else near_parts
        units = [(names.index(part), turn) for part in parts]
        for part, (block, out) in zip(parts, local(units, fetched, gap, tables, *after)):
            ab[part, turn], solved[part, turn] = block, out

    def fold(part, turn, bit, *after, **options):
        if bit == 0:
            return ab[part, turn]
        got = swap(fold(part | 1 << (bit - 1), turn, bit - 1), "head", 1 << (bit - 1))
        near = fold(part, turn, bit - 1)
        levels[bit - 1][part, turn] = (near, got)
        return compose(head_bit[bit - 1], near, got, *after, **options)

    under = head_bits - 1
    *fetched, gap, flags = fetch(far_parts, half, size, doc_start, *inputs)
    tables = gates(far_parts, decay_rows, beta_rows, flags, [(array, 0) for array in far_biases])
    work(far_parts, 1, fetched, gap, tables)
    far, got, near, chip = {}, {}, {}, {}
    far[1], token = fold(
        1 << under, 1, under, *far_biases, with_token=True, carried=len(far_biases)
    )
    near_bias = swap(token, "head", 1 << under)
    got[1] = swap(far[1], "head", 1 << under)
    work(far_parts, 0, fetched, gap, tables, swap(token, "head", 1))
    fetched_near = fetch(near_parts, half, size, None, *inputs, ab[far_parts[-1], 0])
    near_biases = [(near_bias, row) for row in range(len(near_parts))]
    near_tables = gates(near_parts, decay_rows, beta_rows, flags, near_biases, ab[far_parts[-1], 0])
    early = swap(flags, "head", 1)
    far[0] = fold(1 << under, 0, under, fetched_near[0])
    got[0] = swap(far[0], "head", 1 << under)
    work(near_parts, 1, fetched_near, gap, near_tables, far[0], early)
    near[1] = fold(0, 1, under)
    (to_three,) = compose_split(head_bit[under], (1,), near[1], got[1])
    from_three = swap(to_three, "context", 3)
    work(near_parts, 0, fetched_near, gap, near_tables, ab[near_parts[-1], 1], early)

    def look(part, *after):
        names, data, known = (
            (far_parts, fetched, tables) if part in far_parts else (near_parts, fetched_near, near_tables)
        )
        qo[part, 0], qo[part, 1], gain = outlook(
            names.index(part), part, queries, data[1], gap, known, norm_gain[None, :], (solved[part, 0], solved[part, 1]), *after
        )
        return gain

    every_part = far_parts + near_parts
    near[0] = fold(0, 0, under)
    to_one, mine = compose_split(head_bit[under], (1, 0), near[0], got[0])
    from_one = swap(to_one, "context", 1)
    (to_two,) = compose_split(head_bit[under], (0,), near[1], got[1], mine)
    from_two = swap(to_two, "context", 2)
    for turn in (1, 0):
        levels[under][0, turn] = (near[turn], got[turn])

    for part in every_part[:2]:
        look(part, mine)
    only_last = context_bits == 3
    outlooks = [qo[part, 0] for part in every_part[:2]]
    total, before = four(only_last, (mine, from_one, from_two, from_three), *outlooks)
    outer = None
    held = [array for level in levels[:under] for pair in level.values() for array in pair]
    for part in every_part[2:]:
        gain = look(part, total, *held)
    done_by = [qo[part, turn] for part in every_part for turn in (0, 1)] + held
    for bit in range(2, context_bits - 1):
        other = swap(total, "context", 1 << bit)
        total, outer = doubling(context_bit[bit], bit == context_bits - 2, total, other, outer)
    other = swap(total, "context", 1 << (context_bits - 1))

    states = {}
    entering = spread(context_bit[-1], other, before, outer, gate_input, *done_by)
    from_far = {distance: swap(entering[distance], "context", distance) for distance in (3, 2, 1)}
    total_units = 2 * head_count
    strips, waiting, results = [], [], [None]

    def write(part, turn):
        number = len(strips) + 1
        stored = []
        if number in (total_units // 2, total_units - 1, total_units):
            stored, waiting[:] = waiting[:], []
        chained = [strips[-1][0]] if strips and not stored else []
        result, strip = finish(
            (part, turn),
            number == total_units,
            states[part, turn],
            qo[part, turn],
            gate_input,
            gain,
            results[-1],
            [(strips[entry][0], strips[entry][1]) for entry in stored],
            *chained,
        )
        results.append(result)
        waiting.append(len(strips))
        strips.append((strip, (part, turn)))

    leaves = []
    inner = [
        (0, 0, head_bits, (entering[0], from_far[1])),
        (0, 1, head_bits, (from_far[2], from_far[3])),
    ]

    def pass_on(part, turn, below, sources, *after):
        down = list(reversed(range(below)))
        outs = descend(
            [head_bit[bit] for bit in down],
            sources,
            [levels[bit][part, turn] for bit in down],
            strips[-1][0] if strips else None,
            *after,
        )
        states[part, turn] = outs[below]
        if strips:
            strips[-1] = (outs[below + 1], strips[-1][1])
        for level, bit in enumerate(down):
            entry = (part | 1 << bit, turn, bit, (swap(outs[level], "head", 1 << bit),))
            (inner if bit else leaves).append(entry)

    def write_leaves(entries):
        for part, turn, _, (state,) in entries:
            states[part, turn] = state
            write(part, turn)

    depth = head_bits
    while inner:
        inner.sort(key=lambda entry: (-entry[2], entry[1]))
        part, turn, below, sources = inner.pop(0)
        if below < depth:
            write_leaves(leaves)
            leaves.clear()
            depth = below
        known = len(leaves)
        ahead = [leaves[0][3][0]] if turn and below == head_bits else []
        pass_on(part, turn, below, sources, *ahead)
        if not inner:
            write_leaves(leaves[:known])
            del leaves[:known]
        write(part, turn)
    write_leaves(leaves)
    return results[-1]


def solution(mesh):
    return jax.shard_map(
        functools.partial(body, mesh.shape["head"], mesh.shape["context"]),
        mesh=mesh,
        in_specs=(
            P(("context", "head"), None),
            P(("context", "head"), None),
            P(("context", "head"), None),
            P(("context", "head"), None),
            P(("context", "head"), None),
            P(("context", "head"), None),
            P("head"),
            P(),
            P("context"),
        ),
        out_specs=P(("context", "head"), None),
        check_vma=False,
    )
```
